32 devices in a mesh: dp: 8 (over z, x), tensor: 4 (over y, core).
Axes of the slice: x: 2, y: 2, z: 4, core: 2. Of those that a mesh axis runs over, the one named last changes fastest.
Arguments:
- block_in: float32 [8192, 1536], P(('dp', 'tensor')), may hold values from -6 to 6
- cotangent: float32 [8192, 1536], P(('dp', 'tensor')), may hold values from -6 to 6
- in_weight: float32 [3, 1536, 1536], P(None, 'dp', 'tensor'), may hold values from -0.15625 to 0.15625
- conv_weight: float32 [3, 1536], P(None, 'tensor'), may hold values from -3.5 to 3.5
- out_weight: float32 [1536, 1536], P('dp', 'tensor'), may hold values from -0.15625 to 0.15625
- gateup_weight: float32 [2, 1536, 6912], P(None, 'dp', 'tensor'), may hold values from -0.15625 to 0.15625
- down_weight: float32 [1536, 6912], P('dp', 'tensor'), may hold values from -0.078125 to 0.078125
- norm_gains: float32 [2, 1536], replicated, may hold values from 0.25 to 1.75
- in_first: float32 [3, 1536, 1536], P(None, 'dp', 'tensor'), may hold values from -56 to 56
- in_second: float32 [3, 1536, 1536], P(None, 'dp', 'tensor'), may hold values from 409.6 to 1638.4
- conv_first: float32 [3, 1536], P(None, 'tensor'), may hold values from -56 to 56
- conv_second: float32 [3, 1536], P(None, 'tensor'), may hold values from 409.6 to 1638.4
- out_first: float32 [1536, 1536], P('dp', 'tensor'), may hold values from -56 to 56
- out_second: float32 [1536, 1536], P('dp', 'tensor'), may hold values from 409.6 to 1638.4
- gateup_first: float32 [2, 1536, 6912], P(None, 'dp', 'tensor'), may hold values from -16 to 16
- gateup_second: float32 [2, 1536, 6912], P(None, 'dp', 'tensor'), may hold values from 36.864 to 147.456
- down_first: float32 [1536, 6912], P('dp', 'tensor'), may hold values from -28 to 28
- down_second: float32 [1536, 6912], P('dp', 'tensor'), may hold values from 102.4 to 409.6
- gains_first: float32 [2, 1536], replicated, may hold values from -56 to 56
- gains_second: float32 [2, 1536], replicated, may hold values from 409.6 to 1638.4
Outputs:
- block_out: float32 [8192, 1536], P(('dp', 'tensor'))
- input_grad: float32 [8192, 1536], P(('dp', 'tensor'))
- in_grad: float32 [3, 1536, 1536], P(None, 'dp', 'tensor')
- conv_grad: float32 [3, 1536], P(None, 'tensor')
- out_grad: float32 [1536, 1536], P('dp', 'tensor')
- gateup_grad: float32 [2, 1536, 6912], P(None, 'dp', 'tensor')
- down_grad: float32 [1536, 6912], P('dp', 'tensor')
- gains_grad: float32 [2, 1536], replicated
- in_updated: float32 [3, 1536, 1536], P(None, 'dp', 'tensor')
- conv_updated: float32 [3, 1536], P(None, 'tensor')
- out_updated: float32 [1536, 1536], P('dp', 'tensor')
- gateup_updated: float32 [2, 1536, 6912], P(None, 'dp', 'tensor')
- down_updated: float32 [1536, 6912], P('dp', 'tensor')
- gains_updated: float32 [2, 1536], replicated
- in_momentum: float32 [3, 1536, 1536], P(None, 'dp', 'tensor')
- in_variance: float32 [3, 1536, 1536], P(None, 'dp', 'tensor')
- conv_momentum: float32 [3, 1536], P(None, 'tensor')
- conv_variance: float32 [3, 1536], P(None, 'tensor')
- out_momentum: float32 [1536, 1536], P('dp', 'tensor')
- out_variance: float32 [1536, 1536], P('dp', 'tensor')
- gateup_momentum: float32 [2, 1536, 6912], P(None, 'dp', 'tensor')
- gateup_variance: float32 [2, 1536, 6912], P(None, 'dp', 'tensor')
- down_momentum: float32 [1536, 6912], P('dp', 'tensor')
- down_variance: float32 [1536, 6912], P('dp', 'tensor')
- gains_momentum: float32 [2, 1536], replicated
- gains_variance: float32 [2, 1536], replicated
The draws below stay inside these ranges and needn't reach their ends.
All inputs are finite; a program needn't handle non-finite values.
Results may differ from the reference program's by a relative error of at most 0.02.
Values may be sent and summed in bfloat16 or wider, within the bound.
A program may use at most 256 MiB of HBM per device.

```python
import math
import jax
import jax.numpy as jnp
from jax import lax

D = 1536
FF = 6912
KERNEL = 3
LEN = 1024
STEP = 3
TOKENS = 8192
N_DP = 8


def spiked(values, stream_key, source, target, shards_of, factor):
    owner, partner = [(jnp.arange(values.shape[position]) // (values.shape[position] // shards_of)).reshape([-1 if axis == position else 1 for axis in range(values.ndim)]) for position in (source, target)]
    chosen = jax.random.permutation(stream_key, shards_of)[partner]
    strong = (owner == chosen) | (owner == (partner + shards_of // 2) % shards_of)
    return jnp.where(strong, factor * values, values)


def shard_levels(own_key, dims, split, smallest, top_value):
    level = 1.0
    for axis_at, blocks in split:
        heights = jax.random.uniform(jax.random.fold_in(jax.random.fold_in(own_key, 6), axis_at), (blocks,), jnp.float32, smallest / len(split), top_value / len(split))
        level = level * jnp.repeat(jnp.exp(heights), dims[axis_at] // blocks).reshape((-1,) + (1,) * (len(dims) - 1 - axis_at))
    return level


def gaussian(stream_key, dims, width, limit, shards=(), kind=jnp.bfloat16):
    level = shard_levels(stream_key, dims, shards, -0.22, 0.18) if shards else 1.0
    result = jax.random.normal(stream_key, dims, jnp.float32) * width * level
    return jnp.minimum(jnp.maximum(result, -limit), limit).astype(kind)


def noise_with(rng, shape, width, reach, split, heavy, kind=jnp.bfloat16):
    entries = width * jax.random.normal(rng, shape, jnp.float32)
    if split:
        entries = entries * shard_levels(rng, shape, split, -0.22, 0.18)
    return jnp.clip(spiked(entries, jax.random.fold_in(rng, 3), *heavy), -reach, reach).astype(kind)


def setup_inputs(seed: int = 0) -> dict:
    arg_keys = jax.random.split(jax.random.key(seed), 21)
    return {
        "block_in": noise_with(arg_keys[0], (TOKENS, D), 1.0, 6.0, ((0, 32),), (0, 1, 32, 2.75), jnp.float32),
        "cotangent": noise_with(arg_keys[1], (TOKENS, D), 1.0, 6.0, ((0, 32),), (0, 1, 32, 2.75), jnp.float32),
        "in_weight": gaussian(arg_keys[2], (3, D, D), D ** -0.5, 0.15625, ((1, 8), (2, 4)), jnp.float32),
        "conv_weight": gaussian(arg_keys[3], (KERNEL, D), KERNEL ** -0.5, 3.5, ((1, 4),), jnp.float32),
        "out_weight": gaussian(arg_keys[4], (D, D), D ** -0.5, 0.15625, ((0, 8), (1, 4)), jnp.float32),
        "gateup_weight": gaussian(arg_keys[5], (2, D, FF), D ** -0.5, 0.15625, ((1, 8), (2, 4)), jnp.float32),
        "down_weight": gaussian(arg_keys[6], (D, FF), FF ** -0.5, 0.078125, ((0, 8), (1, 4)), jnp.float32),
        "norm_gains": jnp.clip(1.0 + 0.15 * jax.random.normal(arg_keys[7], (2, D), jnp.float32), 0.25, 1.75),
        "in_first": gaussian(arg_keys[8], (3, D, D), (0.1 * TOKENS ** 0.5), 56.0, ((1, 8), (2, 4)), jnp.float32),
        "in_second": jnp.clip(jnp.exp(math.log(1638.4) - 1.3862944 * jax.random.uniform(arg_keys[9], (3, D, D), jnp.float32) ** shard_levels(arg_keys[9], (3, D, D), ((1, 8), (2, 4)), -0.2, 0.2)), 409.6, 1638.4),
        "conv_first": gaussian(arg_keys[10], (KERNEL, D), (0.1 * TOKENS ** 0.5), 56.0, ((1, 4),), jnp.float32),
        "conv_second": jnp.clip(jnp.exp(math.log(1638.4) - 1.3862944 * jax.random.uniform(arg_keys[11], (KERNEL, D), jnp.float32) ** shard_levels(arg_keys[11], (KERNEL, D), ((1, 4),), -0.2, 0.2)), 409.6, 1638.4),
        "out_first": gaussian(arg_keys[12], (D, D), (0.1 * TOKENS ** 0.5), 56.0, ((0, 8), (1, 4)), jnp.float32),
        "out_second": jnp.clip(jnp.exp(math.log(1638.4) - 1.3862944 * jax.random.uniform(arg_keys[13], (D, D), jnp.float32) ** shard_levels(arg_keys[13], (D, D), ((0, 8), (1, 4)), -0.2, 0.2)), 409.6, 1638.4),
        "gateup_first": gaussian(arg_keys[14], (2, D, FF), (0.03 * TOKENS ** 0.5), 16.0, ((1, 8), (2, 4)), jnp.float32),
        "gateup_second": jnp.clip(jnp.exp(math.log(147.456) - 1.3862944 * jax.random.uniform(arg_keys[15], (2, D, FF), jnp.float32) ** shard_levels(arg_keys[15], (2, D, FF), ((1, 8), (2, 4)), -0.2, 0.2)), 36.864, 147.456),
        "down_first": gaussian(arg_keys[16], (D, FF), (0.05 * TOKENS ** 0.5), 28.0, ((0, 8), (1, 4)), jnp.float32),
        "down_second": jnp.clip(jnp.exp(math.log(409.6) - 1.3862944 * jax.random.uniform(arg_keys[17], (D, FF), jnp.float32) ** shard_levels(arg_keys[17], (D, FF), ((0, 8), (1, 4)), -0.2, 0.2)), 102.4, 409.6),
        "gains_first": gaussian(arg_keys[18], (2, D), (0.1 * TOKENS ** 0.5), 56.0, (), jnp.float32),
        "gains_second": jnp.clip(jnp.exp(jax.random.uniform(arg_keys[19], (2, D), jnp.float32, math.log(409.6), math.log(1638.4))), 409.6, 1638.4),
    }


eps_norm = 1e-05
beta_one = 0.9
beta_two = 0.95
adam_eps = 1e-08
decay_matrix = 0.1
rate_matrix = 0.03
rate_small = 0.5

def delayed(values, steps):
    head = jnp.zeros((steps,) + values.shape[1:], values.dtype)
    return jnp.concatenate([head, values[:values.shape[0] - steps]], axis=0)

def advanced(values, steps):
    tail = jnp.zeros((steps,) + values.shape[1:], values.dtype)
    return jnp.concatenate([values[steps:], tail], axis=0)

def norm_scale(values):
    return lax.rsqrt(lax.optimization_barrier(jnp.mean(values * values, axis=-1, keepdims=True)) + eps_norm)

def norm_back(values, scale, gain, upstream):
    weighted = gain * upstream
    normal = values * scale
    return scale * (weighted - normal * lax.optimization_barrier(jnp.mean(weighted * normal, axis=-1, keepdims=True)))

def adamw(weight, gradient, first, second, rate, decay_rate):
    momentum = beta_one * first + (1.0 - beta_one) * gradient
    variance = beta_two * second + (1.0 - beta_two) * gradient * gradient
    corrected = momentum / (1.0 - beta_one ** STEP)
    spread = variance / (1.0 - beta_two ** STEP)
    updated = weight - rate * (corrected / (jnp.sqrt(spread) + adam_eps) + decay_rate * weight)
    return (updated, momentum, variance)

def mm(left, right):
    return jnp.dot(left, right, preferred_element_type=jnp.float32)

def reference(block_in, cotangent, in_weight, conv_weight, out_weight, gateup_weight, down_weight, norm_gains, in_first, in_second, conv_first, conv_second, out_first, out_second, gateup_first, gateup_second, down_first, down_second, gains_first, gains_second):
    in_low = in_weight.astype(jnp.bfloat16)
    out_low = out_weight.astype(jnp.bfloat16)
    gateup_low = gateup_weight.astype(jnp.bfloat16)
    down_low = down_weight.astype(jnp.bfloat16)
    kernel_len = conv_weight.shape[0]

    def one_sequence(totals, inputs):
        seq_in, seq_cot = inputs
        scale_one = norm_scale(seq_in)
        normed_one = (seq_in * scale_one * norm_gains[0]).astype(jnp.bfloat16)
        b_part = mm(normed_one, in_low[0])
        c_part = mm(normed_one, in_low[1])
        v_part = mm(normed_one, in_low[2])
        mixed = b_part * v_part
        convolved = sum((conv_weight[offset] * delayed(mixed, kernel_len - 1 - offset) for offset in range(kernel_len)))
        mixer = (c_part * convolved).astype(jnp.bfloat16)
        middle = seq_in + mm(mixer, out_low.T)
        scale_two = norm_scale(middle)
        normed_two = (middle * scale_two * norm_gains[1]).astype(jnp.bfloat16)
        gate = mm(normed_two, gateup_low[0])
        up_part = mm(normed_two, gateup_low[1])
        hidden = (jax.nn.silu(gate) * up_part).astype(jnp.bfloat16)
        seq_out = middle + mm(hidden, down_low.T)
        low_cot = seq_cot.astype(jnp.bfloat16)
        down_part = mm(low_cot.T, hidden)
        d_hidden = mm(low_cot, down_low)
        sig_gate = jax.nn.sigmoid(gate)
        d_gate = (d_hidden * up_part * sig_gate * (1.0 + gate * (1.0 - sig_gate))).astype(jnp.bfloat16)
        d_up = (d_hidden * jax.nn.silu(gate)).astype(jnp.bfloat16)
        gateup_part = jnp.stack([mm(normed_two.T, d_gate), mm(normed_two.T, d_up)])
        d_normed_two = mm(d_gate, gateup_low[0].T) + mm(d_up, gateup_low[1].T)
        d_middle = seq_cot + norm_back(middle, scale_two, norm_gains[1], d_normed_two)
        low_middle = d_middle.astype(jnp.bfloat16)
        out_part = mm(low_middle.T, mixer)
        d_mixer = mm(low_middle, out_low)
        d_conv = d_mixer * c_part
        d_c = d_mixer * convolved
        conv_part = jnp.stack([lax.optimization_barrier(jnp.sum(d_conv * delayed(mixed, kernel_len - 1 - offset), axis=0)) for offset in range(kernel_len)])
        d_mixed = sum((conv_weight[offset] * advanced(d_conv, kernel_len - 1 - offset) for offset in range(kernel_len)))
        d_proj = [(d_mixed * v_part).astype(jnp.bfloat16), d_c.astype(jnp.bfloat16), (d_mixed * b_part).astype(jnp.bfloat16)]
        in_part = jnp.stack([mm(normed_one.T, d_proj[kind]) for kind in range(3)])
        d_normed_one = mm(d_proj[0], in_low[0].T) + mm(d_proj[1], in_low[1].T) + mm(d_proj[2], in_low[2].T)
        seq_grad = d_middle + norm_back(seq_in, scale_one, norm_gains[0], d_normed_one)
        gain_part = jnp.stack([lax.optimization_barrier(jnp.sum(d_normed_one * seq_in * scale_one, axis=0)), lax.optimization_barrier(jnp.sum(d_normed_two * middle * scale_two, axis=0))])
        parts = (in_part, conv_part, out_part, gateup_part, down_part, gain_part)
        return (jax.tree.map(jnp.add, totals, parts), (seq_out, seq_grad))
    start_totals = (jnp.zeros(in_weight.shape, jnp.float32), jnp.zeros(conv_weight.shape, jnp.float32), jnp.zeros(out_weight.shape, jnp.float32), jnp.zeros(gateup_weight.shape, jnp.float32), jnp.zeros(down_weight.shape, jnp.float32), jnp.zeros(norm_gains.shape, jnp.float32))
    totals, (seq_outs, seq_grads) = lax.scan(one_sequence, start_totals, (block_in.reshape(N_DP, LEN, D), cotangent.reshape(N_DP, LEN, D)))
    in_grad, conv_grad, out_grad, gateup_grad, down_grad, gains_grad = totals
    block_out = seq_outs.reshape(N_DP * LEN, D)
    input_grad = seq_grads.reshape(N_DP * LEN, D)
    in_updated, in_momentum, in_variance = adamw(in_weight, in_grad, in_first, in_second, rate_matrix, decay_matrix)
    conv_updated, conv_momentum, conv_variance = adamw(conv_weight, conv_grad, conv_first, conv_second, rate_small, 0.0)
    out_updated, out_momentum, out_variance = adamw(out_weight, out_grad, out_first, out_second, rate_matrix, decay_matrix)
    gateup_updated, gateup_momentum, gateup_variance = adamw(gateup_weight, gateup_grad, gateup_first, gateup_second, rate_matrix, decay_matrix)
    down_updated, down_momentum, down_variance = adamw(down_weight, down_grad, down_first, down_second, rate_matrix, decay_matrix)
    gains_updated, gains_momentum, gains_variance = adamw(norm_gains, gains_grad, gains_first, gains_second, rate_small, 0.0)
    return (block_out, input_grad, in_grad, conv_grad, out_grad, gateup_grad, down_grad, gains_grad, in_updated, conv_updated, out_updated, gateup_updated, down_updated, gains_updated, in_momentum, in_variance, conv_momentum, conv_variance, out_momentum, out_variance, gateup_momentum, gateup_variance, down_momentum, down_variance, gains_momentum, gains_variance)
```

```python
import functools

import jax
import jax.numpy as jnp
from jax import lax
from jax.experimental import pallas as pl
from jax.experimental.pallas import tpu as pltpu
from jax.sharding import PartitionSpec as P

STEP = 3


eps_norm = 1e-05
beta_one = 0.9
beta_two = 0.95
adam_eps = 1e-08
decay_matrix = 0.1
rate_matrix = 0.03
rate_small = 0.5


def delayed(values, steps):
    head = jnp.zeros((steps,) + values.shape[1:], values.dtype)
    return jnp.concatenate([head, values[: values.shape[0] - steps]], axis=0)


def advanced(values, steps):
    tail = jnp.zeros((steps,) + values.shape[1:], values.dtype)
    return jnp.concatenate([values[steps:], tail], axis=0)


def norm_scale(values):
    return lax.rsqrt(jnp.mean(values * values, axis=-1, keepdims=True) + eps_norm)


def norm_back(values, scale, gain, upstream):
    weighted = gain * upstream
    normal = values * scale
    return scale * (weighted - normal * jnp.mean(weighted * normal, axis=-1, keepdims=True))


def adamw(weight, gradient, first, second, rate, decay_rate):
    momentum = beta_one * first + (1.0 - beta_one) * gradient
    variance = beta_two * second + (1.0 - beta_two) * gradient * gradient
    corrected = momentum / (1.0 - beta_one**STEP)
    spread = variance / (1.0 - beta_two**STEP)
    updated = weight - rate * (corrected / (jnp.sqrt(spread) + adam_eps) + decay_rate * weight)
    return (updated, momentum, variance)


MESH = pl.DeviceIdType.MESH
BF = jnp.bfloat16
F32 = jnp.float32
NN = (((1,), (0,)), ((), ()))
NT = (((1,), (1,)), ((), ()))
TN = (((0,), (0,)), ((), ()))
VMEM_LIMIT = 62 * 1024 * 1024


def dot(left, right, dims=NN):
    return lax.dot_general(left, right, dims, preferred_element_type=F32)


class Ring:
    def __init__(self, n, rows):
        self.n, self.rows = n, rows
        self.sends = n - 1
        d = lax.axis_index("dp")
        t = lax.axis_index("tensor")
        self.d, self.t = d, t
        self.y, self.c = lax.div(t, 2), lax.rem(t, 2)
        self.pos = lax.div(d, 2) + lax.rem(d, 2) * (n - 1 - 2 * lax.div(d, 2))
        self.next = (self.at(self.pos + 1), t)
        self.prev = (self.at(self.pos - 1), t)
        self.core = (d, self.y * 2 + (1 - self.c))
        self.over = (d, (1 - self.y) * 2 + self.c)
        first = (rows // 2 + 15) // 16 * 16
        self.units = ((0, first), (first, rows - first))

    def at(self, q):
        n = self.n
        q = lax.rem(q + 2 * n, n)
        back = lax.div(q, n // 2)
        return (1 - back) * 2 * q + back * (2 * (n - 1 - q) + 1)

    def span(self, q, u):
        start, size = self.units[u]
        return pl.ds(pl.multiple_of(self.at(q) * self.rows + start, 16), size)

    def barrier(self):
        sem = pltpu.get_barrier_semaphore()
        for device in (self.next, self.prev, self.core, self.over):
            pl.semaphore_signal(sem, inc=1, device_id=device, device_id_type=MESH)
        pl.semaphore_wait(sem, 4)


class Gather:
    def __init__(self, ring, mats, send_sem, recv_sem):
        self.ring, self.mats = ring, mats
        self.send_sem, self.recv_sem = send_sem, recv_sem
        self.sent, self.got = 0, set()
        self.total = ring.sends * len(mats)

    def copy(self, index, way, arriving):
        stream, j = divmod(index, self.ring.sends)
        hop, sub = j // 2 + 1, j % 2
        u = sub if way == 0 else 1 - sub
        sign = 1 if way == 0 else -1
        q = self.ring.pos - sign * (hop if arriving else hop - 1)
        ref = self.mats[stream].at[self.ring.span(q, u)]
        return pltpu.make_async_remote_copy(
            ref,
            ref,
            self.send_sem.at[way, index],
            self.recv_sem.at[way, index],
            device_id=self.ring.next if way == 0 else self.ring.prev,
            device_id_type=MESH,
        )

    def wait(self, index):
        if index not in self.got:
            self.got.add(index)
            for way in (0, 1):
                self.copy(index, way, True).wait_recv()

    def upto(self, stream, j):
        if stream >= len(self.mats):
            return
        stop = stream * self.ring.sends + -(-j * self.ring.sends // 7)
        while self.sent < stop:
            index = self.sent
            if index % self.ring.sends >= 2:
                self.wait(index - 2)
            for way in (0, 1):
                self.copy(index, way, False).start()
            self.sent += 1

    def complete(self, stream):
        self.upto(stream, 7)
        self.upto(stream + 1, 2)
        for index in range(stream * self.ring.sends, (stream + 1) * self.ring.sends):
            self.wait(index)

    def drain(self):
        for index in range(self.total):
            for way in (0, 1):
                self.copy(index, way, False).wait_send()


class Tokens:
    def __init__(self, ring, full, send_sem, recv_sem, base):
        self.ring, self.full = ring, full
        self.rows = full.shape[0] // 4
        self.send_sem, self.recv_sem, self.base = send_sem, recv_sem, base

    def copy(self, kind, arriving):
        y, c = self.ring.y, self.ring.c
        other_y, other_c = 1 - y, 1 - c
        if kind == 0:
            owner = (other_y if arriving else y) * 2 + c
        elif kind == 1:
            owner = y * 2 + (other_c if arriving else c)
        else:
            owner = other_y * 2 + (other_c if arriving else c)
        ref = self.full.at[pl.ds(pl.multiple_of(owner * self.rows, 16), self.rows)]
        return pltpu.make_async_remote_copy(
            ref,
            ref,
            self.send_sem.at[self.base + kind],
            self.recv_sem.at[self.base + kind],
            device_id=self.ring.over if kind == 0 else self.ring.core,
            device_id_type=MESH,
        )

    def start(self):
        self.copy(0, False).start()
        self.copy(1, False).start()

    def forward(self):
        self.copy(0, True).wait_recv()
        self.copy(2, False).start()

    def finish(self):
        self.copy(1, True).wait_recv()
        self.copy(2, True).wait_recv()

    def drain(self):
        for kind in range(3):
            self.copy(kind, False).wait_send()


class Sums:
    def __init__(self, ring, out, got, send_sem, recv_sem, base):
        self.ring, self.out, self.got = ring, out, got
        self.send_sem, self.recv_sem, self.base = send_sem, recv_sem, base

    def owner(self, kind):
        y, c = self.ring.y, self.ring.c
        return ((1 - y) * 2 + 1 - c, (1 - y) * 2 + c, y * 2 + 1 - c, y * 2 + c)[kind]

    def copy(self, kind):
        return pltpu.make_async_remote_copy(
            self.out.at[kind],
            self.got.at[kind],
            self.send_sem.at[self.base + kind],
            self.recv_sem.at[self.base + kind],
            device_id=self.ring.over if kind == 1 else self.ring.core,
            device_id_type=MESH,
        )

    def far(self, block):
        self.out[0] = block(self.owner(0)).astype(BF)
        self.copy(0).start()
        part = block(self.owner(1))
        self.copy(0).wait_recv()
        self.out[1] = (part + self.got[0].astype(F32)).astype(BF)
        self.copy(1).start()

    def near(self, block):
        self.out[2] = block(self.owner(2)).astype(BF)
        self.copy(2).start()
        return block(self.owner(3))

    def total(self, part):
        self.copy(2).wait_recv()
        part = part + self.got[2].astype(F32)
        self.copy(1).wait_recv()
        return part + self.got[1].astype(F32)

    def drain(self):
        for kind in range(3):
            self.copy(kind).wait_send()


def forward_kernel(
    n,
    block_ref,
    gains_ref,
    conv_ref,
    in_ref,
    out_ref,
    gateup_ref,
    down_ref,
    cot_ref,
    wc_hbm,
    wg_hbm,
    wu_hbm,
    wd_hbm,
    one_hbm,
    two_hbm,
    fcot_hbm,
    proj_hbm,
    mixer_hbm,
    gate_hbm,
    up_hbm,
    hidden_hbm,
    dgrad_hbm,
    middle_ref,
    wc,
    wg,
    wu,
    low_d,
    stage_c,
    stage_m,
    cot,
    full_one,
    full_two,
    full_cot,
    proj,
    mixer,
    gate_t,
    up_t,
    hidden,
    grad_t,
    sum_out,
    sum_got,
    send_sem,
    recv_sem,
    tok_send,
    tok_recv,
    sum_send,
    sum_recv,
    in_sem,
    save_sem,
    tile_sem,
):
    rows = wc.shape[0] // n
    ring = Ring(n, rows)
    tokens = block_ref.shape[0]
    chan = out_ref.shape[1]
    seq = full_one.shape[0]
    taps = conv_ref.shape[0]
    own = pl.ds(pl.multiple_of(ring.d * rows, 16), rows)
    mine = pl.ds(pl.multiple_of(ring.t * tokens, 16), tokens)

    loads = [pltpu.make_async_copy(in_ref.at[k], stage_c.at[k], in_sem.at[k]) for k in range(3)]
    loads.append(pltpu.make_async_copy(out_ref, stage_c.at[3], in_sem.at[3]))
    loads.append(pltpu.make_async_copy(gateup_ref.at[0], stage_m.at[0], in_sem.at[4]))
    loads.append(pltpu.make_async_copy(gateup_ref.at[1], stage_m.at[1], in_sem.at[5]))
    loads.append(pltpu.make_async_copy(down_ref, stage_m.at[0], in_sem.at[6]))
    loads.append(pltpu.make_async_copy(cot_ref, cot, in_sem.at[7]))
    for k in (0, 1, 2, 3, 4, 5, 7):
        loads[k].start()
    saves = []

    def save(source, target):
        copy = pltpu.make_async_copy(source, target, save_sem.at[len(saves)])
        copy.start()
        saves.append(copy)

    ring.barrier()
    gather = Gather(ring, (wc, wg, wu, wd_hbm), send_sem, recv_sem)
    for k in range(4):
        loads[k].wait()
        wc[own, k * chan : (k + 1) * chan] = stage_c[k].astype(BF)
    gather.upto(0, 2)

    values = block_ref[...]
    scale = lax.rsqrt(jnp.mean(values * values, axis=1, keepdims=True) + eps_norm)
    full_one[mine] = (values * scale * gains_ref[0:1]).astype(BF)
    ones = Tokens(ring, full_one, tok_send, tok_recv, 0)
    ones.start()
    for k, mat in enumerate((wg, wu)):
        loads[4 + k].wait()
        mat[own] = stage_m[k].astype(BF)
        if k == 0:
            loads[6].start()
    loads[6].wait()
    low_d[...] = stage_m[0].astype(BF)
    place = pltpu.make_async_copy(low_d, wd_hbm.at[own], in_sem.at[8])
    place.start()
    loads[7].wait()
    full_cot[mine] = cot[...].astype(BF)
    gather.upto(0, 5)
    ones.forward()
    cots = Tokens(ring, full_cot, tok_send, tok_recv, 3)
    cots.start()
    gather.upto(0, 7)
    ones.finish()
    gather.complete(0)
    save(wc, wc_hbm)
    save(full_one, one_hbm)

    tile = tokens
    proj[0:8] = jnp.zeros((8, 3 * chan), F32)

    def project(i, carry):
        proj[pl.ds(pl.multiple_of(i * tile + 8, 8), tile)] = dot(
            full_one[pl.ds(pl.multiple_of(i * tile, 16), tile)], wc[:, : 3 * chan]
        )
        return carry

    lax.fori_loop(0, seq // tile, project, 0)
    gather.upto(1, 3)

    def convolve(i, carry):
        here = pl.ds(pl.multiple_of(i * tile, 8), tile + 8)
        mixed = proj[here, :chan] * proj[here, 2 * chan :]
        total = conv_ref[taps - 1 : taps] * mixed[8:]
        for back in range(1, taps):
            total += conv_ref[taps - 1 - back : taps - back] * pltpu.roll(mixed, back, 0)[8:]
        c_part = proj[pl.ds(pl.multiple_of(i * tile + 8, 8), tile), chan : 2 * chan]
        mixer[pl.ds(pl.multiple_of(i * tile, 16), tile)] = (c_part * total).astype(BF)
        return carry

    lax.fori_loop(0, seq // tile, convolve, 0)
    save(proj.at[8 : 8 + seq], proj_hbm)
    save(mixer, mixer_hbm)

    def out_block(owner):
        here = pl.ds(pl.multiple_of(owner * tokens, 16), tokens)
        return dot(mixer[here], wc[:, 3 * chan :], NT)

    mids = Sums(ring, sum_out, sum_got, sum_send, sum_recv, 0)
    mids.far(out_block)
    part = mids.near(out_block)
    middle_ref[...] = part
    cots.forward()
    cots.finish()
    gather.upto(1, 5)
    save(full_cot, fcot_hbm)
    middle = block_ref[...] + mids.total(middle_ref[...])
    middle_ref[...] = middle
    scale = lax.rsqrt(jnp.mean(middle * middle, axis=1, keepdims=True) + eps_norm)
    full_two[mine] = (middle * scale * gains_ref[1:2]).astype(BF)
    twos = Tokens(ring, full_two, tok_send, tok_recv, 6)
    twos.start()
    gather.upto(1, 7)
    gather.upto(2, 2)
    twos.forward()
    twos.finish()
    save(full_two, two_hbm)
    gather.complete(1)
    save(wg, wg_hbm)
    place.wait()
    gather.complete(2)
    save(wu, wu_hbm)

    step = tokens // 2
    count = seq // step

    def out_copy(slot, kind, i):
        source, target = ((gate_t, gate_hbm), (up_t, up_hbm))[kind]
        here = pl.ds(pl.multiple_of(i * step, 8), step)
        return pltpu.make_async_copy(source.at[slot], target.at[here], tile_sem.at[kind, slot])

    def gated(i, carry):
        slot = lax.rem(i, 2)
        here = pl.ds(pl.multiple_of(i * step, 16), step)

        @pl.when(i >= 2)
        def _():
            out_copy(slot, 0, i).wait()
            out_copy(slot, 1, i).wait()

        x = full_two[here]
        gate = dot(x, wg[...])
        gate_t[slot] = gate
        up = dot(x, wu[...])
        up_t[slot] = up
        out_copy(slot, 0, i).start()
        out_copy(slot, 1, i).start()
        hidden[here] = (gate * jax.nn.sigmoid(gate) * up).astype(BF)
        return carry

    lax.fori_loop(0, count // 2, gated, 0)
    gather.upto(3, 4)
    lax.fori_loop(count // 2, count, gated, 0)
    for slot in (0, 1):
        for kind in (0, 1):
            out_copy(slot, kind, slot).wait()
    save(hidden, hidden_hbm)
    gather.upto(3, 6)

    width = tokens
    deep = wc.shape[0] // width

    def grad_copy(slot, i):
        here = pl.ds(pl.multiple_of(i * width, 16), width)
        return pltpu.make_async_copy(grad_t.at[slot], dgrad_hbm.at[here], tile_sem.at[2, slot])

    def graded(i, carry):
        slot = lax.rem(i, 2)

        @pl.when(i >= 2)
        def _():
            grad_copy(slot, i).wait()

        x = full_cot[:, pl.ds(pl.multiple_of(i * width, 128), width)]
        grad_t[slot] = dot(x, hidden[...], TN).astype(BF)
        grad_copy(slot, i).start()
        return carry

    lax.fori_loop(0, deep // 2, graded, 0)
    gather.upto(3, 7)
    lax.fori_loop(deep // 2, deep, graded, 0)
    for slot in (0, 1):
        grad_copy(slot, slot).wait()
    gather.complete(3)
    for copy in saves:
        copy.wait()
    for group in (ones, cots, twos, mids):
        group.drain()
    gather.drain()


def forward(n, block_in, cotangent, in_weight, conv_weight, out_weight, gateup_weight, down_weight, norm_gains):
    tokens, model = block_in.shape
    seq = tokens * 4
    chan = out_weight.shape[1]
    units = down_weight.shape[1]
    rows = out_weight.shape[0]
    sends = 4 * (n - 1)
    any_spec = pl.BlockSpec(memory_space=pl.ANY)
    vmem = pl.BlockSpec(memory_space=pltpu.VMEM)
    shape = jax.ShapeDtypeStruct
    dma = pltpu.SemaphoreType.DMA
    return pl.pallas_call(
        functools.partial(forward_kernel, n),
        out_shape=[
            shape((model, 4 * chan), BF),
            shape((model, units), BF),
            shape((model, units), BF),
            shape((model, units), BF),
            shape((seq, model), BF),
            shape((seq, model), BF),
            shape((seq, model), BF),
            shape((seq, 3 * chan), F32),
            shape((seq, chan), BF),
            shape((seq, units), F32),
            shape((seq, units), F32),
            shape((seq, units), BF),
            shape((model, units), BF),
            shape((tokens, model), F32),
        ],
        in_specs=[vmem, vmem, vmem] + [any_spec] * 5,
        out_specs=[any_spec] * 13 + [vmem],
        scratch_shapes=[
            pltpu.VMEM((model, 4 * chan), BF),
            pltpu.VMEM((model, units), BF),
            pltpu.VMEM((model, units), BF),
            pltpu.VMEM((rows, units), BF),
            pltpu.VMEM((4, rows, chan), F32),
            pltpu.VMEM((2, rows, units), F32),
            pltpu.VMEM((tokens, model), F32),
            pltpu.VMEM((seq, model), BF),
            pltpu.VMEM((seq, model), BF),
            pltpu.VMEM((seq, model), BF),
            pltpu.VMEM((seq + 8, 3 * chan), F32),
            pltpu.VMEM((seq, chan), BF),
            pltpu.VMEM((2, tokens // 2, units), F32),
            pltpu.VMEM((2, tokens // 2, units), F32),
            pltpu.VMEM((seq, units), BF),
            pltpu.VMEM((2, tokens, units), BF),
            pltpu.VMEM((3, tokens, model), BF),
            pltpu.VMEM((3, tokens, model), BF),
            dma((2, sends)),
            dma((2, sends)),
            dma((9,)),
            dma((9,)),
            dma((3,)),
            dma((3,)),
            dma((9,)),
            dma((10,)),
            dma((3, 2)),
        ],
        compiler_params=pltpu.CompilerParams(
            collective_id=0, has_side_effects=True, vmem_limit_bytes=VMEM_LIMIT
        ),
        cost_estimate=pl.CostEstimate(flops=10 * seq * model * units, bytes_accessed=10**8, transcendentals=0),
    )(block_in, norm_gains, conv_weight, in_weight, out_weight, gateup_weight, down_weight, cotangent)


def per_device(
    block_in,
    cotangent,
    in_weight,
    conv_weight,
    out_weight,
    gateup_weight,
    down_weight,
    norm_gains,
    in_first,
    in_second,
    conv_first,
    conv_second,
    out_first,
    out_second,
    gateup_first,
    gateup_second,
    down_first,
    down_second,
    gains_first,
    gains_second,
):
    kernel_len = conv_weight.shape[0]
    (
        wide_conv,
        wide_gate,
        wide_up,
        wide_down,
        full_one,
        full_two,
        full_cot,
        proj,
        mixer,
        gate,
        up_part,
        hidden,
        down_part,
        middle,
    ) = forward(
        lax.axis_size("dp"),
        block_in,
        cotangent,
        in_weight,
        conv_weight,
        out_weight,
        gateup_weight,
        down_weight,
        norm_gains,
    )
    chan = conv_weight.shape[1]
    wide_out = wide_conv[:, 3 * chan :]
    b_part, c_part, v_part = (proj[:, k * chan : (k + 1) * chan] for k in range(3))
    mixed = b_part * v_part
    convolved = sum(
        (
            conv_weight[offset] * delayed(mixed, kernel_len - 1 - offset)
            for offset in range(kernel_len)
        )
    )
    scale_one = norm_scale(block_in)
    scale_two = norm_scale(middle)
    block_out = middle + lax.psum_scatter(
        jnp.einsum("tf,df->td", hidden, wide_down, preferred_element_type=jnp.float32).astype(
            jnp.bfloat16
        ),
        "tensor",
        scatter_dimension=0,
        tiled=True,
    ).astype(jnp.float32)
    d_hidden = jnp.einsum("td,df->tf", full_cot, wide_down, preferred_element_type=jnp.float32)
    sig_gate = jax.nn.sigmoid(gate)
    d_gate = (d_hidden * up_part * sig_gate * (1.0 + gate * (1.0 - sig_gate))).astype(jnp.bfloat16)
    d_up = (d_hidden * jax.nn.silu(gate)).astype(jnp.bfloat16)
    gateup_part = jnp.stack(
        [
            jnp.einsum("td,tf->df", full_two, d_gate, preferred_element_type=jnp.float32),
            jnp.einsum("td,tf->df", full_two, d_up, preferred_element_type=jnp.float32),
        ]
    )
    d_normed_two = lax.psum_scatter(
        jnp.einsum("tf,df->td", d_gate, wide_gate, preferred_element_type=jnp.float32)
        + jnp.einsum("tf,df->td", d_up, wide_up, preferred_element_type=jnp.float32),
        "tensor",
        scatter_dimension=0,
        tiled=True,
    )
    gain_two_part = jnp.sum(d_normed_two * middle * scale_two, axis=0)
    d_middle = cotangent + norm_back(middle, scale_two, norm_gains[1], d_normed_two)
    full_middle = lax.all_gather(d_middle.astype(jnp.bfloat16), "tensor", axis=0, tiled=True)
    out_part = jnp.einsum("td,tc->dc", full_middle, mixer, preferred_element_type=jnp.float32)
    d_mixer = jnp.einsum("td,dc->tc", full_middle, wide_out, preferred_element_type=jnp.float32)
    d_conv = d_mixer * c_part
    d_c = d_mixer * convolved
    conv_part = jnp.stack(
        [
            jnp.sum(d_conv * delayed(mixed, kernel_len - 1 - offset), axis=0)
            for offset in range(kernel_len)
        ]
    )
    d_mixed = sum(
        (
            conv_weight[offset] * advanced(d_conv, kernel_len - 1 - offset)
            for offset in range(kernel_len)
        )
    )
    d_proj = jnp.stack(
        [
            (d_mixed * v_part).astype(jnp.bfloat16),
            d_c.astype(jnp.bfloat16),
            (d_mixed * b_part).astype(jnp.bfloat16),
        ]
    )
    in_part = jnp.einsum("td,ktc->kdc", full_one, d_proj, preferred_element_type=jnp.float32)
    d_normed_one = lax.psum_scatter(
        jnp.einsum(
            "tc,dc->td",
            jnp.concatenate([d_proj[0], d_proj[1], d_proj[2]], axis=1),
            wide_conv[:, : 3 * chan],
            preferred_element_type=jnp.float32,
        ).astype(
            jnp.bfloat16
        ),
        "tensor",
        scatter_dimension=0,
        tiled=True,
    ).astype(jnp.float32)
    gain_one_part = jnp.sum(d_normed_one * block_in * scale_one, axis=0)
    input_grad = d_middle + norm_back(block_in, scale_one, norm_gains[0], d_normed_one)
    in_grad, out_grad, gateup_grad, down_grad = (
        lax.psum_scatter(
            in_part.astype(jnp.bfloat16), "dp", scatter_dimension=1, tiled=True
        ).astype(jnp.float32),
        lax.psum_scatter(
            out_part.astype(jnp.bfloat16), "dp", scatter_dimension=0, tiled=True
        ).astype(jnp.float32),
        lax.psum_scatter(
            gateup_part.astype(jnp.bfloat16), "dp", scatter_dimension=1, tiled=True
        ).astype(jnp.float32),
        lax.psum_scatter(
            down_part.astype(jnp.bfloat16), "dp", scatter_dimension=0, tiled=True
        ).astype(jnp.float32),
    )
    channels = conv_part.shape[1]
    channel_start = lax.axis_index("tensor") * channels
    placed = lax.dynamic_update_slice_in_dim(
        jnp.zeros((kernel_len, channels * lax.axis_size("tensor")), jnp.float32),
        conv_part,
        channel_start,
        1,
    )
    gains_grad, conv_total = lax.psum(
        (jnp.stack([gain_one_part, gain_two_part]), placed), ("dp", "tensor")
    )
    conv_grad = lax.dynamic_slice_in_dim(conv_total, channel_start, channels, 1)
    in_updated, in_momentum, in_variance = adamw(
        in_weight, in_grad, in_first, in_second, rate_matrix, decay_matrix
    )
    conv_updated, conv_momentum, conv_variance = adamw(
        conv_weight, conv_grad, conv_first, conv_second, rate_small, 0.0
    )
    out_updated, out_momentum, out_variance = adamw(
        out_weight, out_grad, out_first, out_second, rate_matrix, decay_matrix
    )
    gateup_updated, gateup_momentum, gateup_variance = adamw(
        gateup_weight, gateup_grad, gateup_first, gateup_second, rate_matrix, decay_matrix
    )
    down_updated, down_momentum, down_variance = adamw(
        down_weight, down_grad, down_first, down_second, rate_matrix, decay_matrix
    )
    gains_updated, gains_momentum, gains_variance = adamw(
        norm_gains, gains_grad, gains_first, gains_second, rate_small, 0.0
    )
    return (
        block_out,
        input_grad,
        in_grad,
        conv_grad,
        out_grad,
        gateup_grad,
        down_grad,
        gains_grad,
        in_updated,
        conv_updated,
        out_updated,
        gateup_updated,
        down_updated,
        gains_updated,
        in_momentum,
        in_variance,
        conv_momentum,
        conv_variance,
        out_momentum,
        out_variance,
        gateup_momentum,
        gateup_variance,
        down_momentum,
        down_variance,
        gains_momentum,
        gains_variance,
    )


def solution(mesh):
    in_specs = (
        P(("dp", "tensor"), None),
        P(("dp", "tensor"), None),
        P(None, "dp", "tensor"),
        P(None, "tensor"),
        P("dp", "tensor"),
        P(None, "dp", "tensor"),
        P("dp", "tensor"),
        P(),
        P(None, "dp", "tensor"),
        P(None, "dp", "tensor"),
        P(None, "tensor"),
        P(None, "tensor"),
        P("dp", "tensor"),
        P("dp", "tensor"),
        P(None, "dp", "tensor"),
        P(None, "dp", "tensor"),
        P("dp", "tensor"),
        P("dp", "tensor"),
        P(),
        P(),
    )
    out_specs = (
        P(("dp", "tensor"), None),
        P(("dp", "tensor"), None),
        P(None, "dp", "tensor"),
        P(None, "tensor"),
        P("dp", "tensor"),
        P(None, "dp", "tensor"),
        P("dp", "tensor"),
        P(),
        P(None, "dp", "tensor"),
        P(None, "tensor"),
        P("dp", "tensor"),
        P(None, "dp", "tensor"),
        P("dp", "tensor"),
        P(),
        P(None, "dp", "tensor"),
        P(None, "dp", "tensor"),
        P(None, "tensor"),
        P(None, "tensor"),
        P("dp", "tensor"),
        P("dp", "tensor"),
        P(None, "dp", "tensor"),
        P(None, "dp", "tensor"),
        P("dp", "tensor"),
        P("dp", "tensor"),
        P(),
        P(),
    )
    return jax.shard_map(
        per_device, mesh=mesh, in_specs=in_specs, out_specs=out_specs, check_vma=False
    )
```

```python
import functools

import jax
import jax.numpy as jnp
from jax import lax
from jax.experimental import pallas as pl
from jax.experimental.pallas import tpu as pltpu
from jax.sharding import PartitionSpec as P

STEP = 3


eps_norm = 1e-05
beta_one = 0.9
beta_two = 0.95
adam_eps = 1e-08
decay_matrix = 0.1
rate_matrix = 0.03
rate_small = 0.5


def adamw(weight, gradient, first, second, rate, decay_rate):
    momentum = beta_one * first + (1.0 - beta_one) * gradient
    variance = beta_two * second + (1.0 - beta_two) * gradient * gradient
    corrected = momentum / (1.0 - beta_one**STEP)
    spread = variance / (1.0 - beta_two**STEP)
    updated = weight - rate * (corrected / (jnp.sqrt(spread) + adam_eps) + decay_rate * weight)
    return (updated, momentum, variance)


MESH = pl.DeviceIdType.MESH
BF = jnp.bfloat16
F32 = jnp.float32
NN = (((1,), (0,)), ((), ()))
NT = (((1,), (1,)), ((), ()))
TN = (((0,), (0,)), ((), ()))
VMEM_LIMIT = 63 * 1024 * 1024


def dot(left, right, dims=NN):
    return lax.dot_general(left, right, dims, preferred_element_type=F32)


class Ring:
    def __init__(self, n, rows):
        self.n, self.rows = n, rows
        self.sends = n - 1
        d = lax.axis_index("dp")
        t = lax.axis_index("tensor")
        self.d, self.t = d, t
        self.y, self.c = lax.div(t, 2), lax.rem(t, 2)
        self.pos = lax.div(d, 2) + lax.rem(d, 2) * (n - 1 - 2 * lax.div(d, 2))
        self.next = (self.at(self.pos + 1), t)
        self.prev = (self.at(self.pos - 1), t)
        self.core = (d, self.y * 2 + (1 - self.c))
        self.over = (d, (1 - self.y) * 2 + self.c)
        first = (rows // 2 + 15) // 16 * 16
        self.units = ((0, first), (first, rows - first))

    def at(self, q):
        n = self.n
        q = lax.rem(q + 2 * n, n)
        back = lax.div(q, n // 2)
        return (1 - back) * 2 * q + back * (2 * (n - 1 - q) + 1)

    def span(self, q, u):
        start, size = self.units[u]
        return pl.ds(pl.multiple_of(self.at(q) * self.rows + start, 16), size)

    def barrier(self):
        sem = pltpu.get_barrier_semaphore()
        for device in (self.next, self.prev, self.core, self.over):
            pl.semaphore_signal(sem, inc=1, device_id=device, device_id_type=MESH)
        pl.semaphore_wait(sem, 4)


class Gather:
    def __init__(self, ring, mats, send_sem, recv_sem):
        self.ring, self.mats = ring, mats
        self.send_sem, self.recv_sem = send_sem, recv_sem
        self.sent, self.got = 0, set()
        self.total = ring.sends * len(mats)

    def copy(self, index, way, arriving):
        stream, j = divmod(index, self.ring.sends)
        hop, sub = j // 2 + 1, j % 2
        u = sub if way == 0 else 1 - sub
        sign = 1 if way == 0 else -1
        q = self.ring.pos - sign * (hop if arriving else hop - 1)
        ref = self.mats[stream].at[self.ring.span(q, u)]
        return pltpu.make_async_remote_copy(
            ref,
            ref,
            self.send_sem.at[way, index],
            self.recv_sem.at[way, index],
            device_id=self.ring.next if way == 0 else self.ring.prev,
            device_id_type=MESH,
        )

    def wait(self, index):
        if index not in self.got:
            self.got.add(index)
            for way in (0, 1):
                self.copy(index, way, True).wait_recv()

    def upto(self, stream, j):
        if stream >= len(self.mats):
            return
        stop = stream * self.ring.sends + -(-j * self.ring.sends // 7)
        while self.sent < stop:
            index = self.sent
            if index % self.ring.sends >= 2:
                self.wait(index - 2)
            for way in (0, 1):
                self.copy(index, way, False).start()
            self.sent += 1

    def complete(self, stream):
        self.upto(stream, 7)
        self.upto(stream + 1, 2)
        for index in range(stream * self.ring.sends, (stream + 1) * self.ring.sends):
            self.wait(index)

    def drain(self):
        for index in range(self.total):
            for way in (0, 1):
                self.copy(index, way, False).wait_send()


class Tokens:
    def __init__(self, ring, full, send_sem, recv_sem, base):
        self.ring, self.full = ring, full
        self.rows = full.shape[0] // 4
        self.send_sem, self.recv_sem, self.base = send_sem, recv_sem, base

    def copy(self, kind, arriving):
        y, c = self.ring.y, self.ring.c
        other_y, other_c = 1 - y, 1 - c
        if kind == 0:
            owner = (other_y if arriving else y) * 2 + c
        elif kind == 1:
            owner = y * 2 + (other_c if arriving else c)
        else:
            owner = other_y * 2 + (other_c if arriving else c)
        ref = self.full.at[pl.ds(pl.multiple_of(owner * self.rows, 16), self.rows)]
        return pltpu.make_async_remote_copy(
            ref,
            ref,
            self.send_sem.at[self.base + kind],
            self.recv_sem.at[self.base + kind],
            device_id=self.ring.over if kind == 0 else self.ring.core,
            device_id_type=MESH,
        )

    def start(self):
        self.copy(0, False).start()
        self.copy(1, False).start()

    def forward(self):
        self.copy(0, True).wait_recv()
        self.copy(2, False).start()
        self.copy(1, True).wait_recv()

    def finish(self):
        self.copy(2, True).wait_recv()

    def drain(self):
        for kind in range(3):
            self.copy(kind, False).wait_send()


class Sums:
    def __init__(self, ring, out, got, send_sem, recv_sem, use, over_slot=1):
        self.ring, self.out, self.got = ring, out, got
        self.send_sem, self.recv_sem, self.base = send_sem, recv_sem, use * 3
        self.slots = (0, over_slot, 2)

    def owner(self, kind):
        y, c = self.ring.y, self.ring.c
        return ((1 - y) * 2 + 1 - c, (1 - y) * 2 + c, y * 2 + 1 - c, y * 2 + c)[kind]

    def copy(self, kind):
        return pltpu.make_async_remote_copy(
            self.out.at[kind],
            self.got.at[self.slots[kind]],
            self.send_sem.at[self.base + kind],
            self.recv_sem.at[self.base + kind],
            device_id=self.ring.over if kind == 1 else self.ring.core,
            device_id_type=MESH,
        )

    def far(self, block):
        self.out[0] = block(self.owner(0)).astype(BF)
        self.copy(0).start()
        part = block(self.owner(1))
        self.copy(0).wait_recv()
        self.out[1] = (part + self.got[0].astype(F32)).astype(BF)
        self.copy(1).start()

    def near(self, block):
        self.out[2] = block(self.owner(2)).astype(BF)
        self.copy(2).start()
        return block(self.owner(3))

    def arrive(self):
        self.copy(2).wait_recv()
        self.copy(1).wait_recv()

    def total(self, part, here):
        return part + self.got[2, here].astype(F32) + self.got[self.slots[1], here].astype(F32)

    def drain(self):
        for kind in range(3):
            self.copy(kind).wait_send()


def forward_kernel(
    n,
    block_ref,
    gains_ref,
    conv_ref,
    in_ref,
    out_ref,
    gateup_ref,
    down_ref,
    cot_ref,
    wc_hbm,
    wg_hbm,
    wu_hbm,
    wd_hbm,
    one_hbm,
    two_hbm,
    fcot_hbm,
    proj_hbm,
    gate_hbm,
    up_hbm,
    hidden_hbm,
    dgrad_hbm,
    middle_ref,
    wc,
    wg,
    wu,
    low_d,
    stage_c,
    stage_m,
    cot,
    full_one,
    full_two,
    full_cot,
    proj,
    mixer,
    gate_t,
    up_t,
    hidden,
    grad_t,
    sum_out,
    sum_got,
    send_sem,
    recv_sem,
    tok_send,
    tok_recv,
    sum_send,
    sum_recv,
    in_sem,
    save_sem,
    tile_sem,
):
    rows = wc.shape[0] // n
    ring = Ring(n, rows)
    tokens = block_ref.shape[0]
    chan = out_ref.shape[1]
    seq = full_one.shape[0]
    taps = conv_ref.shape[0]
    own = pl.ds(pl.multiple_of(ring.d * rows, 16), rows)
    mine = pl.ds(pl.multiple_of(ring.t * tokens, 16), tokens)

    loads = [pltpu.make_async_copy(in_ref.at[k], stage_c.at[k], in_sem.at[k]) for k in range(3)]
    loads.append(pltpu.make_async_copy(out_ref, stage_c.at[3], in_sem.at[3]))
    loads.append(pltpu.make_async_copy(gateup_ref.at[0], stage_m.at[0], in_sem.at[4]))
    loads.append(pltpu.make_async_copy(gateup_ref.at[1], stage_m.at[1], in_sem.at[5]))
    loads.append(pltpu.make_async_copy(down_ref, stage_m.at[0], in_sem.at[6]))
    loads.append(pltpu.make_async_copy(cot_ref, cot, in_sem.at[7]))
    for k in (0, 1, 2, 3, 4, 5, 7):
        loads[k].start()
    saves = []

    def save(source, target):
        copy = pltpu.make_async_copy(source, target, save_sem.at[len(saves)])
        copy.start()
        saves.append(copy)

    ring.barrier()
    gather = Gather(ring, (wc, wg, wu, wd_hbm), send_sem, recv_sem)
    for k in range(4):
        loads[k].wait()
        wc[own, k * chan : (k + 1) * chan] = stage_c[k].astype(BF)
    gather.upto(0, 2)

    values = block_ref[...]
    scale = lax.rsqrt(jnp.mean(values * values, axis=1, keepdims=True) + eps_norm)
    full_one[mine] = (values * scale * gains_ref[0:1]).astype(BF)
    ones = Tokens(ring, full_one, tok_send, tok_recv, 0)
    ones.start()
    for k, mat in enumerate((wg, wu)):
        loads[4 + k].wait()
        mat[own] = stage_m[k].astype(BF)
        if k == 0:
            loads[6].start()
    loads[6].wait()
    low_d[...] = stage_m[0].astype(BF)
    place = pltpu.make_async_copy(low_d, wd_hbm.at[own], in_sem.at[8])
    place.start()
    loads[7].wait()
    full_cot[mine] = cot[...].astype(BF)
    gather.upto(0, 5)
    ones.forward()
    cots = Tokens(ring, full_cot, tok_send, tok_recv, 3)
    cots.start()
    gather.upto(0, 7)
    ones.finish()
    gather.complete(0)
    save(wc, wc_hbm)
    save(full_one, one_hbm)

    tile = tokens
    proj[0:8] = jnp.zeros((8, 3 * chan), F32)

    def project(i, carry):
        proj[pl.ds(pl.multiple_of(i * tile + 8, 8), tile)] = dot(
            full_one[pl.ds(pl.multiple_of(i * tile, 16), tile)], wc[:, : 3 * chan]
        )
        return carry

    lax.fori_loop(0, seq // tile, project, 0)
    gather.upto(1, 3)

    def convolve(i, carry):
        here = pl.ds(pl.multiple_of(i * tile, 8), tile + 8)
        mixed = proj[here, :chan] * proj[here, 2 * chan :]
        total = conv_ref[taps - 1 : taps] * mixed[8:]
        for back in range(1, taps):
            total += conv_ref[taps - 1 - back : taps - back] * pltpu.roll(mixed, back, 0)[8:]
        c_part = proj[pl.ds(pl.multiple_of(i * tile + 8, 8), tile), chan : 2 * chan]
        mixer[pl.ds(pl.multiple_of(i * tile, 16), tile)] = (c_part * total).astype(BF)
        return carry

    lax.fori_loop(0, seq // tile, convolve, 0)
    save(proj, proj_hbm)

    def out_block(owner):
        here = pl.ds(pl.multiple_of(owner * tokens, 16), tokens)
        return dot(mixer[here], wc[:, 3 * chan :], NT)

    mids = Sums(ring, sum_out, sum_got, sum_send, sum_recv, 0)
    mids.far(out_block)
    part = mids.near(out_block)
    middle_ref[...] = part
    cots.forward()
    cots.finish()
    gather.upto(1, 5)
    save(full_cot, fcot_hbm)
    mids.arrive()
    middle = block_ref[...] + mids.total(middle_ref[...], slice(None))
    middle_ref[...] = middle
    scale = lax.rsqrt(jnp.mean(middle * middle, axis=1, keepdims=True) + eps_norm)
    full_two[mine] = (middle * scale * gains_ref[1:2]).astype(BF)
    twos = Tokens(ring, full_two, tok_send, tok_recv, 6)
    twos.start()
    gather.upto(1, 7)
    gather.upto(2, 2)
    twos.forward()
    twos.finish()
    save(full_two, two_hbm)
    gather.complete(1)
    save(wg, wg_hbm)
    place.wait()
    gather.complete(2)
    save(wu, wu_hbm)

    step = tokens // 2
    count = seq // step

    def out_copy(slot, kind, i):
        source, target = ((gate_t, gate_hbm), (up_t, up_hbm))[kind]
        here = pl.ds(pl.multiple_of(i * step, 8), step)
        return pltpu.make_async_copy(source.at[slot], target.at[here], tile_sem.at[kind, slot])

    def gated(i, carry):
        slot = lax.rem(i, 2)
        here = pl.ds(pl.multiple_of(i * step, 16), step)

        @pl.when(i >= 2)
        def _():
            out_copy(slot, 0, i).wait()
            out_copy(slot, 1, i).wait()

        x = full_two[here]
        gate = dot(x, wg[...])
        gate_t[slot] = gate
        up = dot(x, wu[...])
        up_t[slot] = up
        out_copy(slot, 0, i).start()
        out_copy(slot, 1, i).start()
        hidden[here] = (gate * jax.nn.sigmoid(gate) * up).astype(BF)
        return carry

    lax.fori_loop(0, count // 2, gated, 0)
    gather.upto(3, 4)
    lax.fori_loop(count // 2, count, gated, 0)
    for slot in (0, 1):
        for kind in (0, 1):
            out_copy(slot, kind, slot).wait()
    save(hidden, hidden_hbm)
    gather.upto(3, 6)

    width = tokens
    deep = wc.shape[0] // width

    def grad_copy(slot, i):
        here = pl.ds(pl.multiple_of(i * width, 16), width)
        return pltpu.make_async_copy(grad_t.at[slot], dgrad_hbm.at[here], tile_sem.at[2, slot])

    def graded(i, carry):
        slot = lax.rem(i, 2)

        @pl.when(i >= 2)
        def _():
            grad_copy(slot, i).wait()

        x = full_cot[:, pl.ds(pl.multiple_of(i * width, 128), width)]
        grad_t[slot] = dot(x, hidden[...], TN).astype(BF)
        grad_copy(slot, i).start()
        return carry

    lax.fori_loop(0, deep // 2, graded, 0)
    gather.upto(3, 7)
    lax.fori_loop(deep // 2, deep, graded, 0)
    for slot in (0, 1):
        grad_copy(slot, slot).wait()
    gather.complete(3)
    for copy in saves:
        copy.wait()
    for group in (ones, cots, twos, mids):
        group.drain()
    gather.drain()


def forward(n, block_in, cotangent, in_weight, conv_weight, out_weight, gateup_weight, down_weight, norm_gains):
    tokens, model = block_in.shape
    seq = tokens * 4
    chan = out_weight.shape[1]
    units = down_weight.shape[1]
    rows = out_weight.shape[0]
    sends = 4 * (n - 1)
    any_spec = pl.BlockSpec(memory_space=pl.ANY)
    vmem = pl.BlockSpec(memory_space=pltpu.VMEM)
    shape = jax.ShapeDtypeStruct
    dma = pltpu.SemaphoreType.DMA
    return pl.pallas_call(
        functools.partial(forward_kernel, n),
        out_shape=[
            shape((model, 4 * chan), BF),
            shape((model, units), BF),
            shape((model, units), BF),
            shape((model, units), BF),
            shape((seq, model), BF),
            shape((seq, model), BF),
            shape((seq, model), BF),
            shape((seq + 8, 3 * chan), F32),
            shape((seq, units), F32),
            shape((seq, units), F32),
            shape((seq, units), BF),
            shape((model, units), BF),
            shape((tokens, model), F32),
        ],
        in_specs=[vmem, vmem, vmem] + [any_spec] * 5,
        out_specs=[any_spec] * 12 + [vmem],
        scratch_shapes=[
            pltpu.VMEM((model, 4 * chan), BF),
            pltpu.VMEM((model, units), BF),
            pltpu.VMEM((model, units), BF),
            pltpu.VMEM((rows, units), BF),
            pltpu.VMEM((4, rows, chan), F32),
            pltpu.VMEM((2, rows, units), F32),
            pltpu.VMEM((tokens, model), F32),
            pltpu.VMEM((seq, model), BF),
            pltpu.VMEM((seq, model), BF),
            pltpu.VMEM((seq, model), BF),
            pltpu.VMEM((seq + 8, 3 * chan), F32),
            pltpu.VMEM((seq, chan), BF),
            pltpu.VMEM((2, tokens // 2, units), F32),
            pltpu.VMEM((2, tokens // 2, units), F32),
            pltpu.VMEM((seq, units), BF),
            pltpu.VMEM((2, tokens, units), BF),
            pltpu.VMEM((3, tokens, model), BF),
            pltpu.VMEM((3, tokens, model), BF),
            dma((2, sends)),
            dma((2, sends)),
            dma((9,)),
            dma((9,)),
            dma((3,)),
            dma((3,)),
            dma((9,)),
            dma((10,)),
            dma((3, 2)),
        ],
        compiler_params=pltpu.CompilerParams(
            collective_id=0, has_side_effects=True, vmem_limit_bytes=VMEM_LIMIT
        ),
        cost_estimate=pl.CostEstimate(flops=10 * seq * model * units, bytes_accessed=10**8, transcendentals=0),
    )(block_in, norm_gains, conv_weight, in_weight, out_weight, gateup_weight, down_weight, cotangent)


class Scatter:
    def __init__(self, ring, mats, outs, slots, stage, send_sem, recv_sem, credit_sem, out_sem):
        self.ring, self.mats, self.outs = ring, mats, outs
        self.slots, self.stage = slots, stage
        self.send_sem, self.recv_sem = send_sem, recv_sem
        self.credit_sem, self.out_sem = credit_sem, out_sem
        self.depth = slots.shape[1]
        self.total = ring.sends * len(mats)
        self.sent, self.used, self.left = 0, 0, set()

    def place(self, index, way):
        stream, j = divmod(index, self.ring.sends)
        away = self.ring.n // 2 - (j + 1) // 2
        return stream, away, j % 2 if way == 0 else 1 - j % 2

    def mat_span(self, index, way, shift):
        stream, away, u = self.place(index, way)
        sign = 1 if way == 0 else -1
        return self.ring.span(self.ring.pos + sign * (away - shift), u)

    def slot(self, index, way):
        stream, _, u = self.place(index, way)
        cols = self.mats[stream].shape[1]
        return self.slots.at[way, index % self.depth, : self.ring.units[u][1], :cols]

    def copy(self, index, way):
        stream = self.place(index, way)[0]
        return pltpu.make_async_remote_copy(
            self.mats[stream].at[self.mat_span(index, way, 0)],
            self.slot(index, way),
            self.send_sem.at[way, index],
            self.recv_sem.at[way, index],
            device_id=self.ring.next if way == 0 else self.ring.prev,
            device_id_type=MESH,
        )

    def out_copy(self, stream, u):
        start, size = self.ring.units[u]
        cols = self.mats[stream].shape[1]
        slot = stream % 2 * 2 + u
        return pltpu.make_async_copy(
            self.stage.at[slot, :size, :cols],
            self.outs[stream].at[pl.ds(start, size)],
            self.out_sem.at[slot],
        )

    def consume(self, index):
        stream, j = divmod(index, self.ring.sends)
        last = self.ring.sends - 1
        for way in (0, 1):
            u = self.place(index, way)[2]
            size = self.ring.units[u][1]
            self.copy(index, way).wait_recv()
            mat = self.mats[stream]
            cols = mat.shape[1]
            here = self.mat_span(index, way, 1)
            got = self.slots[way, index % self.depth, :size, :cols].astype(F32)
            if j < last - 1:
                mat[here] = (mat[here].astype(F32) + got).astype(BF)
            else:
                slot = stream % 2 * 2 + u
                if j == last - 1:
                    if stream >= 2:
                        self.out_copy(stream - 2, u).wait()
                    self.stage[slot, :size, :cols] = mat[here].astype(F32) + got
                else:
                    self.stage[slot, :size, :cols] = self.stage[slot, :size, :cols] + got
                    self.out_copy(stream, u).start()
            if index + self.depth < self.total:
                pl.semaphore_signal(
                    self.credit_sem.at[way],
                    inc=1,
                    device_id=self.ring.prev if way == 0 else self.ring.next,
                    device_id_type=MESH,
                )

    def use(self, stop):
        while self.used < stop:
            self.consume(self.used)
            self.used += 1

    def upto(self, stream, j):
        stop = min(self.total, stream * self.ring.sends + -(-j * self.ring.sends // 7))
        while self.sent < stop:
            index = self.sent
            if index % self.ring.sends >= 2:
                self.use(index - 1)
            for way in (0, 1):
                if index >= self.depth:
                    pl.semaphore_wait(self.credit_sem.at[way], 1)
                self.copy(index, way).start()
            self.sent += 1

    def leave(self, stream):
        for index in range(stream * self.ring.sends, (stream + 1) * self.ring.sends):
            if index not in self.left:
                self.left.add(index)
                for way in (0, 1):
                    self.copy(index, way).wait_send()

    def drain(self):
        self.use(self.total)
        streams = len(self.mats)
        for stream in range(streams):
            self.leave(stream)
        for stream in range(max(0, streams - 2), streams):
            for u in (0, 1):
                self.out_copy(stream, u).wait()


def backward_kernel(
    n,
    gains_ref,
    conv_ref,
    wc_hbm,
    wg_hbm,
    wu_hbm,
    wd_hbm,
    one_hbm,
    two_hbm,
    fcot_hbm,
    proj_hbm,
    gate_hbm,
    up_hbm,
    hidden_hbm,
    dgrad_hbm,
    middle_hbm,
    block_hbm,
    cot_hbm,
    down_out,
    gate_out,
    up_out,
    conv_out,
    block_out,
    input_out,
    small_out,
    wd,
    wg,
    wu,
    gd,
    slots,
    full_cot,
    full_two,
    d_gate,
    d_up,
    stage,
    sum_out,
    sum_got,
    tok_a,
    tok_b,
    tok_c,
    proj_t,
    d_conv,
    taps_sum,
    small_send,
    small_got,
    send_sem,
    recv_sem,
    credit_sem,
    out_sem,
    tok_send,
    tok_recv,
    sum_send,
    sum_recv,
    ladder_send,
    ladder_recv,
    load_sem,
    tile_sem,
    proj_sem,
):
    model = wd.shape[0]
    rows = model // n
    ring = Ring(n, rows)
    tokens = tok_a.shape[0]
    seq = full_cot.shape[0]
    chan = conv_ref.shape[1]
    taps = conv_ref.shape[0]
    wc = wd.at[:, : 4 * chan]
    gc = gd.at[:, : 4 * chan]

    def load(k, source, target):
        copy = pltpu.make_async_copy(source, target, load_sem.at[k])
        copy.start()
        return copy

    load_g = load(0, dgrad_hbm, gd)
    load_c = load(1, fcot_hbm, full_cot)
    load_d = load(2, wd_hbm, wd)
    load_two = load(3, two_hbm, full_two)
    load_gate = load(4, wg_hbm, wg)
    load_up = load(5, wu_hbm, wu)
    load_mid = load(6, middle_hbm, tok_a)
    load_cot = load(7, cot_hbm, tok_b)

    step = tokens // 2
    count = seq // step

    def tile_copy(slot, kind, i):
        source = (gate_hbm, up_hbm)[kind]
        here = pl.ds(pl.multiple_of(i * step, 8), step)
        return pltpu.make_async_copy(source.at[here], stage.at[slot * 2 + kind], tile_sem.at[slot, kind])

    for kind in (0, 1):
        tile_copy(0, kind, 0).start()

    steps = [ring.core, ring.over]
    span = 1
    while span < n:
        steps.append((ring.d + span * (1 - 2 * lax.rem(lax.div(ring.d, span), 2)), ring.t))
        span *= 2
    sem = pltpu.get_barrier_semaphore()
    for device in [ring.next, ring.prev] + steps:
        pl.semaphore_signal(sem, inc=1, device_id=device, device_id_type=MESH)
    pl.semaphore_wait(sem, 2 + len(steps))

    scatter = Scatter(
        ring,
        (gd, wg, wu, gc),
        (down_out, gate_out, up_out, conv_out),
        slots,
        stage,
        send_sem,
        recv_sem,
        credit_sem,
        out_sem,
    )
    load_g.wait()
    scatter.upto(0, 2)
    load_c.wait()
    load_d.wait()

    def hidden_back(i, carry):
        slot = lax.rem(i, 2)
        here = pl.ds(pl.multiple_of(i * step, 16), step)

        @pl.when(i + 1 < count)
        def _():
            for kind in (0, 1):
                tile_copy(1 - slot, kind, i + 1).start()

        d_hidden = dot(full_cot[here], wd[...])
        for kind in (0, 1):
            tile_copy(slot, kind, i).wait()
        gate = stage[slot * 2]
        sig = jax.nn.sigmoid(gate)
        d_up[here] = (d_hidden * (gate * sig)).astype(BF)
        d_gate[here] = (d_hidden * stage[slot * 2 + 1] * sig * (1.0 + gate * (1.0 - sig))).astype(BF)
        return carry

    lax.fori_loop(0, count // 2, hidden_back, 0)
    scatter.upto(0, 3)
    lax.fori_loop(count // 2, count, hidden_back, 0)
    load_gate.wait()
    load_up.wait()
    scatter.upto(0, 4)

    def token_rows(owner):
        return pl.ds(pl.multiple_of(owner * tokens, 16), tokens)

    def two_block(owner):
        here = token_rows(owner)
        return dot(d_gate[here], wg[...], NT) + dot(d_up[here], wu[...], NT)

    twos = Sums(ring, sum_out, sum_got, sum_send, sum_recv, 0)
    twos.far(two_block)
    tok_c[...] = twos.near(two_block)
    scatter.upto(0, 5)
    load_two.wait()

    width = tokens
    deep = model // width

    def grad_into(target, columns, left, right):
        def body(i, carry):
            x = left[:, pl.ds(pl.multiple_of(i * width, 128), width)]
            target[pl.ds(pl.multiple_of(i * width, 16), width), columns] = dot(x, right[...], TN).astype(BF)
            return carry

        return body

    every = slice(None)
    lax.fori_loop(0, deep, grad_into(wg, every, full_two, d_gate), 0)
    load_hidden = load(8, hidden_hbm, d_gate)
    scatter.upto(0, 7)
    scatter.upto(1, 2)

    load_mid.wait()
    load_cot.wait()
    chunk = tokens // 4
    small_send[0] = jnp.zeros(small_send.shape[1:], F32)
    twos.arrive()

    def middle_back(i, carry):
        here = pl.ds(pl.multiple_of(i * chunk, 16), chunk)
        d_two = twos.total(tok_c[here], here)
        middle = tok_a[here]
        scale = lax.rsqrt(jnp.mean(middle * middle, axis=1, keepdims=True) + eps_norm)
        normal = middle * scale
        weighted = gains_ref[1:2] * d_two
        d_middle = tok_b[here] + scale * (
            weighted - normal * jnp.mean(weighted * normal, axis=1, keepdims=True)
        )
        small_send[0, 1:2] += jnp.sum(d_two * normal, axis=0, keepdims=True)
        tok_c[here] = d_middle
        full_cot[pl.ds(pl.multiple_of(ring.t * tokens + i * chunk, 16), chunk)] = d_middle.astype(BF)
        return carry

    lax.fori_loop(0, 4, middle_back, 0)
    mids = Tokens(ring, full_cot, tok_send, tok_recv, 0)
    mids.start()
    load_block = load(9, block_hbm, tok_b)

    lax.fori_loop(0, deep, grad_into(wu, every, full_two, d_up), 0)
    load_one = load(10, one_hbm, full_two)
    scatter.upto(1, 4)
    mids.forward()
    load_hidden.wait()
    twos.drain()

    def down_block(owner):
        return dot(d_gate[token_rows(owner)], wd[...], NT)

    downs = Sums(ring, sum_out, sum_got, sum_send, sum_recv, 1)
    downs.far(down_block)
    scatter.upto(1, 5)
    tok_a[...] = tok_a[...] + downs.near(down_block)
    load_conv = load(11, wc_hbm, wc)
    mids.finish()
    scatter.upto(1, 6)

    def proj_copy(slot, i):
        here = pl.ds(pl.multiple_of(i * step, 8), step + 8)
        return pltpu.make_async_copy(proj_hbm.at[here], proj_t.at[slot], proj_sem.at[slot])

    proj_copy((count - 1) % 2, count - 1).start()
    d_conv[pl.ds(seq, 8)] = jnp.zeros((8, chan), F32)
    taps_sum[...] = jnp.zeros(taps_sum.shape, F32)
    load_conv.wait()
    load_one.wait()

    def conv_back(k, carry):
        i = count - 1 - k
        slot = lax.rem(i, 2)

        @pl.when(i >= 1)
        def _():
            proj_copy(1 - slot, i - 1).start()

        here = pl.ds(pl.multiple_of(i * step, 16), step)
        d_mixer = dot(full_cot[here], wd[:, 3 * chan : 4 * chan])
        proj_copy(slot, i).wait()
        b_part = proj_t[slot, :, :chan]
        c_part = proj_t[slot, 8:, chan : 2 * chan]
        v_part = proj_t[slot, :, 2 * chan :]
        mixed = b_part * v_part
        shifted = [mixed[8:]] + [pltpu.roll(mixed, back, 0)[8:] for back in range(1, taps)]
        total = sum(conv_ref[taps - 1 - back : taps - back] * shifted[back] for back in range(taps))
        d_c = d_mixer * total
        d_here = d_mixer * c_part
        d_up[here, :chan] = (c_part * total).astype(BF)
        d_conv[pl.ds(pl.multiple_of(i * step, 8), step)] = d_here
        for back in range(taps):
            at = taps - 1 - back
            taps_sum[at : at + 1] += jnp.sum(d_here * shifted[back], axis=0, keepdims=True)
        longer = d_conv[pl.ds(pl.multiple_of(i * step, 8), step + 8)]
        d_mixed = conv_ref[taps - 1 : taps] * d_here
        for ahead in range(1, taps):
            moved = pltpu.roll(longer, step + 8 - ahead, 0)[:step]
            d_mixed += conv_ref[taps - 1 - ahead : taps - ahead] * moved
        d_gate[here, :chan] = (d_mixed * v_part[8:]).astype(BF)
        d_gate[here, chan : 2 * chan] = d_c.astype(BF)
        d_gate[here, 2 * chan : 3 * chan] = (d_mixed * b_part[8:]).astype(BF)
        return carry

    lax.fori_loop(0, count // 2, conv_back, 0)
    scatter.upto(1, 7)
    scatter.upto(2, 2)
    lax.fori_loop(count // 2, count, conv_back, 0)
    small_send[0, 2 : 2 + taps, :chan] = taps_sum[:taps]
    scatter.upto(2, 3)

    def one_block(owner):
        return dot(d_gate[token_rows(owner), : 3 * chan], wd[:, : 3 * chan], NT)

    downs.arrive()

    def block_done(i, carry):
        here = pl.ds(pl.multiple_of(i * chunk, 16), chunk)
        tok_a[here] = downs.total(tok_a[here], here)
        return carry

    lax.fori_loop(0, 4, block_done, 0)
    save_block = load(12, tok_a, block_out)
    downs.drain()
    save_block.wait()
    ones = Sums(ring, sum_out, sum_got, sum_send, sum_recv, 2, 3)
    ones.far(one_block)
    tok_a[...] = ones.near(one_block)
    scatter.leave(0)
    proj_one = slice(0, 3 * chan)
    mix_cols = slice(3 * chan, 4 * chan)

    def in_grad(i, carry):
        x = full_two[:, pl.ds(pl.multiple_of(i * width, 128), width)]
        gd[pl.ds(pl.multiple_of(i * width, 16), width), proj_one] = dot(x, d_gate[:, proj_one], TN).astype(BF)
        z = full_cot[:, pl.ds(pl.multiple_of(i * width, 128), width)]
        gd[pl.ds(pl.multiple_of(i * width, 16), width), mix_cols] = dot(z, d_up[:, :chan], TN).astype(BF)
        return carry

    scatter.upto(2, 4)
    lax.fori_loop(0, deep, in_grad, 0)
    scatter.upto(2, 5)
    load_block.wait()
    ones.arrive()

    def input_back(i, carry):
        here = pl.ds(pl.multiple_of(i * chunk, 16), chunk)
        d_one = ones.total(tok_a[here], here)
        values = tok_b[here]
        scale = lax.rsqrt(jnp.mean(values * values, axis=1, keepdims=True) + eps_norm)
        normal = values * scale
        weighted = gains_ref[0:1] * d_one
        tok_c[here] = tok_c[here] + scale * (
            weighted - normal * jnp.mean(weighted * normal, axis=1, keepdims=True)
        )
        small_send[0, 0:1] += jnp.sum(d_one * normal, axis=0, keepdims=True)
        return carry

    lax.fori_loop(0, 4, input_back, 0)
    save_input = load(13, tok_c, input_out)
    scatter.upto(2, 6)

    ladder = [
        pltpu.make_async_remote_copy(
            small_send.at[k],
            small_got.at[k],
            ladder_send.at[k],
            ladder_recv.at[k],
            device_id=device,
            device_id_type=MESH,
        )
        for k, device in enumerate(steps)
    ]
    for k in range(len(steps)):
        ladder[k].start()
        scatter.upto(*((2, 7), (3, 2), (3, 3), (3, 4), (3, 5))[min(k, 4)])
        ladder[k].wait_recv()
        if k < 2:
            small_send[k + 1, 0:2] = small_send[k, 0:2] + small_got[k, 0:2]
            small_send[k + 1, 2:8] = small_send[k, 2:8]
        else:
            small_send[k + 1] = small_send[k] + small_got[k]
    small_out[...] = small_send[len(steps)]
    scatter.upto(3, 7)
    scatter.drain()
    mids.drain()
    ones.drain()
    for copy in ladder:
        copy.wait_send()
    save_input.wait()


def backward(n, conv_weight, norm_gains, saved, block_in, cotangent, depth=4):
    (wc, wg, wu, wd, one, two, fcot, proj, gate, up, hidden, dgrad, middle) = saved
    tokens, model = block_in.shape
    seq = tokens * 4
    chan = conv_weight.shape[1]
    units = wd.shape[1]
    rows = model // n
    sends = 4 * (n - 1)
    steps = 2 + (n - 1).bit_length()
    unit = (rows // 2 + 15) // 16 * 16
    any_spec = pl.BlockSpec(memory_space=pl.ANY)
    vmem = pl.BlockSpec(memory_space=pltpu.VMEM)
    shape = jax.ShapeDtypeStruct
    dma = pltpu.SemaphoreType.DMA
    return pl.pallas_call(
        functools.partial(backward_kernel, n),
        out_shape=[
            shape((rows, units), F32),
            shape((rows, units), F32),
            shape((rows, units), F32),
            shape((rows, 4 * chan), F32),
            shape((tokens, model), F32),
            shape((tokens, model), F32),
            shape((8, model), F32),
        ],
        in_specs=[vmem, vmem] + [any_spec] * 15,
        out_specs=[any_spec] * 6 + [vmem],
        scratch_shapes=[
            pltpu.VMEM((model, units), BF),
            pltpu.VMEM((model, units), BF),
            pltpu.VMEM((model, units), BF),
            pltpu.VMEM((model, units), BF),
            pltpu.VMEM((2, depth, unit, units), BF),
            pltpu.VMEM((seq, model), BF),
            pltpu.VMEM((seq, model), BF),
            pltpu.VMEM((seq, units), BF),
            pltpu.VMEM((seq, units), BF),
            pltpu.VMEM((4, tokens // 2, units), F32),
            pltpu.VMEM((3, tokens, model), BF),
            pltpu.VMEM((4, tokens, model), BF),
            pltpu.VMEM((tokens, model), F32),
            pltpu.VMEM((tokens, model), F32),
            pltpu.VMEM((tokens, model), F32),
            pltpu.VMEM((2, tokens // 2 + 8, 3 * chan), F32),
            pltpu.VMEM((seq + 8, chan), F32),
            pltpu.VMEM((8, chan), F32),
            pltpu.VMEM((steps + 1, 8, model), F32),
            pltpu.VMEM((steps, 8, model), F32),
            dma((2, sends)),
            dma((2, sends)),
            pltpu.SemaphoreType.REGULAR((2,)),
            dma((4,)),
            dma((3,)),
            dma((3,)),
            dma((9,)),
            dma((9,)),
            dma((steps,)),
            dma((steps,)),
            dma((14,)),
            dma((2, 2)),
            dma((2,)),
        ],
        compiler_params=pltpu.CompilerParams(
            collective_id=1, has_side_effects=True, vmem_limit_bytes=VMEM_LIMIT
        ),
        cost_estimate=pl.CostEstimate(flops=16 * seq * model * units, bytes_accessed=10**8, transcendentals=0),
    )(
        norm_gains, conv_weight, wc, wg, wu, wd, one, two, fcot, proj, gate, up, hidden, dgrad,
        middle, block_in, cotangent,
    )


def per_device(
    block_in,
    cotangent,
    in_weight,
    conv_weight,
    out_weight,
    gateup_weight,
    down_weight,
    norm_gains,
    in_first,
    in_second,
    conv_first,
    conv_second,
    out_first,
    out_second,
    gateup_first,
    gateup_second,
    down_first,
    down_second,
    gains_first,
    gains_second,
):
    n = lax.axis_size("dp")
    saved = forward(
        n,
        block_in,
        cotangent,
        in_weight,
        conv_weight,
        out_weight,
        gateup_weight,
        down_weight,
        norm_gains,
    )
    down_grad, gate_grad, up_grad, conv_grads, block_out, input_grad, small = backward(
        n, conv_weight, norm_gains, saved, block_in, cotangent
    )
    chan = conv_weight.shape[1]
    in_grad = jnp.stack([conv_grads[:, k * chan : (k + 1) * chan] for k in range(3)])
    out_grad = conv_grads[:, 3 * chan :]
    gateup_grad = jnp.stack([gate_grad, up_grad])
    gains_grad = small[0:2]
    conv_grad = small[2 : 2 + conv_weight.shape[0], :chan]
    in_updated, in_momentum, in_variance = adamw(
        in_weight, in_grad, in_first, in_second, rate_matrix, decay_matrix
    )
    conv_updated, conv_momentum, conv_variance = adamw(
        conv_weight, conv_grad, conv_first, conv_second, rate_small, 0.0
    )
    out_updated, out_momentum, out_variance = adamw(
        out_weight, out_grad, out_first, out_second, rate_matrix, decay_matrix
    )
    gateup_updated, gateup_momentum, gateup_variance = adamw(
        gateup_weight, gateup_grad, gateup_first, gateup_second, rate_matrix, decay_matrix
    )
    down_updated, down_momentum, down_variance = adamw(
        down_weight, down_grad, down_first, down_second, rate_matrix, decay_matrix
    )
    gains_updated, gains_momentum, gains_variance = adamw(
        norm_gains, gains_grad, gains_first, gains_second, rate_small, 0.0
    )
    return (
        block_out,
        input_grad,
        in_grad,
        conv_grad,
        out_grad,
        gateup_grad,
        down_grad,
        gains_grad,
        in_updated,
        conv_updated,
        out_updated,
        gateup_updated,
        down_updated,
        gains_updated,
        in_momentum,
        in_variance,
        conv_momentum,
        conv_variance,
        out_momentum,
        out_variance,
        gateup_momentum,
        gateup_variance,
        down_momentum,
        down_variance,
        gains_momentum,
        gains_variance,
    )


def solution(mesh):
    in_specs = (
        P(("dp", "tensor"), None),
        P(("dp", "tensor"), None),
        P(None, "dp", "tensor"),
        P(None, "tensor"),
        P("dp", "tensor"),
        P(None, "dp", "tensor"),
        P("dp", "tensor"),
        P(),
        P(None, "dp", "tensor"),
        P(None, "dp", "tensor"),
        P(None, "tensor"),
        P(None, "tensor"),
        P("dp", "tensor"),
        P("dp", "tensor"),
        P(None, "dp", "tensor"),
        P(None, "dp", "tensor"),
        P("dp", "tensor"),
        P("dp", "tensor"),
        P(),
        P(),
    )
    out_specs = (
        P(("dp", "tensor"), None),
        P(("dp", "tensor"), None),
        P(None, "dp", "tensor"),
        P(None, "tensor"),
        P("dp", "tensor"),
        P(None, "dp", "tensor"),
        P("dp", "tensor"),
        P(),
        P(None, "dp", "tensor"),
        P(None, "tensor"),
        P("dp", "tensor"),
        P(None, "dp", "tensor"),
        P("dp", "tensor"),
        P(),
        P(None, "dp", "tensor"),
        P(None, "dp", "tensor"),
        P(None, "tensor"),
        P(None, "tensor"),
        P("dp", "tensor"),
        P("dp", "tensor"),
        P(None, "dp", "tensor"),
        P(None, "dp", "tensor"),
        P("dp", "tensor"),
        P("dp", "tensor"),
        P(),
        P(),
    )
    return jax.shard_map(
        per_device, mesh=mesh, in_specs=in_specs, out_specs=out_specs, check_vma=False
    )
```

```python
import functools

import jax
import jax.numpy as jnp
from jax import lax
from jax.experimental import pallas as pl
from jax.experimental.pallas import tpu as pltpu
from jax.sharding import PartitionSpec as P

STEP = 3


eps_norm = 1e-05
beta_one = 0.9
beta_two = 0.95
adam_eps = 1e-08
decay_matrix = 0.1
rate_matrix = 0.03
rate_small = 0.5


def adamw(weight, gradient, first, second, rate, decay_rate):
    momentum = beta_one * first + (1.0 - beta_one) * gradient
    variance = beta_two * second + (1.0 - beta_two) * gradient * gradient
    corrected = momentum * (1.0 / (1.0 - beta_one**STEP))
    spread = variance * (1.0 / (1.0 - beta_two**STEP))
    updated = weight - rate * (corrected / (jnp.sqrt(spread) + adam_eps) + decay_rate * weight)
    return (updated, momentum, variance)


MESH = pl.DeviceIdType.MESH
BF = jnp.bfloat16
F32 = jnp.float32
NN = (((1,), (0,)), ((), ()))
NT = (((1,), (1,)), ((), ()))
TN = (((0,), (0,)), ((), ()))
VMEM_LIMIT = 63 * 1024 * 1024


def dot(left, right, dims=NN):
    return lax.dot_general(left, right, dims, preferred_element_type=F32)


class Ring:
    def __init__(self, n, rows):
        self.n, self.rows = n, rows
        self.sends = n - 1
        d = lax.axis_index("dp")
        t = lax.axis_index("tensor")
        self.d, self.t = d, t
        self.y, self.c = lax.div(t, 2), lax.rem(t, 2)
        self.pos = lax.div(d, 2) + lax.rem(d, 2) * (n - 1 - 2 * lax.div(d, 2))
        self.next = (self.at(self.pos + 1), t)
        self.prev = (self.at(self.pos - 1), t)
        self.core = (d, self.y * 2 + (1 - self.c))
        self.over = (d, (1 - self.y) * 2 + self.c)
        first = (rows // 2 + 15) // 16 * 16
        self.units = ((0, first), (first, rows - first))

    def at(self, q):
        n = self.n
        q = lax.rem(q + 2 * n, n)
        back = lax.div(q, n // 2)
        return (1 - back) * 2 * q + back * (2 * (n - 1 - q) + 1)

    def span(self, q, u):
        start, size = self.units[u]
        return pl.ds(pl.multiple_of(self.at(q) * self.rows + start, 16), size)

    def barrier(self):
        sem = pltpu.get_barrier_semaphore()
        for device in (self.next, self.prev, self.core, self.over):
            pl.semaphore_signal(sem, inc=1, device_id=device, device_id_type=MESH)
        pl.semaphore_wait(sem, 4)


class Gather:
    def __init__(self, ring, mats, send_sem, recv_sem):
        self.ring, self.mats = ring, mats
        self.send_sem, self.recv_sem = send_sem, recv_sem
        self.sent, self.got = 0, set()
        self.total = ring.sends * len(mats)

    def copy(self, index, way, arriving):
        stream, j = divmod(index, self.ring.sends)
        hop, sub = j // 2 + 1, j % 2
        u = sub if way == 0 else 1 - sub
        sign = 1 if way == 0 else -1
        q = self.ring.pos - sign * (hop if arriving else hop - 1)
        ref = self.mats[stream].at[self.ring.span(q, u)]
        return pltpu.make_async_remote_copy(
            ref,
            ref,
            self.send_sem.at[way, index],
            self.recv_sem.at[way, index],
            device_id=self.ring.next if way == 0 else self.ring.prev,
            device_id_type=MESH,
        )

    def wait(self, index):
        if index not in self.got:
            self.got.add(index)
            for way in (0, 1):
                self.copy(index, way, True).wait_recv()

    def upto(self, stream, j):
        if stream >= len(self.mats):
            return
        stop = stream * self.ring.sends + -(-j * self.ring.sends // 7)
        while self.sent < stop:
            index = self.sent
            if index % self.ring.sends >= 2:
                self.wait(index - 2)
            for way in (0, 1):
                self.copy(index, way, False).start()
            self.sent += 1

    def complete(self, stream):
        self.upto(stream, 7)
        self.upto(stream + 1, 2)
        for index in range(stream * self.ring.sends, (stream + 1) * self.ring.sends):
            self.wait(index)

    def drain(self):
        for index in range(self.total):
            for way in (0, 1):
                self.copy(index, way, False).wait_send()


class Tokens:
    def __init__(self, ring, full, send_sem, recv_sem, base):
        self.ring, self.full = ring, full
        self.rows = full.shape[0] // 4
        self.send_sem, self.recv_sem, self.base = send_sem, recv_sem, base

    def copy(self, kind, arriving):
        y, c = self.ring.y, self.ring.c
        other_y, other_c = 1 - y, 1 - c
        if kind == 0:
            owner = (other_y if arriving else y) * 2 + c
        elif kind == 1:
            owner = y * 2 + (other_c if arriving else c)
        else:
            owner = other_y * 2 + (other_c if arriving else c)
        ref = self.full.at[pl.ds(pl.multiple_of(owner * self.rows, 16), self.rows)]
        return pltpu.make_async_remote_copy(
            ref,
            ref,
            self.send_sem.at[self.base + kind],
            self.recv_sem.at[self.base + kind],
            device_id=self.ring.over if kind == 0 else self.ring.core,
            device_id_type=MESH,
        )

    def start(self):
        self.copy(0, False).start()
        self.copy(1, False).start()

    def forward(self):
        self.copy(0, True).wait_recv()
        self.copy(2, False).start()
        self.copy(1, True).wait_recv()

    def finish(self):
        self.copy(2, True).wait_recv()

    def drain(self):
        for kind in range(3):
            self.copy(kind, False).wait_send()


class Sums:
    def __init__(self, ring, out, got, send_sem, recv_sem, use, over_slot=1):
        self.ring, self.out, self.got = ring, out, got
        self.send_sem, self.recv_sem, self.base = send_sem, recv_sem, use * 3
        self.slots = (0, over_slot, 2)

    def owner(self, kind):
        y, c = self.ring.y, self.ring.c
        return ((1 - y) * 2 + 1 - c, (1 - y) * 2 + c, y * 2 + 1 - c, y * 2 + c)[kind]

    def copy(self, kind):
        return pltpu.make_async_remote_copy(
            self.out.at[kind],
            self.got.at[self.slots[kind]],
            self.send_sem.at[self.base + kind],
            self.recv_sem.at[self.base + kind],
            device_id=self.ring.over if kind == 1 else self.ring.core,
            device_id_type=MESH,
        )

    def far(self, block):
        self.out[0] = block(self.owner(0)).astype(BF)
        self.copy(0).start()
        part = block(self.owner(1))
        self.copy(0).wait_recv()
        self.out[1] = (part + self.got[0].astype(F32)).astype(BF)
        self.copy(1).start()

    def near(self, block):
        self.out[2] = block(self.owner(2)).astype(BF)
        self.copy(2).start()
        return block(self.owner(3))

    def arrive(self):
        self.copy(2).wait_recv()
        self.copy(1).wait_recv()

    def total(self, part, here):
        return part + self.got[2, here].astype(F32) + self.got[self.slots[1], here].astype(F32)

    def drain(self):
        for kind in range(3):
            self.copy(kind).wait_send()


def forward_kernel(
    n,
    block_ref,
    gains_ref,
    conv_ref,
    in_ref,
    out_ref,
    gateup_ref,
    down_ref,
    cot_ref,
    wc_hbm,
    wg_hbm,
    wu_hbm,
    wd_hbm,
    one_hbm,
    two_hbm,
    fcot_hbm,
    proj_hbm,
    gate_hbm,
    up_hbm,
    hidden_hbm,
    dgrad_hbm,
    middle_ref,
    wc,
    wg,
    wu,
    low_d,
    stage_c,
    stage_m,
    cot,
    full_one,
    full_two,
    full_cot,
    proj,
    mixer,
    gate_t,
    up_t,
    hidden,
    grad_t,
    sum_out,
    sum_got,
    send_sem,
    recv_sem,
    tok_send,
    tok_recv,
    sum_send,
    sum_recv,
    in_sem,
    save_sem,
    tile_sem,
):
    rows = wc.shape[0] // n
    ring = Ring(n, rows)
    tokens = block_ref.shape[0]
    chan = out_ref.shape[1]
    seq = full_one.shape[0]
    taps = conv_ref.shape[0]
    own = pl.ds(pl.multiple_of(ring.d * rows, 16), rows)
    mine = pl.ds(pl.multiple_of(ring.t * tokens, 16), tokens)

    loads = [pltpu.make_async_copy(in_ref.at[k], stage_c.at[k], in_sem.at[k]) for k in range(3)]
    loads.append(pltpu.make_async_copy(out_ref, stage_c.at[3], in_sem.at[3]))
    loads.append(pltpu.make_async_copy(gateup_ref.at[0], stage_m.at[0], in_sem.at[4]))
    loads.append(pltpu.make_async_copy(gateup_ref.at[1], stage_m.at[1], in_sem.at[5]))
    loads.append(pltpu.make_async_copy(down_ref, stage_m.at[0], in_sem.at[6]))
    loads.append(pltpu.make_async_copy(cot_ref, cot, in_sem.at[7]))
    for k in (0, 1, 2, 3, 4, 5, 7):
        loads[k].start()
    saves = []

    def save(source, target):
        copy = pltpu.make_async_copy(source, target, save_sem.at[len(saves)])
        copy.start()
        saves.append(copy)

    ring.barrier()
    gather = Gather(ring, (wc, wg, wu, wd_hbm), send_sem, recv_sem)
    for k in range(4):
        loads[k].wait()
        wc[own, k * chan : (k + 1) * chan] = stage_c[k].astype(BF)
    gather.upto(0, 2)

    values = block_ref[...]
    scale = lax.rsqrt(jnp.mean(values * values, axis=1, keepdims=True) + eps_norm)
    full_one[mine] = (values * scale * gains_ref[0:1]).astype(BF)
    ones = Tokens(ring, full_one, tok_send, tok_recv, 0)
    ones.start()
    for k, mat in enumerate((wg, wu)):
        loads[4 + k].wait()
        mat[own] = stage_m[k].astype(BF)
        if k == 0:
            loads[6].start()
    loads[6].wait()
    low_d[...] = stage_m[0].astype(BF)
    place = pltpu.make_async_copy(low_d, wd_hbm.at[own], in_sem.at[8])
    place.start()
    loads[7].wait()
    full_cot[mine] = cot[...].astype(BF)
    gather.upto(0, 5)
    ones.forward()
    cots = Tokens(ring, full_cot, tok_send, tok_recv, 3)
    cots.start()
    gather.upto(0, 7)
    ones.finish()
    gather.complete(0)
    save(wc, wc_hbm)
    save(full_one, one_hbm)

    tile = tokens
    proj[0:8] = jnp.zeros((8, 3 * chan), F32)

    def project(i, carry):
        proj[pl.ds(pl.multiple_of(i * tile + 8, 8), tile)] = dot(
            full_one[pl.ds(pl.multiple_of(i * tile, 16), tile)], wc[:, : 3 * chan]
        )
        return carry

    lax.fori_loop(0, seq // tile, project, 0)
    gather.upto(1, 3)

    def convolve(i, carry):
        here = pl.ds(pl.multiple_of(i * tile, 8), tile + 8)
        mixed = proj[here, :chan] * proj[here, 2 * chan :]
        total = conv_ref[taps - 1 : taps] * mixed[8:]
        for back in range(1, taps):
            total += conv_ref[taps - 1 - back : taps - back] * pltpu.roll(mixed, back, 0)[8:]
        c_part = proj[pl.ds(pl.multiple_of(i * tile + 8, 8), tile), chan : 2 * chan]
        mixer[pl.ds(pl.multiple_of(i * tile, 16), tile)] = (c_part * total).astype(BF)
        return carry

    lax.fori_loop(0, seq // tile, convolve, 0)
    save(proj, proj_hbm)

    def out_block(owner):
        here = pl.ds(pl.multiple_of(owner * tokens, 16), tokens)
        return dot(mixer[here], wc[:, 3 * chan :], NT)

    mids = Sums(ring, sum_out, sum_got, sum_send, sum_recv, 0)
    mids.far(out_block)
    part = mids.near(out_block)
    middle_ref[...] = part
    cots.forward()
    cots.finish()
    gather.upto(1, 5)
    save(full_cot, fcot_hbm)
    mids.arrive()
    middle = block_ref[...] + mids.total(middle_ref[...], slice(None))
    middle_ref[...] = middle
    scale = lax.rsqrt(jnp.mean(middle * middle, axis=1, keepdims=True) + eps_norm)
    full_two[mine] = (middle * scale * gains_ref[1:2]).astype(BF)
    twos = Tokens(ring, full_two, tok_send, tok_recv, 6)
    twos.start()
    gather.upto(1, 7)
    gather.upto(2, 2)
    twos.forward()
    twos.finish()
    save(full_two, two_hbm)
    gather.complete(1)
    save(wg, wg_hbm)
    place.wait()
    gather.complete(2)
    save(wu, wu_hbm)

    step = tokens // 2
    count = seq // step

    def out_copy(slot, kind, i):
        source, target = ((gate_t, gate_hbm), (up_t, up_hbm))[kind]
        here = pl.ds(pl.multiple_of(i * step, 8), step)
        return pltpu.make_async_copy(source.at[slot], target.at[here], tile_sem.at[kind, slot])

    def gated(i, carry):
        slot = lax.rem(i, 2)
        here = pl.ds(pl.multiple_of(i * step, 16), step)

        @pl.when(i >= 2)
        def _():
            out_copy(slot, 0, i).wait()
            out_copy(slot, 1, i).wait()

        x = full_two[here]
        gate = dot(x, wg[...])
        gate_t[slot] = gate
        up = dot(x, wu[...])
        up_t[slot] = up
        out_copy(slot, 0, i).start()
        out_copy(slot, 1, i).start()
        hidden[here] = (gate * jax.nn.sigmoid(gate) * up).astype(BF)
        return carry

    lax.fori_loop(0, count // 2, gated, 0)
    gather.upto(3, 4)
    lax.fori_loop(count // 2, count, gated, 0)
    for slot in (0, 1):
        for kind in (0, 1):
            out_copy(slot, kind, slot).wait()
    save(hidden, hidden_hbm)
    gather.upto(3, 6)

    width = tokens
    deep = wc.shape[0] // width

    def grad_copy(slot, i):
        here = pl.ds(pl.multiple_of(i * width, 16), width)
        return pltpu.make_async_copy(grad_t.at[slot], dgrad_hbm.at[here], tile_sem.at[2, slot])

    def graded(i, carry):
        slot = lax.rem(i, 2)

        @pl.when(i >= 2)
        def _():
            grad_copy(slot, i).wait()

        x = full_cot[:, pl.ds(pl.multiple_of(i * width, 128), width)]
        grad_t[slot] = dot(x, hidden[...], TN).astype(BF)
        grad_copy(slot, i).start()
        return carry

    lax.fori_loop(0, deep // 2, graded, 0)
    gather.upto(3, 7)
    lax.fori_loop(deep // 2, deep, graded, 0)
    for slot in (0, 1):
        grad_copy(slot, slot).wait()
    gather.complete(3)
    for copy in saves:
        copy.wait()
    for group in (ones, cots, twos, mids):
        group.drain()
    gather.drain()


def forward(n, block_in, cotangent, in_weight, conv_weight, out_weight, gateup_weight, down_weight, norm_gains):
    tokens, model = block_in.shape
    seq = tokens * 4
    chan = out_weight.shape[1]
    units = down_weight.shape[1]
    rows = out_weight.shape[0]
    sends = 4 * (n - 1)
    any_spec = pl.BlockSpec(memory_space=pl.ANY)
    vmem = pl.BlockSpec(memory_space=pltpu.VMEM)
    shape = jax.ShapeDtypeStruct
    dma = pltpu.SemaphoreType.DMA
    return pl.pallas_call(
        functools.partial(forward_kernel, n),
        out_shape=[
            shape((model, 4 * chan), BF),
            shape((model, units), BF),
            shape((model, units), BF),
            shape((model, units), BF),
            shape((seq, model), BF),
            shape((seq, model), BF),
            shape((seq, model), BF),
            shape((seq + 8, 3 * chan), F32),
            shape((seq, units), F32),
            shape((seq, units), F32),
            shape((seq, units), BF),
            shape((model, units), BF),
            shape((tokens, model), F32),
        ],
        in_specs=[vmem, vmem, vmem] + [any_spec] * 5,
        out_specs=[any_spec] * 12 + [vmem],
        scratch_shapes=[
            pltpu.VMEM((model, 4 * chan), BF),
            pltpu.VMEM((model, units), BF),
            pltpu.VMEM((model, units), BF),
            pltpu.VMEM((rows, units), BF),
            pltpu.VMEM((4, rows, chan), F32),
            pltpu.VMEM((2, rows, units), F32),
            pltpu.VMEM((tokens, model), F32),
            pltpu.VMEM((seq, model), BF),
            pltpu.VMEM((seq, model), BF),
            pltpu.VMEM((seq, model), BF),
            pltpu.VMEM((seq + 8, 3 * chan), F32),
            pltpu.VMEM((seq, chan), BF),
            pltpu.VMEM((2, tokens // 2, units), F32),
            pltpu.VMEM((2, tokens // 2, units), F32),
            pltpu.VMEM((seq, units), BF),
            pltpu.VMEM((2, tokens, units), BF),
            pltpu.VMEM((3, tokens, model), BF),
            pltpu.VMEM((3, tokens, model), BF),
            dma((2, sends)),
            dma((2, sends)),
            dma((9,)),
            dma((9,)),
            dma((3,)),
            dma((3,)),
            dma((9,)),
            dma((10,)),
            dma((3, 2)),
        ],
        compiler_params=pltpu.CompilerParams(
            collective_id=0, has_side_effects=True, vmem_limit_bytes=VMEM_LIMIT
        ),
        cost_estimate=pl.CostEstimate(flops=10 * seq * model * units, bytes_accessed=10**8, transcendentals=0),
    )(block_in, norm_gains, conv_weight, in_weight, out_weight, gateup_weight, down_weight, cotangent)


class Scatter:
    def __init__(self, ring, first, mats, outs, slots, stage, send_sem, recv_sem, credit_sem, out_sem):
        self.ring, self.first, self.mats, self.outs = ring, first, mats, outs
        self.slots, self.stage = slots, stage
        self.send_sem, self.recv_sem = send_sem, recv_sem
        self.credit_sem, self.out_sem = credit_sem, out_sem
        self.depth = slots.shape[1]
        self.total = ring.sends * len(mats)
        self.sent, self.used, self.left = 0, 0, set()

    def place(self, index, way):
        stream, j = divmod(index, self.ring.sends)
        away = self.ring.n // 2 - (j + 1) // 2
        return stream, away, j % 2 if way == 0 else 1 - j % 2

    def mat_span(self, index, way, shift):
        stream, away, u = self.place(index, way)
        sign = 1 if way == 0 else -1
        return self.ring.span(self.ring.pos + sign * (away - shift), u)

    def slot(self, index, way):
        stream, _, u = self.place(index, way)
        cols = self.mats[stream].shape[1]
        return self.slots.at[way, index % self.depth, : self.ring.units[u][1], :cols]

    def copy(self, index, way):
        stream = self.place(index, way)[0]
        mat = self.first if index < 2 else self.mats[stream]
        return pltpu.make_async_remote_copy(
            mat.at[self.mat_span(index, way, 0)],
            self.slot(index, way),
            self.send_sem.at[way, index],
            self.recv_sem.at[way, index],
            device_id=self.ring.next if way == 0 else self.ring.prev,
            device_id_type=MESH,
        )

    def out_copy(self, stream, u):
        start, size = self.ring.units[u]
        cols = self.mats[stream].shape[1]
        slot = stream % 2 * 2 + u
        return pltpu.make_async_copy(
            self.stage.at[slot, :size, :cols],
            self.outs[stream].at[pl.ds(start, size)],
            self.out_sem.at[slot],
        )

    def consume(self, index):
        stream, j = divmod(index, self.ring.sends)
        last = self.ring.sends - 1
        for way in (0, 1):
            u = self.place(index, way)[2]
            size = self.ring.units[u][1]
            self.copy(index, way).wait_recv()
            mat = self.mats[stream]
            cols = mat.shape[1]
            here = self.mat_span(index, way, 1)
            got = self.slots[way, index % self.depth, :size, :cols].astype(F32)
            if j < last - 1:
                mat[here] = (mat[here].astype(F32) + got).astype(BF)
            else:
                slot = stream % 2 * 2 + u
                if j == last - 1:
                    if stream >= 2:
                        self.out_copy(stream - 2, u).wait()
                    self.stage[slot, :size, :cols] = mat[here].astype(F32) + got
                else:
                    self.stage[slot, :size, :cols] = self.stage[slot, :size, :cols] + got
                    self.out_copy(stream, u).start()
            if index + self.depth < self.total:
                pl.semaphore_signal(
                    self.credit_sem.at[way],
                    inc=1,
                    device_id=self.ring.prev if way == 0 else self.ring.next,
                    device_id_type=MESH,
                )

    def use(self, stop):
        while self.used < stop:
            self.consume(self.used)
            self.used += 1

    def upto(self, stream, j):
        stop = min(self.total, stream * self.ring.sends + -(-j * self.ring.sends // 7))
        while self.sent < stop:
            index = self.sent
            if index % self.ring.sends >= 2:
                self.use(index - 1)
            for way in (0, 1):
                if index >= self.depth:
                    pl.semaphore_wait(self.credit_sem.at[way], 1)
                self.copy(index, way).start()
            self.sent += 1

    def leave(self, stream):
        for index in range(stream * self.ring.sends, (stream + 1) * self.ring.sends):
            if index not in self.left:
                self.left.add(index)
                for way in (0, 1):
                    self.copy(index, way).wait_send()

    def drain(self):
        self.use(self.total)
        streams = len(self.mats)
        for stream in range(streams):
            self.leave(stream)
        for stream in range(max(0, streams - 2), streams):
            for u in (0, 1):
                self.out_copy(stream, u).wait()


def backward_kernel(
    n,
    gains_ref,
    conv_ref,
    wc_hbm,
    wg_hbm,
    wu_hbm,
    wd_hbm,
    one_hbm,
    two_hbm,
    fcot_hbm,
    proj_hbm,
    gate_hbm,
    up_hbm,
    hidden_hbm,
    dgrad_hbm,
    middle_hbm,
    block_hbm,
    cot_hbm,
    down_out,
    gate_out,
    up_out,
    conv_out,
    block_out,
    input_out,
    small_out,
    wd,
    wg,
    wu,
    gd,
    slots,
    full_cot,
    full_two,
    d_gate,
    d_up,
    stage,
    sum_out,
    sum_got,
    tok_a,
    tok_b,
    tok_c,
    proj_t,
    d_conv,
    taps_sum,
    small_send,
    small_got,
    send_sem,
    recv_sem,
    credit_sem,
    out_sem,
    tok_send,
    tok_recv,
    sum_send,
    sum_recv,
    ladder_send,
    ladder_recv,
    load_sem,
    tile_sem,
    proj_sem,
):
    model = wd.shape[0]
    rows = model // n
    ring = Ring(n, rows)
    tokens = tok_a.shape[0]
    seq = full_cot.shape[0]
    chan = conv_ref.shape[1]
    taps = conv_ref.shape[0]
    wc = wd.at[:, : 4 * chan]
    gc = gd.at[:, : 4 * chan]

    def load(k, source, target):
        copy = pltpu.make_async_copy(source, target, load_sem.at[k])
        copy.start()
        return copy

    load_g = load(0, dgrad_hbm, gd)
    load_c = load(1, fcot_hbm, full_cot)
    load_d = load(2, wd_hbm, wd)
    load_two = load(3, two_hbm, full_two)
    load_gate = load(4, wg_hbm, wg)
    load_up = load(5, wu_hbm, wu)
    load_mid = load(6, middle_hbm, tok_a)
    load_cot = load(7, cot_hbm, tok_b)

    step = tokens // 2
    count = seq // step

    def tile_copy(slot, kind, i):
        source = (gate_hbm, up_hbm)[kind]
        here = pl.ds(pl.multiple_of(i * step, 8), step)
        return pltpu.make_async_copy(source.at[here], stage.at[slot * 2 + kind], tile_sem.at[slot, kind])

    for kind in (0, 1):
        tile_copy(0, kind, 0).start()

    steps = [ring.core, ring.over]
    span = 1
    while span < n:
        steps.append((ring.d + span * (1 - 2 * lax.rem(lax.div(ring.d, span), 2)), ring.t))
        span *= 2
    sem = pltpu.get_barrier_semaphore()
    for device in [ring.next, ring.prev] + steps:
        pl.semaphore_signal(sem, inc=1, device_id=device, device_id_type=MESH)
    pl.semaphore_wait(sem, 2 + len(steps))

    scatter = Scatter(
        ring,
        dgrad_hbm,
        (gd, wg, wu, gc),
        (down_out, gate_out, up_out, conv_out),
        slots,
        stage,
        send_sem,
        recv_sem,
        credit_sem,
        out_sem,
    )
    scatter.upto(0, 2)
    load_g.wait()
    load_c.wait()
    load_d.wait()

    def hidden_back(i, carry):
        slot = lax.rem(i, 2)
        here = pl.ds(pl.multiple_of(i * step, 16), step)

        @pl.when(i + 1 < count)
        def _():
            for kind in (0, 1):
                tile_copy(1 - slot, kind, i + 1).start()

        d_hidden = dot(full_cot[here], wd[...])
        for kind in (0, 1):
            tile_copy(slot, kind, i).wait()
        gate = stage[slot * 2]
        sig = jax.nn.sigmoid(gate)
        d_up[here] = (d_hidden * (gate * sig)).astype(BF)
        d_gate[here] = (d_hidden * stage[slot * 2 + 1] * sig * (1.0 + gate * (1.0 - sig))).astype(BF)
        return carry

    lax.fori_loop(0, count // 2, hidden_back, 0)
    scatter.upto(0, 3)
    lax.fori_loop(count // 2, count, hidden_back, 0)
    load_gate.wait()
    load_up.wait()
    scatter.upto(0, 4)

    def token_rows(owner):
        return pl.ds(pl.multiple_of(owner * tokens, 16), tokens)

    def two_block(owner):
        here = token_rows(owner)
        return dot(d_gate[here], wg[...], NT) + dot(d_up[here], wu[...], NT)

    twos = Sums(ring, sum_out, sum_got, sum_send, sum_recv, 0)
    twos.far(two_block)
    tok_c[...] = twos.near(two_block)
    scatter.upto(0, 5)
    load_two.wait()

    width = tokens
    deep = model // width

    def grad_into(target, columns, left, right):
        def body(i, carry):
            x = left[:, pl.ds(pl.multiple_of(i * width, 128), width)]
            target[pl.ds(pl.multiple_of(i * width, 16), width), columns] = dot(x, right[...], TN).astype(BF)
            return carry

        return body

    every = slice(None)
    lax.fori_loop(0, deep, grad_into(wg, every, full_two, d_gate), 0)
    load_hidden = load(8, hidden_hbm, d_gate)
    scatter.upto(0, 7)
    scatter.upto(1, 2)

    load_mid.wait()
    load_cot.wait()
    chunk = tokens // 4
    small_send[0] = jnp.zeros(small_send.shape[1:], F32)
    twos.arrive()

    def middle_back(i, carry):
        here = pl.ds(pl.multiple_of(i * chunk, 16), chunk)
        d_two = twos.total(tok_c[here], here)
        middle = tok_a[here]
        scale = lax.rsqrt(jnp.mean(middle * middle, axis=1, keepdims=True) + eps_norm)
        normal = middle * scale
        weighted = gains_ref[1:2] * d_two
        d_middle = tok_b[here] + scale * (
            weighted - normal * jnp.mean(weighted * normal, axis=1, keepdims=True)
        )
        small_send[0, 1:2] += jnp.sum(d_two * normal, axis=0, keepdims=True)
        tok_c[here] = d_middle
        full_cot[pl.ds(pl.multiple_of(ring.t * tokens + i * chunk, 16), chunk)] = d_middle.astype(BF)
        return carry

    lax.fori_loop(0, 4, middle_back, 0)
    mids = Tokens(ring, full_cot, tok_send, tok_recv, 0)
    mids.start()
    load_block = load(9, block_hbm, tok_b)

    lax.fori_loop(0, deep, grad_into(wu, every, full_two, d_up), 0)
    load_one = load(10, one_hbm, full_two)
    scatter.upto(1, 4)
    mids.forward()
    load_hidden.wait()
    twos.drain()

    def down_block(owner):
        return dot(d_gate[token_rows(owner)], wd[...], NT)

    downs = Sums(ring, sum_out, sum_got, sum_send, sum_recv, 1)
    downs.far(down_block)
    scatter.upto(1, 5)
    tok_a[...] = tok_a[...] + downs.near(down_block)
    load_conv = load(11, wc_hbm, wc)
    mids.finish()
    scatter.upto(1, 6)

    def proj_copy(slot, i):
        here = pl.ds(pl.multiple_of(i * step, 8), step + 8)
        return pltpu.make_async_copy(proj_hbm.at[here], proj_t.at[slot], proj_sem.at[slot])

    proj_copy((count - 1) % 2, count - 1).start()
    d_conv[pl.ds(seq, 8)] = jnp.zeros((8, chan), F32)
    taps_sum[...] = jnp.zeros(taps_sum.shape, F32)
    load_conv.wait()
    load_one.wait()

    def conv_back(k, carry):
        i = count - 1 - k
        slot = lax.rem(i, 2)

        @pl.when(i >= 1)
        def _():
            proj_copy(1 - slot, i - 1).start()

        here = pl.ds(pl.multiple_of(i * step, 16), step)
        d_mixer = dot(full_cot[here], wd[:, 3 * chan : 4 * chan])
        proj_copy(slot, i).wait()
        b_part = proj_t[slot, :, :chan]
        c_part = proj_t[slot, 8:, chan : 2 * chan]
        v_part = proj_t[slot, :, 2 * chan :]
        mixed = b_part * v_part
        shifted = [mixed[8:]] + [pltpu.roll(mixed, back, 0)[8:] for back in range(1, taps)]
        total = sum(conv_ref[taps - 1 - back : taps - back] * shifted[back] for back in range(taps))
        d_c = d_mixer * total
        d_here = d_mixer * c_part
        d_up[here, :chan] = (c_part * total).astype(BF)
        d_conv[pl.ds(pl.multiple_of(i * step, 8), step)] = d_here
        for back in range(taps):
            at = taps - 1 - back
            taps_sum[at : at + 1] += jnp.sum(d_here * shifted[back], axis=0, keepdims=True)
        longer = d_conv[pl.ds(pl.multiple_of(i * step, 8), step + 8)]
        d_mixed = conv_ref[taps - 1 : taps] * d_here
        for ahead in range(1, taps):
            moved = pltpu.roll(longer, step + 8 - ahead, 0)[:step]
            d_mixed += conv_ref[taps - 1 - ahead : taps - ahead] * moved
        d_gate[here, :chan] = (d_mixed * v_part[8:]).astype(BF)
        d_gate[here, chan : 2 * chan] = d_c.astype(BF)
        d_gate[here, 2 * chan : 3 * chan] = (d_mixed * b_part[8:]).astype(BF)
        return carry

    lax.fori_loop(0, count // 2, conv_back, 0)
    scatter.upto(1, 7)
    scatter.upto(2, 2)
    lax.fori_loop(count // 2, count, conv_back, 0)
    small_send[0, 2 : 2 + taps, :chan] = taps_sum[:taps]
    scatter.upto(2, 3)

    def one_block(owner):
        return dot(d_gate[token_rows(owner), : 3 * chan], wd[:, : 3 * chan], NT)

    downs.arrive()

    def block_done(i, carry):
        here = pl.ds(pl.multiple_of(i * chunk, 16), chunk)
        tok_a[here] = downs.total(tok_a[here], here)
        return carry

    lax.fori_loop(0, 4, block_done, 0)
    save_block = load(12, tok_a, block_out)
    downs.drain()
    save_block.wait()
    ones = Sums(ring, sum_out, sum_got, sum_send, sum_recv, 2, 3)
    ones.far(one_block)
    tok_a[...] = ones.near(one_block)
    scatter.leave(0)
    proj_one = slice(0, 3 * chan)
    mix_cols = slice(3 * chan, 4 * chan)

    def in_grad(i, carry):
        x = full_two[:, pl.ds(pl.multiple_of(i * width, 128), width)]
        gd[pl.ds(pl.multiple_of(i * width, 16), width), proj_one] = dot(x, d_gate[:, proj_one], TN).astype(BF)
        z = full_cot[:, pl.ds(pl.multiple_of(i * width, 128), width)]
        gd[pl.ds(pl.multiple_of(i * width, 16), width), mix_cols] = dot(z, d_up[:, :chan], TN).astype(BF)
        return carry

    scatter.upto(2, 4)
    lax.fori_loop(0, deep, in_grad, 0)
    scatter.upto(2, 5)
    load_block.wait()
    ones.arrive()

    def input_back(i, carry):
        here = pl.ds(pl.multiple_of(i * chunk, 16), chunk)
        d_one = ones.total(tok_a[here], here)
        values = tok_b[here]
        scale = lax.rsqrt(jnp.mean(values * values, axis=1, keepdims=True) + eps_norm)
        normal = values * scale
        weighted = gains_ref[0:1] * d_one
        tok_c[here] = tok_c[here] + scale * (
            weighted - normal * jnp.mean(weighted * normal, axis=1, keepdims=True)
        )
        small_send[0, 0:1] += jnp.sum(d_one * normal, axis=0, keepdims=True)
        return carry

    lax.fori_loop(0, 4, input_back, 0)
    save_input = load(13, tok_c, input_out)
    scatter.upto(2, 6)

    ladder = [
        pltpu.make_async_remote_copy(
            small_send.at[k],
            small_got.at[k],
            ladder_send.at[k],
            ladder_recv.at[k],
            device_id=device,
            device_id_type=MESH,
        )
        for k, device in enumerate(steps)
    ]
    for k in range(len(steps)):
        ladder[k].start()
        scatter.upto(*((2, 7), (3, 2), (3, 3), (3, 4), (3, 5))[min(k, 4)])
        ladder[k].wait_recv()
        if k < 2:
            small_send[k + 1, 0:2] = small_send[k, 0:2] + small_got[k, 0:2]
            small_send[k + 1, 2:8] = small_send[k, 2:8]
        else:
            small_send[k + 1] = small_send[k] + small_got[k]
    small_out[...] = small_send[len(steps)]
    scatter.upto(3, 7)
    scatter.drain()
    mids.drain()
    ones.drain()
    for copy in ladder:
        copy.wait_send()
    save_input.wait()


def backward(n, conv_weight, norm_gains, saved, block_in, cotangent, depth=4):
    (wc, wg, wu, wd, one, two, fcot, proj, gate, up, hidden, dgrad, middle) = saved
    tokens, model = block_in.shape
    seq = tokens * 4
    chan = conv_weight.shape[1]
    units = wd.shape[1]
    rows = model // n
    sends = 4 * (n - 1)
    steps = 2 + (n - 1).bit_length()
    unit = (rows // 2 + 15) // 16 * 16
    any_spec = pl.BlockSpec(memory_space=pl.ANY)
    vmem = pl.BlockSpec(memory_space=pltpu.VMEM)
    shape = jax.ShapeDtypeStruct
    dma = pltpu.SemaphoreType.DMA
    return pl.pallas_call(
        functools.partial(backward_kernel, n),
        out_shape=[
            shape((rows, units), F32),
            shape((rows, units), F32),
            shape((rows, units), F32),
            shape((rows, 4 * chan), F32),
            shape((tokens, model), F32),
            shape((tokens, model), F32),
            shape((8, model), F32),
        ],
        in_specs=[vmem, vmem] + [any_spec] * 15,
        out_specs=[any_spec] * 6 + [vmem],
        scratch_shapes=[
            pltpu.VMEM((model, units), BF),
            pltpu.VMEM((model, units), BF),
            pltpu.VMEM((model, units), BF),
            pltpu.VMEM((model, units), BF),
            pltpu.VMEM((2, depth, unit, units), BF),
            pltpu.VMEM((seq, model), BF),
            pltpu.VMEM((seq, model), BF),
            pltpu.VMEM((seq, units), BF),
            pltpu.VMEM((seq, units), BF),
            pltpu.VMEM((4, tokens // 2, units), F32),
            pltpu.VMEM((3, tokens, model), BF),
            pltpu.VMEM((4, tokens, model), BF),
            pltpu.VMEM((tokens, model), F32),
            pltpu.VMEM((tokens, model), F32),
            pltpu.VMEM((tokens, model), F32),
            pltpu.VMEM((2, tokens // 2 + 8, 3 * chan), F32),
            pltpu.VMEM((seq + 8, chan), F32),
            pltpu.VMEM((8, chan), F32),
            pltpu.VMEM((steps + 1, 8, model), F32),
            pltpu.VMEM((steps, 8, model), F32),
            dma((2, sends)),
            dma((2, sends)),
            pltpu.SemaphoreType.REGULAR((2,)),
            dma((4,)),
            dma((3,)),
            dma((3,)),
            dma((9,)),
            dma((9,)),
            dma((steps,)),
            dma((steps,)),
            dma((14,)),
            dma((2, 2)),
            dma((2,)),
        ],
        compiler_params=pltpu.CompilerParams(
            collective_id=1, has_side_effects=True, vmem_limit_bytes=VMEM_LIMIT
        ),
        cost_estimate=pl.CostEstimate(flops=16 * seq * model * units, bytes_accessed=10**8, transcendentals=0),
    )(
        norm_gains, conv_weight, wc, wg, wu, wd, one, two, fcot, proj, gate, up, hidden, dgrad,
        middle, block_in, cotangent,
    )


def finish_kernel(
    down_ref,
    gate_ref,
    up_ref,
    conv_ref,
    block_ref,
    input_ref,
    small_ref,
    in_w,
    in_m,
    in_v,
    out_w,
    out_m,
    out_v,
    gateup_w,
    gateup_m,
    gateup_v,
    down_w,
    down_m,
    down_v,
    taps_w,
    taps_m,
    taps_v,
    gains_w,
    gains_m,
    gains_v,
    block_out,
    input_out,
    in_grad,
    taps_grad,
    out_grad,
    gateup_grad,
    down_grad,
    gains_grad,
    in_up,
    taps_up,
    out_up,
    gateup_up,
    down_up,
    gains_up,
    in_mo,
    in_va,
    taps_mo,
    taps_va,
    out_mo,
    out_va,
    gateup_mo,
    gateup_va,
    down_mo,
    down_va,
    gains_mo,
    gains_va,
):
    chan = out_w.shape[1]
    block_out[...] = block_ref[...]
    input_out[...] = input_ref[...]
    for k in range(3):
        grad = conv_ref[:, k * chan : (k + 1) * chan]
        in_grad[k] = grad
        in_up[k], in_mo[k], in_va[k] = adamw(in_w[k], grad, in_m[k], in_v[k], rate_matrix, decay_matrix)
    grad = conv_ref[:, 3 * chan :]
    out_grad[...] = grad
    out_up[...], out_mo[...], out_va[...] = adamw(
        out_w[...], grad, out_m[...], out_v[...], rate_matrix, decay_matrix
    )
    for k, ref in enumerate((gate_ref, up_ref)):
        grad = ref[...]
        gateup_grad[k] = grad
        gateup_up[k], gateup_mo[k], gateup_va[k] = adamw(
            gateup_w[k], grad, gateup_m[k], gateup_v[k], rate_matrix, decay_matrix
        )
    grad = down_ref[...]
    down_grad[...] = grad
    down_up[...], down_mo[...], down_va[...] = adamw(
        down_w[...], grad, down_m[...], down_v[...], rate_matrix, decay_matrix
    )

    @pl.when(pl.program_id(0) == 0)
    def _():
        taps = taps_w.shape[0]
        grad = small_ref[0:2]
        gains_grad[...] = grad
        gains_up[...], gains_mo[...], gains_va[...] = adamw(
            gains_w[...], grad, gains_m[...], gains_v[...], rate_small, 0.0
        )
        grad = small_ref[2 : 2 + taps, :chan]
        taps_grad[...] = grad
        taps_up[...], taps_mo[...], taps_va[...] = adamw(
            taps_w[...], grad, taps_m[...], taps_v[...], rate_small, 0.0
        )


def finish(grads, in_set, out_set, gateup_set, down_set, taps_set, gains_set):
    rows, units = grads[0].shape
    tokens, model = grads[4].shape
    chan = out_set[0].shape[1]
    taps = taps_set[0].shape[0]
    parts = max(g for g in (1, 2, 3) if rows % (8 * g) == 0 and tokens % (8 * g) == 0)
    r, t = rows // parts, tokens // parts
    wide = lambda width: pl.BlockSpec((r, width), lambda i: (i, 0))
    deep = lambda count, width: pl.BlockSpec((count, r, width), lambda i: (0, i, 0))
    token = pl.BlockSpec((t, model), lambda i: (i, 0))
    whole = lambda *dims: pl.BlockSpec(dims, lambda i: (0, 0))
    in_spec, out_spec, gateup_spec, down_spec = deep(3, chan), wide(chan), deep(2, units), wide(units)
    taps_spec, gains_spec = whole(taps, chan), whole(2, model)
    like = lambda group: jax.ShapeDtypeStruct(group[0].shape, F32)
    shape = [jax.ShapeDtypeStruct((tokens, model), F32)] * 2
    matrices = (in_set, taps_set, out_set, gateup_set, down_set, gains_set)
    specs = (in_spec, taps_spec, out_spec, gateup_spec, down_spec, gains_spec)
    out_shape = shape + [like(m) for m in matrices] * 2
    out_specs = [token, token] + list(specs) * 2
    for m, spec in zip(matrices, specs):
        out_shape += [like(m)] * 2
        out_specs += [spec] * 2
    return pl.pallas_call(
        finish_kernel,
        grid=(parts,),
        out_shape=out_shape,
        in_specs=[wide(units)] * 3
        + [wide(4 * chan), token, token, whole(8, model)]
        + [in_spec] * 3
        + [out_spec] * 3
        + [gateup_spec] * 3
        + [down_spec] * 3
        + [taps_spec] * 3
        + [gains_spec] * 3,
        out_specs=out_specs,
        compiler_params=pltpu.CompilerParams(vmem_limit_bytes=VMEM_LIMIT),
    )(*grads, *in_set, *out_set, *gateup_set, *down_set, *taps_set, *gains_set)


def per_device(
    block_in,
    cotangent,
    in_weight,
    conv_weight,
    out_weight,
    gateup_weight,
    down_weight,
    norm_gains,
    in_first,
    in_second,
    conv_first,
    conv_second,
    out_first,
    out_second,
    gateup_first,
    gateup_second,
    down_first,
    down_second,
    gains_first,
    gains_second,
):
    n = lax.axis_size("dp")
    saved = forward(
        n,
        block_in,
        cotangent,
        in_weight,
        conv_weight,
        out_weight,
        gateup_weight,
        down_weight,
        norm_gains,
    )
    grads = backward(n, conv_weight, norm_gains, saved, block_in, cotangent)
    return tuple(
        finish(
            grads,
            (in_weight, in_first, in_second),
            (out_weight, out_first, out_second),
            (gateup_weight, gateup_first, gateup_second),
            (down_weight, down_first, down_second),
            (conv_weight, conv_first, conv_second),
            (norm_gains, gains_first, gains_second),
        )
    )


def solution(mesh):
    in_specs = (
        P(("dp", "tensor"), None),
        P(("dp", "tensor"), None),
        P(None, "dp", "tensor"),
        P(None, "tensor"),
        P("dp", "tensor"),
        P(None, "dp", "tensor"),
        P("dp", "tensor"),
        P(),
        P(None, "dp", "tensor"),
        P(None, "dp", "tensor"),
        P(None, "tensor"),
        P(None, "tensor"),
        P("dp", "tensor"),
        P("dp", "tensor"),
        P(None, "dp", "tensor"),
        P(None, "dp", "tensor"),
        P("dp", "tensor"),
        P("dp", "tensor"),
        P(),
        P(),
    )
    out_specs = (
        P(("dp", "tensor"), None),
        P(("dp", "tensor"), None),
        P(None, "dp", "tensor"),
        P(None, "tensor"),
        P("dp", "tensor"),
        P(None, "dp", "tensor"),
        P("dp", "tensor"),
        P(),
        P(None, "dp", "tensor"),
        P(None, "tensor"),
        P("dp", "tensor"),
        P(None, "dp", "tensor"),
        P("dp", "tensor"),
        P(),
        P(None, "dp", "tensor"),
        P(None, "dp", "tensor"),
        P(None, "tensor"),
        P(None, "tensor"),
        P("dp", "tensor"),
        P("dp", "tensor"),
        P(None, "dp", "tensor"),
        P(None, "dp", "tensor"),
        P("dp", "tensor"),
        P("dp", "tensor"),
        P(),
        P(),
    )
    return jax.shard_map(
        per_device, mesh=mesh, in_specs=in_specs, out_specs=out_specs, check_vma=False
    )
```

```python
import functools

import jax
import jax.numpy as jnp
from jax import lax
from jax.experimental import pallas as pl
from jax.experimental.pallas import tpu as pltpu
from jax.sharding import PartitionSpec as P

STEP = 3


eps_norm = 1e-05
beta_one = 0.9
beta_two = 0.95
adam_eps = 1e-08
decay_matrix = 0.1
rate_matrix = 0.03
rate_small = 0.5


def adamw(weight, gradient, first, second, rate, decay_rate):
    momentum = beta_one * first + (1.0 - beta_one) * gradient
    variance = beta_two * second + (1.0 - beta_two) * gradient * gradient
    corrected = momentum * (1.0 / (1.0 - beta_one**STEP))
    spread = variance * (1.0 / (1.0 - beta_two**STEP))
    updated = weight - rate * (corrected / (jnp.sqrt(spread) + adam_eps) + decay_rate * weight)
    return (updated, momentum, variance)


MESH = pl.DeviceIdType.MESH
BF = jnp.bfloat16
F32 = jnp.float32
NN = (((1,), (0,)), ((), ()))
NT = (((1,), (1,)), ((), ()))
TN = (((0,), (0,)), ((), ()))
VMEM_LIMIT = 63 * 1024 * 1024


def dot(left, right, dims=NN):
    return lax.dot_general(left, right, dims, preferred_element_type=F32)


class Ring:
    def __init__(self, n, rows):
        self.n, self.rows = n, rows
        self.sends = n - 1
        d = lax.axis_index("dp")
        t = lax.axis_index("tensor")
        self.d, self.t = d, t
        self.y, self.c = lax.div(t, 2), lax.rem(t, 2)
        self.pos = lax.div(d, 2) + lax.rem(d, 2) * (n - 1 - 2 * lax.div(d, 2))
        self.next = (self.at(self.pos + 1), t)
        self.prev = (self.at(self.pos - 1), t)
        self.core = (d, self.y * 2 + (1 - self.c))
        self.over = (d, (1 - self.y) * 2 + self.c)
        first = (rows // 2 + 15) // 16 * 16
        self.units = ((0, first), (first, rows - first))

    def at(self, q):
        n = self.n
        q = lax.rem(q + 2 * n, n)
        back = lax.div(q, n // 2)
        return (1 - back) * 2 * q + back * (2 * (n - 1 - q) + 1)

    def span(self, q, u):
        start, size = self.units[u]
        return pl.ds(pl.multiple_of(self.at(q) * self.rows + start, 16), size)

    def barrier(self):
        sem = pltpu.get_barrier_semaphore()
        for device in (self.next, self.prev, self.core, self.over):
            pl.semaphore_signal(sem, inc=1, device_id=device, device_id_type=MESH)
        pl.semaphore_wait(sem, 4)


def split(units):
    main = units // 128 * 128
    return main, units - main


class Gather:
    def __init__(self, ring, mats, send_sem, recv_sem):
        self.ring, self.mats = ring, mats
        self.send_sem, self.recv_sem = send_sem, recv_sem
        self.sent, self.got = 0, set()
        self.total = ring.sends * len(mats)

    def copy(self, index, way, arriving):
        stream, j = divmod(index, self.ring.sends)
        hop, sub = j // 2 + 1, j % 2
        u = sub if way == 0 else 1 - sub
        sign = 1 if way == 0 else -1
        q = self.ring.pos - sign * (hop if arriving else hop - 1)
        ref = self.mats[stream].at[self.ring.span(q, u)]
        return pltpu.make_async_remote_copy(
            ref,
            ref,
            self.send_sem.at[way, index],
            self.recv_sem.at[way, index],
            device_id=self.ring.next if way == 0 else self.ring.prev,
            device_id_type=MESH,
        )

    def wait(self, index):
        if index not in self.got:
            self.got.add(index)
            for way in (0, 1):
                self.copy(index, way, True).wait_recv()

    def upto(self, stream, j):
        if stream >= len(self.mats):
            return
        stop = stream * self.ring.sends + -(-j * self.ring.sends // 7)
        while self.sent < stop:
            index = self.sent
            if index % self.ring.sends >= 2:
                self.wait(index - 2)
            for way in (0, 1):
                self.copy(index, way, False).start()
            self.sent += 1

    def complete(self, stream):
        self.upto(stream, 7)
        self.upto(stream + 1, 2)
        for index in range(stream * self.ring.sends, (stream + 1) * self.ring.sends):
            self.wait(index)

    def drain(self):
        for index in range(self.total):
            for way in (0, 1):
                self.copy(index, way, False).wait_send()


class Tokens:
    def __init__(self, ring, full, send_sem, recv_sem, base):
        self.ring, self.full = ring, full
        self.rows = full.shape[0] // 4
        self.send_sem, self.recv_sem, self.base = send_sem, recv_sem, base

    def copy(self, kind, arriving):
        y, c = self.ring.y, self.ring.c
        other_y, other_c = 1 - y, 1 - c
        if kind == 0:
            owner = (other_y if arriving else y) * 2 + c
        elif kind == 1:
            owner = y * 2 + (other_c if arriving else c)
        else:
            owner = other_y * 2 + (other_c if arriving else c)
        ref = self.full.at[pl.ds(pl.multiple_of(owner * self.rows, 16), self.rows)]
        return pltpu.make_async_remote_copy(
            ref,
            ref,
            self.send_sem.at[self.base + kind],
            self.recv_sem.at[self.base + kind],
            device_id=self.ring.over if kind == 0 else self.ring.core,
            device_id_type=MESH,
        )

    def start(self):
        self.copy(0, False).start()
        self.copy(1, False).start()

    def forward(self):
        self.copy(0, True).wait_recv()
        self.copy(2, False).start()
        self.copy(1, True).wait_recv()

    def finish(self):
        self.copy(2, True).wait_recv()

    def drain(self):
        for kind in range(3):
            self.copy(kind, False).wait_send()


class Sums:
    def __init__(self, ring, out, got, send_sem, recv_sem, use, over_slot=1):
        self.ring, self.out, self.got = ring, out, got
        self.send_sem, self.recv_sem, self.base = send_sem, recv_sem, use * 3
        self.slots = (0, over_slot, 2)

    def owner(self, kind):
        y, c = self.ring.y, self.ring.c
        return ((1 - y) * 2 + 1 - c, (1 - y) * 2 + c, y * 2 + 1 - c, y * 2 + c)[kind]

    def copy(self, kind):
        return pltpu.make_async_remote_copy(
            self.out.at[kind],
            self.got.at[self.slots[kind]],
            self.send_sem.at[self.base + kind],
            self.recv_sem.at[self.base + kind],
            device_id=self.ring.over if kind == 1 else self.ring.core,
            device_id_type=MESH,
        )

    def far(self, block):
        self.out[0] = block(self.owner(0)).astype(BF)
        self.copy(0).start()
        part = block(self.owner(1))
        self.copy(0).wait_recv()
        self.out[1] = (part + self.got[0].astype(F32)).astype(BF)
        self.copy(1).start()

    def near(self, block):
        self.out[2] = block(self.owner(2)).astype(BF)
        self.copy(2).start()
        return block(self.owner(3))

    def arrive(self):
        self.copy(2).wait_recv()
        self.copy(1).wait_recv()

    def total(self, part, here):
        return part + self.got[2, here].astype(F32) + self.got[self.slots[1], here].astype(F32)

    def drain(self):
        for kind in range(3):
            self.copy(kind).wait_send()


def forward_kernel(
    n,
    block_ref,
    gains_ref,
    conv_ref,
    in_ref,
    out_ref,
    gateup_ref,
    down_ref,
    cot_ref,
    wc_hbm,
    wgu_hbm,
    wd_hbm,
    one_hbm,
    two_hbm,
    fcot_hbm,
    proj_hbm,
    gate_hbm,
    up_hbm,
    hidden_hbm,
    dgrad_hbm,
    middle_ref,
    wc,
    wgu,
    low_d,
    stage_c,
    stage_m,
    cot,
    full_one,
    full_two,
    full_cot,
    proj,
    mixer,
    gate_t,
    up_t,
    hidden,
    grad_t,
    sum_out,
    sum_got,
    send_sem,
    recv_sem,
    tok_send,
    tok_recv,
    sum_send,
    sum_recv,
    in_sem,
    save_sem,
    tile_sem,
):
    rows = wc.shape[0] // n
    ring = Ring(n, rows)
    tokens = block_ref.shape[0]
    chan = out_ref.shape[1]
    seq = full_one.shape[0]
    taps = conv_ref.shape[0]
    own = pl.ds(pl.multiple_of(ring.d * rows, 16), rows)
    mine = pl.ds(pl.multiple_of(ring.t * tokens, 16), tokens)

    loads = [pltpu.make_async_copy(in_ref.at[k], stage_c.at[k], in_sem.at[k]) for k in range(3)]
    loads.append(pltpu.make_async_copy(out_ref, stage_c.at[3], in_sem.at[3]))
    loads.append(pltpu.make_async_copy(gateup_ref.at[0], stage_m.at[0], in_sem.at[4]))
    loads.append(pltpu.make_async_copy(gateup_ref.at[1], stage_m.at[1], in_sem.at[5]))
    loads.append(pltpu.make_async_copy(down_ref, stage_m.at[0], in_sem.at[6]))
    loads.append(pltpu.make_async_copy(cot_ref, cot, in_sem.at[7]))
    for k in (0, 1, 2, 3, 4, 5, 7):
        loads[k].start()
    saves = []

    def save(source, target):
        copy = pltpu.make_async_copy(source, target, save_sem.at[len(saves)])
        copy.start()
        saves.append(copy)

    ring.barrier()
    gather = Gather(ring, (wc, wgu, wd_hbm), send_sem, recv_sem)
    main, tail = split(hidden.shape[1])
    for k in range(4):
        loads[k].wait()
        wc[own, k * chan : (k + 1) * chan] = stage_c[k].astype(BF)
    gather.upto(0, 2)

    values = block_ref[...]
    scale = lax.rsqrt(jnp.mean(values * values, axis=1, keepdims=True) + eps_norm)
    full_one[mine] = (values * scale * gains_ref[0:1]).astype(BF)
    ones = Tokens(ring, full_one, tok_send, tok_recv, 0)
    ones.start()
    loads[4].wait()
    loads[5].wait()
    for k in (0, 1):
        wgu[own, k * main : (k + 1) * main] = stage_m[k, :, :main].astype(BF)
    if tail:
        ends = jnp.concatenate([stage_m[0, :, main:], stage_m[1, :, main:]], axis=1)
        wgu[own, 2 * main :] = ends.astype(BF)
    loads[6].start()
    loads[6].wait()
    low_d[...] = stage_m[0].astype(BF)
    place = pltpu.make_async_copy(low_d, wd_hbm.at[own], in_sem.at[8])
    place.start()
    loads[7].wait()
    full_cot[mine] = cot[...].astype(BF)
    gather.upto(0, 5)
    ones.forward()
    cots = Tokens(ring, full_cot, tok_send, tok_recv, 3)
    cots.start()
    gather.upto(0, 7)
    ones.finish()
    gather.complete(0)
    save(wc, wc_hbm)
    save(full_one, one_hbm)

    tile = tokens
    proj[0:8] = jnp.zeros((8, 3 * chan), F32)

    def project(i, carry):
        proj[pl.ds(pl.multiple_of(i * tile + 8, 8), tile)] = dot(
            full_one[pl.ds(pl.multiple_of(i * tile, 16), tile)], wc[:, : 3 * chan]
        )
        return carry

    lax.fori_loop(0, seq // tile, project, 0)

    def convolve(i, carry):
        here = pl.ds(pl.multiple_of(i * tile, 8), tile + 8)
        mixed = proj[here, :chan] * proj[here, 2 * chan :]
        total = conv_ref[taps - 1 : taps] * mixed[8:]
        for back in range(1, taps):
            total += conv_ref[taps - 1 - back : taps - back] * pltpu.roll(mixed, back, 0)[8:]
        c_part = proj[pl.ds(pl.multiple_of(i * tile + 8, 8), tile), chan : 2 * chan]
        mixer[pl.ds(pl.multiple_of(i * tile, 16), tile)] = (c_part * total).astype(BF)
        return carry

    lax.fori_loop(0, seq // tile, convolve, 0)
    save(proj, proj_hbm)

    def out_block(owner):
        here = pl.ds(pl.multiple_of(owner * tokens, 16), tokens)
        return dot(mixer[here], wc[:, 3 * chan :], NT)

    mids = Sums(ring, sum_out, sum_got, sum_send, sum_recv, 0)
    mids.far(out_block)
    part = mids.near(out_block)
    middle_ref[...] = part
    gather.upto(1, 3)
    cots.forward()
    cots.finish()
    gather.upto(1, 4)
    save(full_cot, fcot_hbm)
    mids.arrive()
    middle = block_ref[...] + mids.total(middle_ref[...], slice(None))
    middle_ref[...] = middle
    scale = lax.rsqrt(jnp.mean(middle * middle, axis=1, keepdims=True) + eps_norm)
    full_two[mine] = (middle * scale * gains_ref[1:2]).astype(BF)
    twos = Tokens(ring, full_two, tok_send, tok_recv, 6)
    twos.start()
    gather.upto(1, 5)
    twos.forward()
    gather.upto(1, 6)
    twos.finish()
    save(full_two, two_hbm)
    place.wait()
    gather.complete(1)
    save(wgu, wgu_hbm)

    step = tokens // 2
    count = seq // step

    def out_copy(slot, kind, i):
        source, target = ((gate_t, gate_hbm), (up_t, up_hbm))[kind]
        here = pl.ds(pl.multiple_of(i * step, 8), step)
        return pltpu.make_async_copy(source.at[slot], target.at[here], tile_sem.at[kind, slot])

    def gated(i, carry):
        slot = lax.rem(i, 2)
        here = pl.ds(pl.multiple_of(i * step, 16), step)

        @pl.when(i >= 2)
        def _():
            out_copy(slot, 0, i).wait()
            out_copy(slot, 1, i).wait()

        x = full_two[here]
        both = dot(x, wgu[...])
        gate_t[slot, :, :main] = both[:, :main]
        up_t[slot, :, :main] = both[:, main : 2 * main]
        if tail:
            ends = both[:, 2 * main :]
            gate_t[slot, :, main:] = ends[:, :tail]
            up_t[slot, :, main:] = ends[:, tail:]
        gate = gate_t[slot]
        up = up_t[slot]
        out_copy(slot, 0, i).start()
        out_copy(slot, 1, i).start()
        hidden[here] = (gate * jax.nn.sigmoid(gate) * up).astype(BF)
        return carry

    lax.fori_loop(0, count // 2, gated, 0)
    gather.upto(2, 4)
    lax.fori_loop(count // 2, count, gated, 0)
    for slot in (0, 1):
        for kind in (0, 1):
            out_copy(slot, kind, slot).wait()
    save(hidden, hidden_hbm)
    gather.upto(2, 6)

    width = tokens
    deep = wc.shape[0] // width

    def grad_copy(slot, i):
        here = pl.ds(pl.multiple_of(i * width, 16), width)
        return pltpu.make_async_copy(grad_t.at[slot], dgrad_hbm.at[here], tile_sem.at[2, slot])

    def graded(i, carry):
        slot = lax.rem(i, 2)

        @pl.when(i >= 2)
        def _():
            grad_copy(slot, i).wait()

        x = full_cot[:, pl.ds(pl.multiple_of(i * width, 128), width)]
        grad_t[slot] = dot(x, hidden[...], TN).astype(BF)
        grad_copy(slot, i).start()
        return carry

    lax.fori_loop(0, deep // 2, graded, 0)
    gather.upto(2, 7)
    lax.fori_loop(deep // 2, deep, graded, 0)
    for slot in (0, 1):
        grad_copy(slot, slot).wait()
    gather.complete(2)
    for copy in saves:
        copy.wait()
    for group in (ones, cots, twos, mids):
        group.drain()
    gather.drain()


def forward(n, block_in, cotangent, in_weight, conv_weight, out_weight, gateup_weight, down_weight, norm_gains):
    tokens, model = block_in.shape
    seq = tokens * 4
    chan = out_weight.shape[1]
    units = down_weight.shape[1]
    rows = out_weight.shape[0]
    sends = 3 * (n - 1)
    any_spec = pl.BlockSpec(memory_space=pl.ANY)
    vmem = pl.BlockSpec(memory_space=pltpu.VMEM)
    shape = jax.ShapeDtypeStruct
    dma = pltpu.SemaphoreType.DMA
    return pl.pallas_call(
        functools.partial(forward_kernel, n),
        out_shape=[
            shape((model, 4 * chan), BF),
            shape((model, 2 * units), BF),
            shape((model, units), BF),
            shape((seq, model), BF),
            shape((seq, model), BF),
            shape((seq, model), BF),
            shape((seq + 8, 3 * chan), F32),
            shape((seq, units), F32),
            shape((seq, units), F32),
            shape((seq, units), BF),
            shape((model, units), BF),
            shape((tokens, model), F32),
        ],
        in_specs=[vmem, vmem, vmem] + [any_spec] * 5,
        out_specs=[any_spec] * 11 + [vmem],
        scratch_shapes=[
            pltpu.VMEM((model, 4 * chan), BF),
            pltpu.VMEM((model, 2 * units), BF),
            pltpu.VMEM((rows, units), BF),
            pltpu.VMEM((4, rows, chan), F32),
            pltpu.VMEM((2, rows, units), F32),
            pltpu.VMEM((tokens, model), F32),
            pltpu.VMEM((seq, model), BF),
            pltpu.VMEM((seq, model), BF),
            pltpu.VMEM((seq, model), BF),
            pltpu.VMEM((seq + 8, 3 * chan), F32),
            pltpu.VMEM((seq, chan), BF),
            pltpu.VMEM((2, tokens // 2, units), F32),
            pltpu.VMEM((2, tokens // 2, units), F32),
            pltpu.VMEM((seq, units), BF),
            pltpu.VMEM((2, tokens, units), BF),
            pltpu.VMEM((3, tokens, model), BF),
            pltpu.VMEM((3, tokens, model), BF),
            dma((2, sends)),
            dma((2, sends)),
            dma((9,)),
            dma((9,)),
            dma((3,)),
            dma((3,)),
            dma((9,)),
            dma((10,)),
            dma((3, 2)),
        ],
        compiler_params=pltpu.CompilerParams(
            collective_id=0, has_side_effects=True, vmem_limit_bytes=VMEM_LIMIT
        ),
        cost_estimate=pl.CostEstimate(flops=10 * seq * model * units, bytes_accessed=10**8, transcendentals=0),
    )(block_in, norm_gains, conv_weight, in_weight, out_weight, gateup_weight, down_weight, cotangent)


class Scatter:
    def __init__(self, ring, first, mats, outs, slots, stage, send_sem, recv_sem, credit_sem, out_sem):
        self.ring, self.first, self.mats, self.outs = ring, first, mats, outs
        self.slots, self.stage = slots, stage
        self.send_sem, self.recv_sem = send_sem, recv_sem
        self.credit_sem, self.out_sem = credit_sem, out_sem
        self.depth = slots.shape[1]
        self.total = ring.sends * len(mats)
        self.sent, self.used, self.left = 0, 0, set()

    def place(self, index, way):
        stream, j = divmod(index, self.ring.sends)
        away = self.ring.n // 2 - (j + 1) // 2
        return stream, away, j % 2 if way == 0 else 1 - j % 2

    def mat_span(self, index, way, shift):
        stream, away, u = self.place(index, way)
        sign = 1 if way == 0 else -1
        return self.ring.span(self.ring.pos + sign * (away - shift), u)

    def slot(self, index, way):
        stream, _, u = self.place(index, way)
        cols = self.mats[stream].shape[1]
        return self.slots.at[way, index % self.depth, : self.ring.units[u][1], :cols]

    def copy(self, index, way):
        stream = self.place(index, way)[0]
        mat = self.first if index < 2 else self.mats[stream]
        return pltpu.make_async_remote_copy(
            mat.at[self.mat_span(index, way, 0)],
            self.slot(index, way),
            self.send_sem.at[way, index],
            self.recv_sem.at[way, index],
            device_id=self.ring.next if way == 0 else self.ring.prev,
            device_id_type=MESH,
        )

    def out_copy(self, stream, u):
        start, size = self.ring.units[u]
        cols = self.mats[stream].shape[1]
        slot = stream % 2 * 2 + u
        return pltpu.make_async_copy(
            self.stage.at[slot, :size, :cols],
            self.outs[stream].at[pl.ds(start, size)],
            self.out_sem.at[slot],
        )

    def consume(self, index):
        stream, j = divmod(index, self.ring.sends)
        last = self.ring.sends - 1
        for way in (0, 1):
            u = self.place(index, way)[2]
            size = self.ring.units[u][1]
            self.copy(index, way).wait_recv()
            mat = self.mats[stream]
            cols = mat.shape[1]
            here = self.mat_span(index, way, 1)
            got = self.slots[way, index % self.depth, :size, :cols].astype(F32)
            if j < last - 1:
                mat[here] = (mat[here].astype(F32) + got).astype(BF)
            else:
                slot = stream % 2 * 2 + u
                if j == last - 1:
                    if stream >= 2:
                        self.out_copy(stream - 2, u).wait()
                    self.stage[slot, :size, :cols] = mat[here].astype(F32) + got
                else:
                    self.stage[slot, :size, :cols] = self.stage[slot, :size, :cols] + got
                    self.out_copy(stream, u).start()
            if index + self.depth < self.total:
                pl.semaphore_signal(
                    self.credit_sem.at[way],
                    inc=1,
                    device_id=self.ring.prev if way == 0 else self.ring.next,
                    device_id_type=MESH,
                )

    def use(self, stop):
        while self.used < stop:
            self.consume(self.used)
            self.used += 1

    def upto(self, stream, j):
        stop = min(self.total, stream * self.ring.sends + -(-j * self.ring.sends // 7))
        while self.sent < stop:
            index = self.sent
            if index % self.ring.sends >= 2:
                self.use(index - 1)
            for way in (0, 1):
                if index >= self.depth:
                    pl.semaphore_wait(self.credit_sem.at[way], 1)
                self.copy(index, way).start()
            self.sent += 1

    def leave(self, stream):
        for index in range(stream * self.ring.sends, (stream + 1) * self.ring.sends):
            if index not in self.left:
                self.left.add(index)
                for way in (0, 1):
                    self.copy(index, way).wait_send()

    def drain(self):
        self.use(self.total)
        streams = len(self.mats)
        for stream in range(streams):
            self.leave(stream)
        for stream in range(max(0, streams - 2), streams):
            for u in (0, 1):
                self.out_copy(stream, u).wait()


def backward_kernel(
    n,
    gains_ref,
    conv_ref,
    wc_hbm,
    wgu_hbm,
    wd_hbm,
    one_hbm,
    two_hbm,
    fcot_hbm,
    proj_hbm,
    gate_hbm,
    up_hbm,
    hidden_hbm,
    dgrad_hbm,
    middle_hbm,
    block_hbm,
    cot_hbm,
    down_out,
    gate_out,
    up_out,
    conv_out,
    block_out,
    input_out,
    small_out,
    wd,
    wg,
    wu,
    gd,
    slots,
    full_cot,
    full_two,
    d_gate,
    d_up,
    stage,
    sum_out,
    sum_got,
    tok_a,
    tok_b,
    tok_c,
    proj_t,
    d_conv,
    taps_sum,
    small_send,
    small_got,
    send_sem,
    recv_sem,
    credit_sem,
    out_sem,
    tok_send,
    tok_recv,
    sum_send,
    sum_recv,
    ladder_send,
    ladder_recv,
    load_sem,
    tile_sem,
    proj_sem,
):
    model = wd.shape[0]
    rows = model // n
    ring = Ring(n, rows)
    tokens = tok_a.shape[0]
    seq = full_cot.shape[0]
    chan = conv_ref.shape[1]
    taps = conv_ref.shape[0]
    wc = wd.at[:, : 4 * chan]
    gc = gd.at[:, : 4 * chan]

    def load(k, source, target):
        copy = pltpu.make_async_copy(source, target, load_sem.at[k])
        copy.start()
        return copy

    load_g = load(0, dgrad_hbm, gd)
    load_c = load(1, fcot_hbm, full_cot)
    load_d = load(2, wd_hbm, wd)
    main, tail = split(wg.shape[1])
    load_gate = load(4, wgu_hbm.at[:, :main], wg.at[:, :main])
    load_up = load(5, wgu_hbm.at[:, main : 2 * main], wu.at[:, :main])
    half = model // 2
    if tail:
        load_ends = [
            load(k, wgu_hbm.at[pl.ds(q * half, half), 2 * main :], full_two.at[:half, q * 128 : (q + 1) * 128])
            for q, k in ((0, 3), (1, 14))
        ]
    load_mid = load(6, middle_hbm, tok_a)
    load_cot = load(7, cot_hbm, tok_b)

    step = tokens // 2
    count = seq // step

    def tile_copy(slot, kind, i):
        source = (gate_hbm, up_hbm)[kind]
        here = pl.ds(pl.multiple_of(i * step, 8), step)
        return pltpu.make_async_copy(source.at[here], stage.at[slot * 2 + kind], tile_sem.at[slot, kind])

    for kind in (0, 1):
        tile_copy(0, kind, 0).start()

    steps = [ring.core, ring.over]
    span = 1
    while span < n:
        steps.append((ring.d + span * (1 - 2 * lax.rem(lax.div(ring.d, span), 2)), ring.t))
        span *= 2
    sem = pltpu.get_barrier_semaphore()
    for device in [ring.next, ring.prev] + steps:
        pl.semaphore_signal(sem, inc=1, device_id=device, device_id_type=MESH)
    pl.semaphore_wait(sem, 2 + len(steps))

    scatter = Scatter(
        ring,
        dgrad_hbm,
        (gd, wg, wu, gc),
        (down_out, gate_out, up_out, conv_out),
        slots,
        stage,
        send_sem,
        recv_sem,
        credit_sem,
        out_sem,
    )
    scatter.upto(0, 2)
    load_g.wait()
    load_c.wait()
    load_d.wait()

    def hidden_back(i, carry):
        slot = lax.rem(i, 2)
        here = pl.ds(pl.multiple_of(i * step, 16), step)

        @pl.when(i + 1 < count)
        def _():
            for kind in (0, 1):
                tile_copy(1 - slot, kind, i + 1).start()

        d_hidden = dot(full_cot[here], wd[...])
        for kind in (0, 1):
            tile_copy(slot, kind, i).wait()
        gate = stage[slot * 2]
        sig = jax.nn.sigmoid(gate)
        d_up[here] = (d_hidden * (gate * sig)).astype(BF)
        d_gate[here] = (d_hidden * stage[slot * 2 + 1] * sig * (1.0 + gate * (1.0 - sig))).astype(BF)
        return carry

    lax.fori_loop(0, count // 2, hidden_back, 0)
    scatter.upto(0, 3)
    lax.fori_loop(count // 2, count, hidden_back, 0)
    load_gate.wait()
    load_up.wait()
    if tail:
        for q in (0, 1):
            load_ends[q].wait()
            here = pl.ds(q * half, half)
            ends = full_two[:half, q * 128 : (q + 1) * 128]
            wg[here, main:] = ends[:, :tail]
            wu[here, main:] = ends[:, tail:]
    load_two = load(3, two_hbm, full_two)
    scatter.upto(0, 4)

    def token_rows(owner):
        return pl.ds(pl.multiple_of(owner * tokens, 16), tokens)

    def two_block(owner):
        here = token_rows(owner)
        return dot(d_gate[here], wg[...], NT) + dot(d_up[here], wu[...], NT)

    twos = Sums(ring, sum_out, sum_got, sum_send, sum_recv, 0)
    twos.far(two_block)
    tok_c[...] = twos.near(two_block)
    scatter.upto(0, 5)
    load_two.wait()

    width = tokens
    deep = model // width

    def grad_into(target, columns, left, right):
        def body(i, carry):
            x = left[:, pl.ds(pl.multiple_of(i * width, 128), width)]
            target[pl.ds(pl.multiple_of(i * width, 16), width), columns] = dot(x, right[...], TN).astype(BF)
            return carry

        return body

    every = slice(None)
    lax.fori_loop(0, deep, grad_into(wg, every, full_two, d_gate), 0)
    load_hidden = load(8, hidden_hbm, d_gate)
    scatter.upto(0, 7)
    scatter.upto(1, 2)

    load_mid.wait()
    load_cot.wait()
    chunk = tokens // 4
    small_send[0] = jnp.zeros(small_send.shape[1:], F32)
    twos.arrive()

    def middle_back(i, carry):
        here = pl.ds(pl.multiple_of(i * chunk, 16), chunk)
        d_two = twos.total(tok_c[here], here)
        middle = tok_a[here]
        scale = lax.rsqrt(jnp.mean(middle * middle, axis=1, keepdims=True) + eps_norm)
        normal = middle * scale
        weighted = gains_ref[1:2] * d_two
        d_middle = tok_b[here] + scale * (
            weighted - normal * jnp.mean(weighted * normal, axis=1, keepdims=True)
        )
        small_send[0, 1:2] += jnp.sum(d_two * normal, axis=0, keepdims=True)
        tok_c[here] = d_middle
        full_cot[pl.ds(pl.multiple_of(ring.t * tokens + i * chunk, 16), chunk)] = d_middle.astype(BF)
        return carry

    lax.fori_loop(0, 4, middle_back, 0)
    mids = Tokens(ring, full_cot, tok_send, tok_recv, 0)
    mids.start()
    load_block = load(9, block_hbm, tok_b)

    lax.fori_loop(0, deep, grad_into(wu, every, full_two, d_up), 0)
    load_one = load(10, one_hbm, full_two)
    scatter.upto(1, 4)
    mids.forward()
    load_hidden.wait()
    twos.drain()

    def down_block(owner):
        return dot(d_gate[token_rows(owner)], wd[...], NT)

    downs = Sums(ring, sum_out, sum_got, sum_send, sum_recv, 1)
    downs.far(down_block)
    scatter.upto(1, 5)
    tok_a[...] = tok_a[...] + downs.near(down_block)
    load_conv = load(11, wc_hbm, wc)
    mids.finish()
    scatter.upto(1, 6)

    def proj_copy(slot, i):
        here = pl.ds(pl.multiple_of(i * step, 8), step + 8)
        return pltpu.make_async_copy(proj_hbm.at[here], proj_t.at[slot], proj_sem.at[slot])

    proj_copy((count - 1) % 2, count - 1).start()
    d_conv[pl.ds(seq, 8)] = jnp.zeros((8, chan), F32)
    taps_sum[...] = jnp.zeros(taps_sum.shape, F32)
    load_conv.wait()
    load_one.wait()

    def conv_back(k, carry):
        i = count - 1 - k
        slot = lax.rem(i, 2)

        @pl.when(i >= 1)
        def _():
            proj_copy(1 - slot, i - 1).start()

        here = pl.ds(pl.multiple_of(i * step, 16), step)
        d_mixer = dot(full_cot[here], wd[:, 3 * chan : 4 * chan])
        proj_copy(slot, i).wait()
        b_part = proj_t[slot, :, :chan]
        c_part = proj_t[slot, 8:, chan : 2 * chan]
        v_part = proj_t[slot, :, 2 * chan :]
        mixed = b_part * v_part
        shifted = [mixed[8:]] + [pltpu.roll(mixed, back, 0)[8:] for back in range(1, taps)]
        total = sum(conv_ref[taps - 1 - back : taps - back] * shifted[back] for back in range(taps))
        d_c = d_mixer * total
        d_here = d_mixer * c_part
        d_up[here, :chan] = (c_part * total).astype(BF)
        d_conv[pl.ds(pl.multiple_of(i * step, 8), step)] = d_here
        for back in range(taps):
            at = taps - 1 - back
            taps_sum[at : at + 1] += jnp.sum(d_here * shifted[back], axis=0, keepdims=True)
        longer = d_conv[pl.ds(pl.multiple_of(i * step, 8), step + 8)]
        d_mixed = conv_ref[taps - 1 : taps] * d_here
        for ahead in range(1, taps):
            moved = pltpu.roll(longer, step + 8 - ahead, 0)[:step]
            d_mixed += conv_ref[taps - 1 - ahead : taps - ahead] * moved
        d_gate[here, :chan] = (d_mixed * v_part[8:]).astype(BF)
        d_gate[here, chan : 2 * chan] = d_c.astype(BF)
        d_gate[here, 2 * chan : 3 * chan] = (d_mixed * b_part[8:]).astype(BF)
        return carry

    lax.fori_loop(0, count // 2, conv_back, 0)
    scatter.upto(1, 7)
    scatter.upto(2, 2)
    lax.fori_loop(count // 2, count, conv_back, 0)
    small_send[0, 2 : 2 + taps, :chan] = taps_sum[:taps]
    scatter.upto(2, 3)

    def one_block(owner):
        return dot(d_gate[token_rows(owner), : 3 * chan], wd[:, : 3 * chan], NT)

    downs.arrive()

    def block_done(i, carry):
        here = pl.ds(pl.multiple_of(i * chunk, 16), chunk)
        tok_a[here] = downs.total(tok_a[here], here)
        return carry

    lax.fori_loop(0, 4, block_done, 0)
    save_block = load(12, tok_a, block_out)
    downs.drain()
    save_block.wait()
    ones = Sums(ring, sum_out, sum_got, sum_send, sum_recv, 2, 3)
    ones.far(one_block)
    tok_a[...] = ones.near(one_block)
    scatter.leave(0)
    proj_one = slice(0, 3 * chan)
    mix_cols = slice(3 * chan, 4 * chan)

    def in_grad(i, carry):
        x = full_two[:, pl.ds(pl.multiple_of(i * width, 128), width)]
        gd[pl.ds(pl.multiple_of(i * width, 16), width), proj_one] = dot(x, d_gate[:, proj_one], TN).astype(BF)
        z = full_cot[:, pl.ds(pl.multiple_of(i * width, 128), width)]
        gd[pl.ds(pl.multiple_of(i * width, 16), width), mix_cols] = dot(z, d_up[:, :chan], TN).astype(BF)
        return carry

    scatter.upto(2, 4)
    lax.fori_loop(0, deep, in_grad, 0)
    scatter.upto(2, 5)
    load_block.wait()
    ones.arrive()

    def input_back(i, carry):
        here = pl.ds(pl.multiple_of(i * chunk, 16), chunk)
        d_one = ones.total(tok_a[here], here)
        values = tok_b[here]
        scale = lax.rsqrt(jnp.mean(values * values, axis=1, keepdims=True) + eps_norm)
        normal = values * scale
        weighted = gains_ref[0:1] * d_one
        tok_c[here] = tok_c[here] + scale * (
            weighted - normal * jnp.mean(weighted * normal, axis=1, keepdims=True)
        )
        small_send[0, 0:1] += jnp.sum(d_one * normal, axis=0, keepdims=True)
        return carry

    lax.fori_loop(0, 4, input_back, 0)
    save_input = load(13, tok_c, input_out)
    scatter.upto(2, 6)

    ladder = [
        pltpu.make_async_remote_copy(
            small_send.at[k],
            small_got.at[k],
            ladder_send.at[k],
            ladder_recv.at[k],
            device_id=device,
            device_id_type=MESH,
        )
        for k, device in enumerate(steps)
    ]
    for k in range(len(steps)):
        ladder[k].start()
        scatter.upto(*((2, 7), (3, 2), (3, 3), (3, 4), (3, 5))[min(k, 4)])
        ladder[k].wait_recv()
        if k < 2:
            small_send[k + 1, 0:2] = small_send[k, 0:2] + small_got[k, 0:2]
            small_send[k + 1, 2:8] = small_send[k, 2:8]
        else:
            small_send[k + 1] = small_send[k] + small_got[k]
    small_out[...] = small_send[len(steps)]
    scatter.upto(3, 7)
    scatter.drain()
    mids.drain()
    ones.drain()
    for copy in ladder:
        copy.wait_send()
    save_input.wait()


def backward(n, conv_weight, norm_gains, saved, block_in, cotangent, depth=4):
    (wc, wgu, wd, one, two, fcot, proj, gate, up, hidden, dgrad, middle) = saved
    tokens, model = block_in.shape
    seq = tokens * 4
    chan = conv_weight.shape[1]
    units = wd.shape[1]
    rows = model // n
    sends = 4 * (n - 1)
    steps = 2 + (n - 1).bit_length()
    unit = (rows // 2 + 15) // 16 * 16
    any_spec = pl.BlockSpec(memory_space=pl.ANY)
    vmem = pl.BlockSpec(memory_space=pltpu.VMEM)
    shape = jax.ShapeDtypeStruct
    dma = pltpu.SemaphoreType.DMA
    return pl.pallas_call(
        functools.partial(backward_kernel, n),
        out_shape=[
            shape((rows, units), F32),
            shape((rows, units), F32),
            shape((rows, units), F32),
            shape((rows, 4 * chan), F32),
            shape((tokens, model), F32),
            shape((tokens, model), F32),
            shape((8, model), F32),
        ],
        in_specs=[vmem, vmem] + [any_spec] * 14,
        out_specs=[any_spec] * 6 + [vmem],
        scratch_shapes=[
            pltpu.VMEM((model, units), BF),
            pltpu.VMEM((model, units), BF),
            pltpu.VMEM((model, units), BF),
            pltpu.VMEM((model, units), BF),
            pltpu.VMEM((2, depth, unit, units), BF),
            pltpu.VMEM((seq, model), BF),
            pltpu.VMEM((seq, model), BF),
            pltpu.VMEM((seq, units), BF),
            pltpu.VMEM((seq, units), BF),
            pltpu.VMEM((4, tokens // 2, units), F32),
            pltpu.VMEM((3, tokens, model), BF),
            pltpu.VMEM((4, tokens, model), BF),
            pltpu.VMEM((tokens, model), F32),
            pltpu.VMEM((tokens, model), F32),
            pltpu.VMEM((tokens, model), F32),
            pltpu.VMEM((2, tokens // 2 + 8, 3 * chan), F32),
            pltpu.VMEM((seq + 8, chan), F32),
            pltpu.VMEM((8, chan), F32),
            pltpu.VMEM((steps + 1, 8, model), F32),
            pltpu.VMEM((steps, 8, model), F32),
            dma((2, sends)),
            dma((2, sends)),
            pltpu.SemaphoreType.REGULAR((2,)),
            dma((4,)),
            dma((3,)),
            dma((3,)),
            dma((9,)),
            dma((9,)),
            dma((steps,)),
            dma((steps,)),
            dma((15,)),
            dma((2, 2)),
            dma((2,)),
        ],
        compiler_params=pltpu.CompilerParams(
            collective_id=1, has_side_effects=True, vmem_limit_bytes=VMEM_LIMIT
        ),
        cost_estimate=pl.CostEstimate(flops=16 * seq * model * units, bytes_accessed=10**8, transcendentals=0),
    )(
        norm_gains, conv_weight, wc, wgu, wd, one, two, fcot, proj, gate, up, hidden, dgrad,
        middle, block_in, cotangent,
    )


def finish_kernel(
    down_ref,
    gate_ref,
    up_ref,
    conv_ref,
    block_ref,
    input_ref,
    small_ref,
    in_w,
    in_m,
    in_v,
    out_w,
    out_m,
    out_v,
    gateup_w,
    gateup_m,
    gateup_v,
    down_w,
    down_m,
    down_v,
    taps_w,
    taps_m,
    taps_v,
    gains_w,
    gains_m,
    gains_v,
    block_out,
    input_out,
    in_grad,
    taps_grad,
    out_grad,
    gateup_grad,
    down_grad,
    gains_grad,
    in_up,
    taps_up,
    out_up,
    gateup_up,
    down_up,
    gains_up,
    in_mo,
    in_va,
    taps_mo,
    taps_va,
    out_mo,
    out_va,
    gateup_mo,
    gateup_va,
    down_mo,
    down_va,
    gains_mo,
    gains_va,
):
    chan = out_w.shape[1]
    block_out[...] = block_ref[...]
    input_out[...] = input_ref[...]
    for k in range(3):
        grad = conv_ref[:, k * chan : (k + 1) * chan]
        in_grad[k] = grad
        in_up[k], in_mo[k], in_va[k] = adamw(in_w[k], grad, in_m[k], in_v[k], rate_matrix, decay_matrix)
    grad = conv_ref[:, 3 * chan :]
    out_grad[...] = grad
    out_up[...], out_mo[...], out_va[...] = adamw(
        out_w[...], grad, out_m[...], out_v[...], rate_matrix, decay_matrix
    )
    for k, ref in enumerate((gate_ref, up_ref)):
        grad = ref[...]
        gateup_grad[k] = grad
        gateup_up[k], gateup_mo[k], gateup_va[k] = adamw(
            gateup_w[k], grad, gateup_m[k], gateup_v[k], rate_matrix, decay_matrix
        )
    grad = down_ref[...]
    down_grad[...] = grad
    down_up[...], down_mo[...], down_va[...] = adamw(
        down_w[...], grad, down_m[...], down_v[...], rate_matrix, decay_matrix
    )

    @pl.when(pl.program_id(0) == 0)
    def _():
        taps = taps_w.shape[0]
        grad = small_ref[0:2]
        gains_grad[...] = grad
        gains_up[...], gains_mo[...], gains_va[...] = adamw(
            gains_w[...], grad, gains_m[...], gains_v[...], rate_small, 0.0
        )
        grad = small_ref[2 : 2 + taps, :chan]
        taps_grad[...] = grad
        taps_up[...], taps_mo[...], taps_va[...] = adamw(
            taps_w[...], grad, taps_m[...], taps_v[...], rate_small, 0.0
        )


def finish(grads, in_set, out_set, gateup_set, down_set, taps_set, gains_set):
    rows, units = grads[0].shape
    tokens, model = grads[4].shape
    chan = out_set[0].shape[1]
    taps = taps_set[0].shape[0]
    parts = max(g for g in (1, 2, 3) if rows % (8 * g) == 0 and tokens % (8 * g) == 0)
    r, t = rows // parts, tokens // parts
    wide = lambda width: pl.BlockSpec((r, width), lambda i: (i, 0))
    deep = lambda count, width: pl.BlockSpec((count, r, width), lambda i: (0, i, 0))
    token = pl.BlockSpec((t, model), lambda i: (i, 0))
    whole = lambda *dims: pl.BlockSpec(dims, lambda i: (0, 0))
    in_spec, out_spec, gateup_spec, down_spec = deep(3, chan), wide(chan), deep(2, units), wide(units)
    taps_spec, gains_spec = whole(taps, chan), whole(2, model)
    like = lambda group: jax.ShapeDtypeStruct(group[0].shape, F32)
    shape = [jax.ShapeDtypeStruct((tokens, model), F32)] * 2
    matrices = (in_set, taps_set, out_set, gateup_set, down_set, gains_set)
    specs = (in_spec, taps_spec, out_spec, gateup_spec, down_spec, gains_spec)
    out_shape = shape + [like(m) for m in matrices] * 2
    out_specs = [token, token] + list(specs) * 2
    for m, spec in zip(matrices, specs):
        out_shape += [like(m)] * 2
        out_specs += [spec] * 2
    return pl.pallas_call(
        finish_kernel,
        grid=(parts,),
        out_shape=out_shape,
        in_specs=[wide(units)] * 3
        + [wide(4 * chan), token, token, whole(8, model)]
        + [in_spec] * 3
        + [out_spec] * 3
        + [gateup_spec] * 3
        + [down_spec] * 3
        + [taps_spec] * 3
        + [gains_spec] * 3,
        out_specs=out_specs,
        compiler_params=pltpu.CompilerParams(vmem_limit_bytes=VMEM_LIMIT),
    )(*grads, *in_set, *out_set, *gateup_set, *down_set, *taps_set, *gains_set)


def per_device(
    block_in,
    cotangent,
    in_weight,
    conv_weight,
    out_weight,
    gateup_weight,
    down_weight,
    norm_gains,
    in_first,
    in_second,
    conv_first,
    conv_second,
    out_first,
    out_second,
    gateup_first,
    gateup_second,
    down_first,
    down_second,
    gains_first,
    gains_second,
):
    n = lax.axis_size("dp")
    saved = forward(
        n,
        block_in,
        cotangent,
        in_weight,
        conv_weight,
        out_weight,
        gateup_weight,
        down_weight,
        norm_gains,
    )
    grads = backward(n, conv_weight, norm_gains, saved, block_in, cotangent)
    return tuple(
        finish(
            grads,
            (in_weight, in_first, in_second),
            (out_weight, out_first, out_second),
            (gateup_weight, gateup_first, gateup_second),
            (down_weight, down_first, down_second),
            (conv_weight, conv_first, conv_second),
            (norm_gains, gains_first, gains_second),
        )
    )


def solution(mesh):
    in_specs = (
        P(("dp", "tensor"), None),
        P(("dp", "tensor"), None),
        P(None, "dp", "tensor"),
        P(None, "tensor"),
        P("dp", "tensor"),
        P(None, "dp", "tensor"),
        P("dp", "tensor"),
        P(),
        P(None, "dp", "tensor"),
        P(None, "dp", "tensor"),
        P(None, "tensor"),
        P(None, "tensor"),
        P("dp", "tensor"),
        P("dp", "tensor"),
        P(None, "dp", "tensor"),
        P(None, "dp", "tensor"),
        P("dp", "tensor"),
        P("dp", "tensor"),
        P(),
        P(),
    )
    out_specs = (
        P(("dp", "tensor"), None),
        P(("dp", "tensor"), None),
        P(None, "dp", "tensor"),
        P(None, "tensor"),
        P("dp", "tensor"),
        P(None, "dp", "tensor"),
        P("dp", "tensor"),
        P(),
        P(None, "dp", "tensor"),
        P(None, "tensor"),
        P("dp", "tensor"),
        P(None, "dp", "tensor"),
        P("dp", "tensor"),
        P(),
        P(None, "dp", "tensor"),
        P(None, "dp", "tensor"),
        P(None, "tensor"),
        P(None, "tensor"),
        P("dp", "tensor"),
        P("dp", "tensor"),
        P(None, "dp", "tensor"),
        P(None, "dp", "tensor"),
        P("dp", "tensor"),
        P("dp", "tensor"),
        P(),
        P(),
    )
    return jax.shard_map(
        per_device, mesh=mesh, in_specs=in_specs, out_specs=out_specs, check_vma=False
    )
```

```python
import functools

import jax
import jax.numpy as jnp
from jax import lax
from jax.experimental import pallas as pl
from jax.experimental.pallas import tpu as pltpu
from jax.sharding import PartitionSpec as P

STEP = 3


eps_norm = 1e-05
beta_one = 0.9
beta_two = 0.95
adam_eps = 1e-08
decay_matrix = 0.1
rate_matrix = 0.03
rate_small = 0.5


def adamw(weight, gradient, first, second, rate, decay_rate):
    momentum = beta_one * first + (1.0 - beta_one) * gradient
    variance = beta_two * second + (1.0 - beta_two) * gradient * gradient
    corrected = momentum * (1.0 / (1.0 - beta_one**STEP))
    spread = variance * (1.0 / (1.0 - beta_two**STEP))
    updated = weight - rate * (corrected / (jnp.sqrt(spread) + adam_eps) + decay_rate * weight)
    return (updated, momentum, variance)


MESH = pl.DeviceIdType.MESH
BF = jnp.bfloat16
F32 = jnp.float32
NN = (((1,), (0,)), ((), ()))
NT = (((1,), (1,)), ((), ()))
TN = (((0,), (0,)), ((), ()))
VMEM_LIMIT = 63 * 1024 * 1024


def dot(left, right, dims=NN):
    return lax.dot_general(left, right, dims, preferred_element_type=F32)


class Ring:
    def __init__(self, n, rows):
        self.n, self.rows = n, rows
        self.sends = n - 1
        d = lax.axis_index("dp")
        t = lax.axis_index("tensor")
        self.d, self.t = d, t
        self.y, self.c = lax.div(t, 2), lax.rem(t, 2)
        self.pos = lax.div(d, 2) + lax.rem(d, 2) * (n - 1 - 2 * lax.div(d, 2))
        self.next = (self.at(self.pos + 1), t)
        self.prev = (self.at(self.pos - 1), t)
        self.core = (d, self.y * 2 + (1 - self.c))
        self.over = (d, (1 - self.y) * 2 + self.c)
        first = (rows // 2 + 15) // 16 * 16
        self.units = ((0, first), (first, rows - first))

    def at(self, q):
        n = self.n
        q = lax.rem(q + 2 * n, n)
        back = lax.div(q, n // 2)
        return (1 - back) * 2 * q + back * (2 * (n - 1 - q) + 1)

    def span(self, q, u):
        start, size = self.units[u]
        return pl.ds(pl.multiple_of(self.at(q) * self.rows + start, 16), size)

    def barrier(self):
        sem = pltpu.get_barrier_semaphore()
        for device in (self.next, self.prev, self.core, self.over):
            pl.semaphore_signal(sem, inc=1, device_id=device, device_id_type=MESH)
        pl.semaphore_wait(sem, 4)


def split(units):
    main = units // 128 * 128
    return main, units - main


class Gather:
    def __init__(self, ring, mats, send_sem, recv_sem):
        self.ring, self.mats = ring, mats
        self.send_sem, self.recv_sem = send_sem, recv_sem
        self.sent, self.got = 0, set()
        self.total = ring.sends * len(mats)

    def copy(self, index, way, arriving):
        stream, j = divmod(index, self.ring.sends)
        hop, sub = j // 2 + 1, j % 2
        u = sub if way == 0 else 1 - sub
        sign = 1 if way == 0 else -1
        q = self.ring.pos - sign * (hop if arriving else hop - 1)
        ref = self.mats[stream].at[self.ring.span(q, u)]
        return pltpu.make_async_remote_copy(
            ref,
            ref,
            self.send_sem.at[way, index],
            self.recv_sem.at[way, index],
            device_id=self.ring.next if way == 0 else self.ring.prev,
            device_id_type=MESH,
        )

    def wait(self, index):
        if index not in self.got:
            self.got.add(index)
            for way in (0, 1):
                self.copy(index, way, True).wait_recv()

    def upto(self, stream, j):
        if stream >= len(self.mats):
            return
        stop = stream * self.ring.sends + -(-j * self.ring.sends // 7)
        while self.sent < stop:
            index = self.sent
            if index % self.ring.sends >= 2:
                self.wait(index - 2)
            for way in (0, 1):
                self.copy(index, way, False).start()
            self.sent += 1

    def complete(self, stream):
        self.upto(stream, 7)
        self.upto(stream + 1, 2)
        for index in range(stream * self.ring.sends, (stream + 1) * self.ring.sends):
            self.wait(index)

    def drain(self):
        for index in range(self.total):
            for way in (0, 1):
                self.copy(index, way, False).wait_send()


class Tokens:
    def __init__(self, ring, full, send_sem, recv_sem, base):
        self.ring, self.full = ring, full
        self.rows = full.shape[0] // 4
        self.send_sem, self.recv_sem, self.base = send_sem, recv_sem, base

    def copy(self, kind, arriving):
        y, c = self.ring.y, self.ring.c
        other_y, other_c = 1 - y, 1 - c
        if kind == 0:
            owner = (other_y if arriving else y) * 2 + c
        elif kind == 1:
            owner = y * 2 + (other_c if arriving else c)
        else:
            owner = other_y * 2 + (other_c if arriving else c)
        ref = self.full.at[pl.ds(pl.multiple_of(owner * self.rows, 16), self.rows)]
        return pltpu.make_async_remote_copy(
            ref,
            ref,
            self.send_sem.at[self.base + kind],
            self.recv_sem.at[self.base + kind],
            device_id=self.ring.over if kind == 0 else self.ring.core,
            device_id_type=MESH,
        )

    def start(self):
        self.copy(0, False).start()
        self.copy(1, False).start()

    def forward(self):
        self.copy(0, True).wait_recv()
        self.copy(2, False).start()
        self.copy(1, True).wait_recv()

    def finish(self):
        self.copy(2, True).wait_recv()

    def drain(self):
        for kind in range(3):
            self.copy(kind, False).wait_send()


class Sums:
    def __init__(self, ring, out, got, send_sem, recv_sem, use, over_slot=1):
        self.ring, self.out, self.got = ring, out, got
        self.send_sem, self.recv_sem, self.base = send_sem, recv_sem, use * 3
        self.slots = (0, over_slot, 2)

    def owner(self, kind):
        y, c = self.ring.y, self.ring.c
        return ((1 - y) * 2 + 1 - c, (1 - y) * 2 + c, y * 2 + 1 - c, y * 2 + c)[kind]

    def copy(self, kind):
        return pltpu.make_async_remote_copy(
            self.out.at[kind],
            self.got.at[self.slots[kind]],
            self.send_sem.at[self.base + kind],
            self.recv_sem.at[self.base + kind],
            device_id=self.ring.over if kind == 1 else self.ring.core,
            device_id_type=MESH,
        )

    def far(self, block):
        self.out[0] = block(self.owner(0)).astype(BF)
        self.copy(0).start()
        part = block(self.owner(1))
        self.copy(0).wait_recv()
        self.out[1] = (part + self.got[0].astype(F32)).astype(BF)
        self.copy(1).start()

    def near(self, block):
        self.out[2] = block(self.owner(2)).astype(BF)
        self.copy(2).start()
        return block(self.owner(3))

    def arrive(self):
        self.copy(2).wait_recv()
        self.copy(1).wait_recv()

    def total(self, part, here):
        return part + self.got[2, here].astype(F32) + self.got[self.slots[1], here].astype(F32)

    def drain(self):
        for kind in range(3):
            self.copy(kind).wait_send()


def forward_kernel(
    n,
    block_ref,
    gains_ref,
    conv_ref,
    in_ref,
    out_ref,
    gateup_ref,
    down_ref,
    cot_ref,
    wc_hbm,
    wgu_hbm,
    wd_hbm,
    one_hbm,
    two_hbm,
    fcot_hbm,
    proj_hbm,
    gate_hbm,
    up_hbm,
    hidden_hbm,
    dgrad_hbm,
    middle_ref,
    wc,
    wgu,
    low_d,
    stage_c,
    stage_m,
    cot,
    full_one,
    full_two,
    full_cot,
    proj,
    mixer,
    gate_t,
    up_t,
    hidden,
    grad_t,
    sum_out,
    sum_got,
    send_sem,
    recv_sem,
    tok_send,
    tok_recv,
    sum_send,
    sum_recv,
    in_sem,
    save_sem,
    tile_sem,
):
    rows = wc.shape[0] // n
    ring = Ring(n, rows)
    tokens = block_ref.shape[0]
    chan = out_ref.shape[1]
    seq = full_one.shape[0]
    taps = conv_ref.shape[0]
    own = pl.ds(pl.multiple_of(ring.d * rows, 16), rows)
    mine = pl.ds(pl.multiple_of(ring.t * tokens, 16), tokens)

    loads = [pltpu.make_async_copy(in_ref.at[k], stage_c.at[k], in_sem.at[k]) for k in range(3)]
    loads.append(pltpu.make_async_copy(out_ref, stage_c.at[3], in_sem.at[3]))
    loads.append(pltpu.make_async_copy(gateup_ref.at[0], stage_m.at[0], in_sem.at[4]))
    loads.append(pltpu.make_async_copy(gateup_ref.at[1], stage_m.at[1], in_sem.at[5]))
    loads.append(pltpu.make_async_copy(down_ref, stage_m.at[0], in_sem.at[6]))
    loads.append(pltpu.make_async_copy(cot_ref, cot, in_sem.at[7]))
    for k in (0, 1, 2, 3, 4, 5, 7):
        loads[k].start()
    saves = []

    def save(source, target):
        copy = pltpu.make_async_copy(source, target, save_sem.at[len(saves)])
        copy.start()
        saves.append(copy)

    ring.barrier()
    gather = Gather(ring, (wc, wgu, wd_hbm), send_sem, recv_sem)
    main, tail = split(hidden.shape[1])
    for k in range(4):
        loads[k].wait()
        wc[own, k * chan : (k + 1) * chan] = stage_c[k].astype(BF)
    gather.upto(0, 2)

    values = block_ref[...]
    scale = lax.rsqrt(jnp.mean(values * values, axis=1, keepdims=True) + eps_norm)
    full_one[mine] = (values * scale * gains_ref[0:1]).astype(BF)
    ones = Tokens(ring, full_one, tok_send, tok_recv, 0)
    ones.start()
    loads[4].wait()
    loads[5].wait()
    for k in (0, 1):
        wgu[own, k * main : (k + 1) * main] = stage_m[k, :, :main].astype(BF)
    if tail:
        ends = jnp.concatenate([stage_m[0, :, main:], stage_m[1, :, main:]], axis=1)
        wgu[own, 2 * main :] = ends.astype(BF)
    loads[6].start()
    loads[6].wait()
    low_d[...] = stage_m[0].astype(BF)
    place = pltpu.make_async_copy(low_d, wd_hbm.at[own], in_sem.at[8])
    place.start()
    loads[7].wait()
    full_cot[mine] = cot[...].astype(BF)
    gather.upto(0, 5)
    ones.forward()
    cots = Tokens(ring, full_cot, tok_send, tok_recv, 3)
    cots.start()
    gather.upto(0, 7)
    ones.finish()
    gather.complete(0)
    save(wc, wc_hbm)
    save(full_one, one_hbm)

    tile = tokens
    proj[0:8] = jnp.zeros((8, 3 * chan), F32)

    def project(i, carry):
        proj[pl.ds(pl.multiple_of(i * tile + 8, 8), tile)] = dot(
            full_one[pl.ds(pl.multiple_of(i * tile, 16), tile)], wc[:, : 3 * chan]
        )
        return carry

    lax.fori_loop(0, seq // tile, project, 0)

    def convolve(i, carry):
        here = pl.ds(pl.multiple_of(i * tile, 8), tile + 8)
        mixed = proj[here, :chan] * proj[here, 2 * chan :]
        total = conv_ref[taps - 1 : taps] * mixed[8:]
        for back in range(1, taps):
            total += conv_ref[taps - 1 - back : taps - back] * pltpu.roll(mixed, back, 0)[8:]
        c_part = proj[pl.ds(pl.multiple_of(i * tile + 8, 8), tile), chan : 2 * chan]
        mixer[pl.ds(pl.multiple_of(i * tile, 16), tile)] = (c_part * total).astype(BF)
        return carry

    lax.fori_loop(0, seq // tile, convolve, 0)
    save(proj, proj_hbm)

    def out_block(owner):
        here = pl.ds(pl.multiple_of(owner * tokens, 16), tokens)
        return dot(mixer[here], wc[:, 3 * chan :], NT)

    mids = Sums(ring, sum_out, sum_got, sum_send, sum_recv, 0)
    mids.far(out_block)
    part = mids.near(out_block)
    middle_ref[...] = part
    gather.upto(1, 3)
    cots.forward()
    cots.finish()
    gather.upto(1, 4)
    save(full_cot, fcot_hbm)
    mids.arrive()
    middle = block_ref[...] + mids.total(middle_ref[...], slice(None))
    middle_ref[...] = middle
    scale = lax.rsqrt(jnp.mean(middle * middle, axis=1, keepdims=True) + eps_norm)
    full_two[mine] = (middle * scale * gains_ref[1:2]).astype(BF)
    twos = Tokens(ring, full_two, tok_send, tok_recv, 6)
    twos.start()
    gather.upto(1, 5)
    twos.forward()
    gather.upto(1, 6)
    twos.finish()
    save(full_two, two_hbm)
    place.wait()
    gather.complete(1)
    save(wgu, wgu_hbm)

    step = tokens // 2
    count = seq // step

    def out_copy(slot, kind, i):
        source, target = ((gate_t, gate_hbm), (up_t, up_hbm))[kind]
        here = pl.ds(pl.multiple_of(i * step, 8), step)
        return pltpu.make_async_copy(source.at[slot], target.at[here], tile_sem.at[kind, slot])

    def gated(i, carry):
        slot = lax.rem(i, 2)
        here = pl.ds(pl.multiple_of(i * step, 16), step)

        @pl.when(i >= 2)
        def _():
            out_copy(slot, 0, i).wait()
            out_copy(slot, 1, i).wait()

        x = full_two[here]
        both = dot(x, wgu[...])
        gate_t[slot, :, :main] = both[:, :main]
        up_t[slot, :, :main] = both[:, main : 2 * main]
        if tail:
            ends = both[:, 2 * main :]
            gate_t[slot, :, main:] = ends[:, :tail]
            up_t[slot, :, main:] = ends[:, tail:]
        gate = gate_t[slot]
        up = up_t[slot]
        out_copy(slot, 0, i).start()
        out_copy(slot, 1, i).start()
        hidden[here] = (gate * jax.nn.sigmoid(gate) * up).astype(BF)
        return carry

    lax.fori_loop(0, count // 2, gated, 0)
    gather.upto(2, 4)
    lax.fori_loop(count // 2, count, gated, 0)
    for slot in (0, 1):
        for kind in (0, 1):
            out_copy(slot, kind, slot).wait()
    save(hidden, hidden_hbm)
    gather.upto(2, 6)

    width = tokens
    deep = wc.shape[0] // width

    def grad_copy(slot, i):
        here = pl.ds(pl.multiple_of(i * width, 16), width)
        return pltpu.make_async_copy(grad_t.at[slot], dgrad_hbm.at[here], tile_sem.at[2, slot])

    def graded(i, carry):
        slot = lax.rem(i, 2)

        @pl.when(i >= 2)
        def _():
            grad_copy(slot, i).wait()

        x = full_cot[:, pl.ds(pl.multiple_of(i * width, 128), width)]
        grad_t[slot] = dot(x, hidden[...], TN).astype(BF)
        grad_copy(slot, i).start()
        return carry

    lax.fori_loop(0, deep // 2, graded, 0)
    gather.upto(2, 7)
    lax.fori_loop(deep // 2, deep, graded, 0)
    for slot in (0, 1):
        grad_copy(slot, slot).wait()
    gather.complete(2)
    for copy in saves:
        copy.wait()
    for group in (ones, cots, twos, mids):
        group.drain()
    gather.drain()


def forward(n, block_in, cotangent, in_weight, conv_weight, out_weight, gateup_weight, down_weight, norm_gains):
    tokens, model = block_in.shape
    seq = tokens * 4
    chan = out_weight.shape[1]
    units = down_weight.shape[1]
    rows = out_weight.shape[0]
    sends = 3 * (n - 1)
    any_spec = pl.BlockSpec(memory_space=pl.ANY)
    vmem = pl.BlockSpec(memory_space=pltpu.VMEM)
    shape = jax.ShapeDtypeStruct
    dma = pltpu.SemaphoreType.DMA
    return pl.pallas_call(
        functools.partial(forward_kernel, n),
        out_shape=[
            shape((model, 4 * chan), BF),
            shape((model, 2 * units), BF),
            shape((model, units), BF),
            shape((seq, model), BF),
            shape((seq, model), BF),
            shape((seq, model), BF),
            shape((seq + 8, 3 * chan), F32),
            shape((seq, units), F32),
            shape((seq, units), F32),
            shape((seq, units), BF),
            shape((model, units), BF),
            shape((tokens, model), F32),
        ],
        in_specs=[vmem, vmem, vmem] + [any_spec] * 5,
        out_specs=[any_spec] * 11 + [vmem],
        scratch_shapes=[
            pltpu.VMEM((model, 4 * chan), BF),
            pltpu.VMEM((model, 2 * units), BF),
            pltpu.VMEM((rows, units), BF),
            pltpu.VMEM((4, rows, chan), F32),
            pltpu.VMEM((2, rows, units), F32),
            pltpu.VMEM((tokens, model), F32),
            pltpu.VMEM((seq, model), BF),
            pltpu.VMEM((seq, model), BF),
            pltpu.VMEM((seq, model), BF),
            pltpu.VMEM((seq + 8, 3 * chan), F32),
            pltpu.VMEM((seq, chan), BF),
            pltpu.VMEM((2, tokens // 2, units), F32),
            pltpu.VMEM((2, tokens // 2, units), F32),
            pltpu.VMEM((seq, units), BF),
            pltpu.VMEM((2, tokens, units), BF),
            pltpu.VMEM((3, tokens, model), BF),
            pltpu.VMEM((3, tokens, model), BF),
            dma((2, sends)),
            dma((2, sends)),
            dma((9,)),
            dma((9,)),
            dma((3,)),
            dma((3,)),
            dma((9,)),
            dma((10,)),
            dma((3, 2)),
        ],
        compiler_params=pltpu.CompilerParams(
            collective_id=0, has_side_effects=True, vmem_limit_bytes=VMEM_LIMIT
        ),
        cost_estimate=pl.CostEstimate(flops=10 * seq * model * units, bytes_accessed=10**8, transcendentals=0),
    )(block_in, norm_gains, conv_weight, in_weight, out_weight, gateup_weight, down_weight, cotangent)


class Scatter:
    def __init__(self, ring, first, mats, outs, slots, stage, send_sem, recv_sem, credit_sem, out_sem):
        self.ring, self.first, self.mats, self.outs = ring, first, mats, outs
        self.slots, self.stage = slots, stage
        self.send_sem, self.recv_sem = send_sem, recv_sem
        self.credit_sem, self.out_sem = credit_sem, out_sem
        self.depth = slots.shape[1]
        self.total = ring.sends * len(mats)
        self.sent, self.used, self.left = 0, 0, set()

    def place(self, index, way):
        stream, j = divmod(index, self.ring.sends)
        away = self.ring.n // 2 - (j + 1) // 2
        return stream, away, j % 2 if way == 0 else 1 - j % 2

    def mat_span(self, index, way, shift):
        stream, away, u = self.place(index, way)
        sign = 1 if way == 0 else -1
        return self.ring.span(self.ring.pos + sign * (away - shift), u)

    def slot(self, index, way):
        stream, _, u = self.place(index, way)
        cols = self.mats[stream].shape[1]
        return self.slots.at[way, index % self.depth, : self.ring.units[u][1], :cols]

    def copy(self, index, way):
        stream = self.place(index, way)[0]
        mat = self.first if index < 2 else self.mats[stream]
        return pltpu.make_async_remote_copy(
            mat.at[self.mat_span(index, way, 0)],
            self.slot(index, way),
            self.send_sem.at[way, index],
            self.recv_sem.at[way, index],
            device_id=self.ring.next if way == 0 else self.ring.prev,
            device_id_type=MESH,
        )

    def out_copy(self, stream, u):
        start, size = self.ring.units[u]
        cols = self.mats[stream].shape[1]
        slot = stream % 2 * 2 + u
        return pltpu.make_async_copy(
            self.stage.at[slot, :size, :cols],
            self.outs[stream].at[pl.ds(start, size)],
            self.out_sem.at[slot],
        )

    def consume(self, index):
        stream, j = divmod(index, self.ring.sends)
        last = self.ring.sends - 1
        for way in (0, 1):
            u = self.place(index, way)[2]
            size = self.ring.units[u][1]
            self.copy(index, way).wait_recv()
            mat = self.mats[stream]
            cols = mat.shape[1]
            here = self.mat_span(index, way, 1)
            got = self.slots[way, index % self.depth, :size, :cols].astype(F32)
            if j < last - 1:
                mat[here] = (mat[here].astype(F32) + got).astype(BF)
            else:
                slot = stream % 2 * 2 + u
                if j == last - 1:
                    if stream >= 2:
                        self.out_copy(stream - 2, u).wait()
                    self.stage[slot, :size, :cols] = mat[here].astype(F32) + got
                else:
                    self.stage[slot, :size, :cols] = self.stage[slot, :size, :cols] + got
                    self.out_copy(stream, u).start()
            if index + self.depth < self.total:
                pl.semaphore_signal(
                    self.credit_sem.at[way],
                    inc=1,
                    device_id=self.ring.prev if way == 0 else self.ring.next,
                    device_id_type=MESH,
                )

    def use(self, stop):
        while self.used < stop:
            self.consume(self.used)
            self.used += 1

    def upto(self, stream, j):
        stop = min(self.total, stream * self.ring.sends + -(-j * self.ring.sends // 7))
        while self.sent < stop:
            index = self.sent
            if index % self.ring.sends >= 2:
                self.use(index - 1)
            for way in (0, 1):
                if index >= self.depth:
                    pl.semaphore_wait(self.credit_sem.at[way], 1)
                self.copy(index, way).start()
            self.sent += 1

    def leave(self, stream):
        for index in range(stream * self.ring.sends, (stream + 1) * self.ring.sends):
            if index not in self.left:
                self.left.add(index)
                for way in (0, 1):
                    self.copy(index, way).wait_send()

    def drain(self):
        self.use(self.total)
        streams = len(self.mats)
        for stream in range(streams):
            self.leave(stream)
        for stream in range(max(0, streams - 2), streams):
            for u in (0, 1):
                self.out_copy(stream, u).wait()


def backward_kernel(
    n,
    gains_ref,
    conv_ref,
    wc_hbm,
    wgu_hbm,
    wd_hbm,
    one_hbm,
    two_hbm,
    fcot_hbm,
    proj_hbm,
    gate_hbm,
    up_hbm,
    hidden_hbm,
    dgrad_hbm,
    middle_hbm,
    block_hbm,
    cot_hbm,
    down_out,
    gate_out,
    up_out,
    conv_out,
    block_out,
    input_out,
    small_out,
    wd,
    wg,
    wu,
    gd,
    slots,
    full_cot,
    full_two,
    d_gate,
    d_up,
    stage,
    sum_out,
    sum_got,
    tok_a,
    tok_b,
    tok_c,
    proj_t,
    d_conv,
    taps_sum,
    small_send,
    small_got,
    send_sem,
    recv_sem,
    credit_sem,
    out_sem,
    tok_send,
    tok_recv,
    sum_send,
    sum_recv,
    ladder_send,
    ladder_recv,
    load_sem,
    tile_sem,
    proj_sem,
):
    model = wd.shape[0]
    rows = model // n
    ring = Ring(n, rows)
    tokens = tok_a.shape[0]
    seq = full_cot.shape[0]
    chan = conv_ref.shape[1]
    taps = conv_ref.shape[0]
    wc = wd.at[:, : 4 * chan]
    main, tail = split(wg.shape[1])
    gc = gd.at[:, : 4 * chan + 2 * tail]

    def load(k, source, target):
        copy = pltpu.make_async_copy(source, target, load_sem.at[k])
        copy.start()
        return copy

    load_g = load(0, dgrad_hbm, gd)
    load_c = load(1, fcot_hbm, full_cot)
    load_d = load(2, wd_hbm, wd)
    load_gate = load(4, wgu_hbm.at[:, :main], wg.at[:, :main])
    load_up = load(5, wgu_hbm.at[:, main : 2 * main], wu.at[:, :main])
    half = model // 2
    if tail:
        load_ends = [
            load(k, wgu_hbm.at[pl.ds(q * half, half), 2 * main :], full_two.at[:half, q * 128 : (q + 1) * 128])
            for q, k in ((0, 3), (1, 14))
        ]
    load_mid = load(6, middle_hbm, tok_a)
    load_cot = load(7, cot_hbm, tok_b)

    step = tokens // 2
    count = seq // step

    def tile_copy(slot, kind, i):
        source = (gate_hbm, up_hbm)[kind]
        here = pl.ds(pl.multiple_of(i * step, 8), step)
        return pltpu.make_async_copy(source.at[here], stage.at[slot * 2 + kind], tile_sem.at[slot, kind])

    for kind in (0, 1):
        tile_copy(0, kind, 0).start()

    steps = [ring.core, ring.over]
    span = 1
    while span < n:
        steps.append((ring.d + span * (1 - 2 * lax.rem(lax.div(ring.d, span), 2)), ring.t))
        span *= 2
    sem = pltpu.get_barrier_semaphore()
    for device in [ring.next, ring.prev] + steps:
        pl.semaphore_signal(sem, inc=1, device_id=device, device_id_type=MESH)
    pl.semaphore_wait(sem, 2 + len(steps))

    scatter = Scatter(
        ring,
        dgrad_hbm,
        (gd, wg.at[:, :main], wu.at[:, :main], gc),
        (down_out, gate_out, up_out, conv_out),
        slots,
        stage,
        send_sem,
        recv_sem,
        credit_sem,
        out_sem,
    )
    scatter.upto(0, 2)
    load_g.wait()
    load_c.wait()
    load_d.wait()

    def hidden_back(i, carry):
        slot = lax.rem(i, 2)
        here = pl.ds(pl.multiple_of(i * step, 16), step)

        @pl.when(i + 1 < count)
        def _():
            for kind in (0, 1):
                tile_copy(1 - slot, kind, i + 1).start()

        d_hidden = dot(full_cot[here], wd[...])
        for kind in (0, 1):
            tile_copy(slot, kind, i).wait()
        gate = stage[slot * 2]
        sig = jax.nn.sigmoid(gate)
        d_up[here] = (d_hidden * (gate * sig)).astype(BF)
        d_gate[here] = (d_hidden * stage[slot * 2 + 1] * sig * (1.0 + gate * (1.0 - sig))).astype(BF)
        return carry

    lax.fori_loop(0, count // 2, hidden_back, 0)
    scatter.upto(0, 3)
    lax.fori_loop(count // 2, count, hidden_back, 0)
    load_gate.wait()
    load_up.wait()
    if tail:
        for q in (0, 1):
            load_ends[q].wait()
            here = pl.ds(q * half, half)
            ends = full_two[:half, q * 128 : (q + 1) * 128]
            wg[here, main:] = ends[:, :tail]
            wu[here, main:] = ends[:, tail:]
    load_two = load(3, two_hbm, full_two)
    scatter.upto(0, 4)

    def token_rows(owner):
        return pl.ds(pl.multiple_of(owner * tokens, 16), tokens)

    def two_block(owner):
        here = token_rows(owner)
        return dot(d_gate[here], wg[...], NT) + dot(d_up[here], wu[...], NT)

    twos = Sums(ring, sum_out, sum_got, sum_send, sum_recv, 0)
    twos.far(two_block)
    tok_c[...] = twos.near(two_block)
    scatter.upto(0, 5)
    load_two.wait()

    width = tokens
    deep = model // width

    def grad_into(target, columns, left, right):
        def body(i, carry):
            x = left[:, pl.ds(pl.multiple_of(i * width, 128), width)]
            target[pl.ds(pl.multiple_of(i * width, 16), width), columns] = dot(x, right[...], TN).astype(BF)
            return carry

        return body

    every = slice(None)
    lax.fori_loop(0, deep, grad_into(wg, every, full_two, d_gate), 0)
    load_hidden = load(8, hidden_hbm, d_gate)
    scatter.upto(0, 7)
    scatter.upto(1, 2)

    load_mid.wait()
    load_cot.wait()
    chunk = tokens // 4
    small_send[0] = jnp.zeros(small_send.shape[1:], F32)
    twos.arrive()

    def middle_back(i, carry):
        here = pl.ds(pl.multiple_of(i * chunk, 16), chunk)
        d_two = twos.total(tok_c[here], here)
        middle = tok_a[here]
        scale = lax.rsqrt(jnp.mean(middle * middle, axis=1, keepdims=True) + eps_norm)
        normal = middle * scale
        weighted = gains_ref[1:2] * d_two
        d_middle = tok_b[here] + scale * (
            weighted - normal * jnp.mean(weighted * normal, axis=1, keepdims=True)
        )
        small_send[0, 1:2] += jnp.sum(d_two * normal, axis=0, keepdims=True)
        tok_c[here] = d_middle
        full_cot[pl.ds(pl.multiple_of(ring.t * tokens + i * chunk, 16), chunk)] = d_middle.astype(BF)
        return carry

    lax.fori_loop(0, 4, middle_back, 0)
    mids = Tokens(ring, full_cot, tok_send, tok_recv, 0)
    mids.start()
    load_block = load(9, block_hbm, tok_b)

    lax.fori_loop(0, deep, grad_into(wu, every, full_two, d_up), 0)
    load_one = load(10, one_hbm, full_two)
    scatter.upto(1, 4)
    mids.forward()
    load_hidden.wait()
    twos.drain()

    def down_block(owner):
        return dot(d_gate[token_rows(owner)], wd[...], NT)

    downs = Sums(ring, sum_out, sum_got, sum_send, sum_recv, 1)
    downs.far(down_block)
    scatter.upto(1, 5)
    tok_a[...] = tok_a[...] + downs.near(down_block)
    load_conv = load(11, wc_hbm, wc)
    mids.finish()
    scatter.upto(1, 6)

    def proj_copy(slot, i):
        here = pl.ds(pl.multiple_of(i * step, 8), step + 8)
        return pltpu.make_async_copy(proj_hbm.at[here], proj_t.at[slot], proj_sem.at[slot])

    proj_copy((count - 1) % 2, count - 1).start()
    d_conv[pl.ds(seq, 8)] = jnp.zeros((8, chan), F32)
    taps_sum[...] = jnp.zeros(taps_sum.shape, F32)
    load_conv.wait()
    load_one.wait()

    def conv_back(k, carry):
        i = count - 1 - k
        slot = lax.rem(i, 2)

        @pl.when(i >= 1)
        def _():
            proj_copy(1 - slot, i - 1).start()

        here = pl.ds(pl.multiple_of(i * step, 16), step)
        d_mixer = dot(full_cot[here], wd[:, 3 * chan : 4 * chan])
        proj_copy(slot, i).wait()
        b_part = proj_t[slot, :, :chan]
        c_part = proj_t[slot, 8:, chan : 2 * chan]
        v_part = proj_t[slot, :, 2 * chan :]
        mixed = b_part * v_part
        shifted = [mixed[8:]] + [pltpu.roll(mixed, back, 0)[8:] for back in range(1, taps)]
        total = sum(conv_ref[taps - 1 - back : taps - back] * shifted[back] for back in range(taps))
        d_c = d_mixer * total
        d_here = d_mixer * c_part
        d_up[here, :chan] = (c_part * total).astype(BF)
        d_conv[pl.ds(pl.multiple_of(i * step, 8), step)] = d_here
        for back in range(taps):
            at = taps - 1 - back
            taps_sum[at : at + 1] += jnp.sum(d_here * shifted[back], axis=0, keepdims=True)
        longer = d_conv[pl.ds(pl.multiple_of(i * step, 8), step + 8)]
        d_mixed = conv_ref[taps - 1 : taps] * d_here
        for ahead in range(1, taps):
            moved = pltpu.roll(longer, step + 8 - ahead, 0)[:step]
            d_mixed += conv_ref[taps - 1 - ahead : taps - ahead] * moved
        d_gate[here, :chan] = (d_mixed * v_part[8:]).astype(BF)
        d_gate[here, chan : 2 * chan] = d_c.astype(BF)
        d_gate[here, 2 * chan : 3 * chan] = (d_mixed * b_part[8:]).astype(BF)
        return carry

    lax.fori_loop(0, count // 2, conv_back, 0)
    scatter.upto(1, 7)
    scatter.upto(2, 2)
    lax.fori_loop(count // 2, count, conv_back, 0)
    small_send[0, 2 : 2 + taps, :chan] = taps_sum[:taps]
    scatter.upto(2, 3)

    def one_block(owner):
        return dot(d_gate[token_rows(owner), : 3 * chan], wd[:, : 3 * chan], NT)

    downs.arrive()

    def block_done(i, carry):
        here = pl.ds(pl.multiple_of(i * chunk, 16), chunk)
        tok_a[here] = downs.total(tok_a[here], here)
        return carry

    lax.fori_loop(0, 4, block_done, 0)
    save_block = load(12, tok_a, block_out)
    downs.drain()
    save_block.wait()
    ones = Sums(ring, sum_out, sum_got, sum_send, sum_recv, 2, 3)
    ones.far(one_block)
    tok_a[...] = ones.near(one_block)
    scatter.leave(0)
    proj_one = slice(0, 3 * chan)
    mix_cols = slice(3 * chan, 4 * chan)

    def in_grad(i, carry):
        x = full_two[:, pl.ds(pl.multiple_of(i * width, 128), width)]
        gd[pl.ds(pl.multiple_of(i * width, 16), width), proj_one] = dot(x, d_gate[:, proj_one], TN).astype(BF)
        z = full_cot[:, pl.ds(pl.multiple_of(i * width, 128), width)]
        gd[pl.ds(pl.multiple_of(i * width, 16), width), mix_cols] = dot(z, d_up[:, :chan], TN).astype(BF)
        if tail:
            here = pl.ds(pl.multiple_of(i * width, 16), width)
            ends = [wg[here, main:].astype(F32), wu[here, main:].astype(F32)]
            gd[here, 4 * chan : 4 * chan + 2 * tail] = jnp.concatenate(ends, axis=1).astype(BF)
        return carry

    scatter.upto(2, 4)
    lax.fori_loop(0, deep, in_grad, 0)
    scatter.upto(2, 5)
    load_block.wait()
    ones.arrive()

    def input_back(i, carry):
        here = pl.ds(pl.multiple_of(i * chunk, 16), chunk)
        d_one = ones.total(tok_a[here], here)
        values = tok_b[here]
        scale = lax.rsqrt(jnp.mean(values * values, axis=1, keepdims=True) + eps_norm)
        normal = values * scale
        weighted = gains_ref[0:1] * d_one
        tok_c[here] = tok_c[here] + scale * (
            weighted - normal * jnp.mean(weighted * normal, axis=1, keepdims=True)
        )
        small_send[0, 0:1] += jnp.sum(d_one * normal, axis=0, keepdims=True)
        return carry

    lax.fori_loop(0, 4, input_back, 0)
    save_input = load(13, tok_c, input_out)
    scatter.upto(2, 6)

    ladder = [
        pltpu.make_async_remote_copy(
            small_send.at[k],
            small_got.at[k],
            ladder_send.at[k],
            ladder_recv.at[k],
            device_id=device,
            device_id_type=MESH,
        )
        for k, device in enumerate(steps)
    ]
    for k in range(len(steps)):
        ladder[k].start()
        scatter.upto(*((2, 7), (3, 2), (3, 3), (3, 4), (3, 5))[min(k, 4)])
        ladder[k].wait_recv()
        if k < 2:
            small_send[k + 1, 0:2] = small_send[k, 0:2] + small_got[k, 0:2]
            small_send[k + 1, 2:8] = small_send[k, 2:8]
        else:
            small_send[k + 1] = small_send[k] + small_got[k]
    small_out[...] = small_send[len(steps)]
    scatter.upto(3, 7)
    scatter.drain()
    mids.drain()
    ones.drain()
    for copy in ladder:
        copy.wait_send()
    save_input.wait()


def backward(n, conv_weight, norm_gains, saved, block_in, cotangent, depth=4):
    (wc, wgu, wd, one, two, fcot, proj, gate, up, hidden, dgrad, middle) = saved
    tokens, model = block_in.shape
    seq = tokens * 4
    chan = conv_weight.shape[1]
    units = wd.shape[1]
    rows = model // n
    sends = 4 * (n - 1)
    steps = 2 + (n - 1).bit_length()
    unit = (rows // 2 + 15) // 16 * 16
    any_spec = pl.BlockSpec(memory_space=pl.ANY)
    vmem = pl.BlockSpec(memory_space=pltpu.VMEM)
    shape = jax.ShapeDtypeStruct
    dma = pltpu.SemaphoreType.DMA
    return pl.pallas_call(
        functools.partial(backward_kernel, n),
        out_shape=[
            shape((rows, units), F32),
            shape((rows, split(units)[0]), F32),
            shape((rows, split(units)[0]), F32),
            shape((rows, 4 * chan + 2 * split(units)[1]), F32),
            shape((tokens, model), F32),
            shape((tokens, model), F32),
            shape((8, model), F32),
        ],
        in_specs=[vmem, vmem] + [any_spec] * 14,
        out_specs=[any_spec] * 6 + [vmem],
        scratch_shapes=[
            pltpu.VMEM((model, units), BF),
            pltpu.VMEM((model, units), BF),
            pltpu.VMEM((model, units), BF),
            pltpu.VMEM((model, units), BF),
            pltpu.VMEM((2, depth, unit, units), BF),
            pltpu.VMEM((seq, model), BF),
            pltpu.VMEM((seq, model), BF),
            pltpu.VMEM((seq, units), BF),
            pltpu.VMEM((seq, units), BF),
            pltpu.VMEM((4, tokens // 2, units), F32),
            pltpu.VMEM((3, tokens, model), BF),
            pltpu.VMEM((4, tokens, model), BF),
            pltpu.VMEM((tokens, model), F32),
            pltpu.VMEM((tokens, model), F32),
            pltpu.VMEM((tokens, model), F32),
            pltpu.VMEM((2, tokens // 2 + 8, 3 * chan), F32),
            pltpu.VMEM((seq + 8, chan), F32),
            pltpu.VMEM((8, chan), F32),
            pltpu.VMEM((steps + 1, 8, model), F32),
            pltpu.VMEM((steps, 8, model), F32),
            dma((2, sends)),
            dma((2, sends)),
            pltpu.SemaphoreType.REGULAR((2,)),
            dma((4,)),
            dma((3,)),
            dma((3,)),
            dma((9,)),
            dma((9,)),
            dma((steps,)),
            dma((steps,)),
            dma((15,)),
            dma((2, 2)),
            dma((2,)),
        ],
        compiler_params=pltpu.CompilerParams(
            collective_id=1, has_side_effects=True, vmem_limit_bytes=VMEM_LIMIT
        ),
        cost_estimate=pl.CostEstimate(flops=16 * seq * model * units, bytes_accessed=10**8, transcendentals=0),
    )(
        norm_gains, conv_weight, wc, wgu, wd, one, two, fcot, proj, gate, up, hidden, dgrad,
        middle, block_in, cotangent,
    )


def finish_kernel(
    down_ref,
    gate_ref,
    up_ref,
    conv_ref,
    block_ref,
    input_ref,
    small_ref,
    in_w,
    in_m,
    in_v,
    out_w,
    out_m,
    out_v,
    gateup_w,
    gateup_m,
    gateup_v,
    down_w,
    down_m,
    down_v,
    taps_w,
    taps_m,
    taps_v,
    gains_w,
    gains_m,
    gains_v,
    block_out,
    input_out,
    in_grad,
    taps_grad,
    out_grad,
    gateup_grad,
    down_grad,
    gains_grad,
    in_up,
    taps_up,
    out_up,
    gateup_up,
    down_up,
    gains_up,
    in_mo,
    in_va,
    taps_mo,
    taps_va,
    out_mo,
    out_va,
    gateup_mo,
    gateup_va,
    down_mo,
    down_va,
    gains_mo,
    gains_va,
):
    chan = out_w.shape[1]
    block_out[...] = block_ref[...]
    input_out[...] = input_ref[...]
    for k in range(3):
        grad = conv_ref[:, k * chan : (k + 1) * chan]
        in_grad[k] = grad
        in_up[k], in_mo[k], in_va[k] = adamw(in_w[k], grad, in_m[k], in_v[k], rate_matrix, decay_matrix)
    grad = conv_ref[:, 3 * chan : 4 * chan]
    out_grad[...] = grad
    out_up[...], out_mo[...], out_va[...] = adamw(
        out_w[...], grad, out_m[...], out_v[...], rate_matrix, decay_matrix
    )
    for k, ref in enumerate((gate_ref, up_ref)):
        tail = gateup_w.shape[2] - ref.shape[1]
        gateup_grad[k, :, : ref.shape[1]] = ref[...]
        if tail:
            start = 4 * chan + k * tail
            gateup_grad[k, :, ref.shape[1] :] = conv_ref[:, start : start + tail]
        grad = gateup_grad[k]
        gateup_up[k], gateup_mo[k], gateup_va[k] = adamw(
            gateup_w[k], grad, gateup_m[k], gateup_v[k], rate_matrix, decay_matrix
        )
    grad = down_ref[...]
    down_grad[...] = grad
    down_up[...], down_mo[...], down_va[...] = adamw(
        down_w[...], grad, down_m[...], down_v[...], rate_matrix, decay_matrix
    )

    @pl.when(pl.program_id(0) == 0)
    def _():
        taps = taps_w.shape[0]
        grad = small_ref[0:2]
        gains_grad[...] = grad
        gains_up[...], gains_mo[...], gains_va[...] = adamw(
            gains_w[...], grad, gains_m[...], gains_v[...], rate_small, 0.0
        )
        grad = small_ref[2 : 2 + taps, :chan]
        taps_grad[...] = grad
        taps_up[...], taps_mo[...], taps_va[...] = adamw(
            taps_w[...], grad, taps_m[...], taps_v[...], rate_small, 0.0
        )


def finish(grads, in_set, out_set, gateup_set, down_set, taps_set, gains_set):
    rows, units = grads[0].shape
    tokens, model = grads[4].shape
    chan = out_set[0].shape[1]
    taps = taps_set[0].shape[0]
    parts = max(g for g in (1, 2, 3) if rows % (8 * g) == 0 and tokens % (8 * g) == 0)
    r, t = rows // parts, tokens // parts
    wide = lambda width: pl.BlockSpec((r, width), lambda i: (i, 0))
    deep = lambda count, width: pl.BlockSpec((count, r, width), lambda i: (0, i, 0))
    token = pl.BlockSpec((t, model), lambda i: (i, 0))
    whole = lambda *dims: pl.BlockSpec(dims, lambda i: (0, 0))
    in_spec, out_spec, gateup_spec, down_spec = deep(3, chan), wide(chan), deep(2, units), wide(units)
    taps_spec, gains_spec = whole(taps, chan), whole(2, model)
    like = lambda group: jax.ShapeDtypeStruct(group[0].shape, F32)
    shape = [jax.ShapeDtypeStruct((tokens, model), F32)] * 2
    matrices = (in_set, taps_set, out_set, gateup_set, down_set, gains_set)
    specs = (in_spec, taps_spec, out_spec, gateup_spec, down_spec, gains_spec)
    out_shape = shape + [like(m) for m in matrices] * 2
    out_specs = [token, token] + list(specs) * 2
    for m, spec in zip(matrices, specs):
        out_shape += [like(m)] * 2
        out_specs += [spec] * 2
    return pl.pallas_call(
        finish_kernel,
        grid=(parts,),
        out_shape=out_shape,
        in_specs=[wide(grad.shape[1]) for grad in grads[:4]]
        + [token, token, whole(8, model)]
        + [in_spec] * 3
        + [out_spec] * 3
        + [gateup_spec] * 3
        + [down_spec] * 3
        + [taps_spec] * 3
        + [gains_spec] * 3,
        out_specs=out_specs,
        compiler_params=pltpu.CompilerParams(vmem_limit_bytes=VMEM_LIMIT),
    )(*grads, *in_set, *out_set, *gateup_set, *down_set, *taps_set, *gains_set)


def per_device(
    block_in,
    cotangent,
    in_weight,
    conv_weight,
    out_weight,
    gateup_weight,
    down_weight,
    norm_gains,
    in_first,
    in_second,
    conv_first,
    conv_second,
    out_first,
    out_second,
    gateup_first,
    gateup_second,
    down_first,
    down_second,
    gains_first,
    gains_second,
):
    n = lax.axis_size("dp")
    saved = forward(
        n,
        block_in,
        cotangent,
        in_weight,
        conv_weight,
        out_weight,
        gateup_weight,
        down_weight,
        norm_gains,
    )
    grads = backward(n, conv_weight, norm_gains, saved, block_in, cotangent)
    return tuple(
        finish(
            grads,
            (in_weight, in_first, in_second),
            (out_weight, out_first, out_second),
            (gateup_weight, gateup_first, gateup_second),
            (down_weight, down_first, down_second),
            (conv_weight, conv_first, conv_second),
            (norm_gains, gains_first, gains_second),
        )
    )


def solution(mesh):
    in_specs = (
        P(("dp", "tensor"), None),
        P(("dp", "tensor"), None),
        P(None, "dp", "tensor"),
        P(None, "tensor"),
        P("dp", "tensor"),
        P(None, "dp", "tensor"),
        P("dp", "tensor"),
        P(),
        P(None, "dp", "tensor"),
        P(None, "dp", "tensor"),
        P(None, "tensor"),
        P(None, "tensor"),
        P("dp", "tensor"),
        P("dp", "tensor"),
        P(None, "dp", "tensor"),
        P(None, "dp", "tensor"),
        P("dp", "tensor"),
        P("dp", "tensor"),
        P(),
        P(),
    )
    out_specs = (
        P(("dp", "tensor"), None),
        P(("dp", "tensor"), None),
        P(None, "dp", "tensor"),
        P(None, "tensor"),
        P("dp", "tensor"),
        P(None, "dp", "tensor"),
        P("dp", "tensor"),
        P(),
        P(None, "dp", "tensor"),
        P(None, "tensor"),
        P("dp", "tensor"),
        P(None, "dp", "tensor"),
        P("dp", "tensor"),
        P(),
        P(None, "dp", "tensor"),
        P(None, "dp", "tensor"),
        P(None, "tensor"),
        P(None, "tensor"),
        P("dp", "tensor"),
        P("dp", "tensor"),
        P(None, "dp", "tensor"),
        P(None, "dp", "tensor"),
        P("dp", "tensor"),
        P("dp", "tensor"),
        P(),
        P(),
    )
    return jax.shard_map(
        per_device, mesh=mesh, in_specs=in_specs, out_specs=out_specs, check_vma=False
    )
```
